32 devices in a mesh: dp: 8 (over z, y), fsdp: 4 (over x, core).
Axes of the slice: x: 2, y: 2, z: 4, core: 2. Of those that a mesh axis runs over, the one named last changes fastest.
Arguments:
- tokens: bfloat16 [65536, 512], P(('dp', 'fsdp')), may hold values from -6 to 6
- cotangent: bfloat16 [65536, 512], P(('dp', 'fsdp')), may hold values from -6 to 6
- cond_frames: int32 [64], P(('dp', 'fsdp')), may hold values from 1 to 3
- qkv_weight: float32 [32, 24576], P(('dp', 'fsdp')), may hold values from -0.25 to 0.25
- proj_weight: float32 [32, 8192], P(('dp', 'fsdp')), may hold values from -0.375 to 0.375
- up_weight: float32 [32, 32768], P(('dp', 'fsdp')), may hold values from -0.25 to 0.25
- down_weight: float32 [32, 32768], P(('dp', 'fsdp')), may hold values from -0.125 to 0.125
- vectors: float32 [32, 208], P(('dp', 'fsdp')), may hold values from -0.6 to 1.4, as said below
- qkv_first: float32 [32, 24576], P(('dp', 'fsdp')), may hold values from -160 to 160
- proj_first: float32 [32, 8192], P(('dp', 'fsdp')), may hold values from -40 to 40
- up_first: float32 [32, 32768], P(('dp', 'fsdp')), may hold values from -80 to 80
- down_first: float32 [32, 32768], P(('dp', 'fsdp')), may hold values from -80 to 80
- vector_first: float32 [32, 208], P(('dp', 'fsdp')), may hold values from -128 to 128
- qkv_second: float32 [32, 24576], P(('dp', 'fsdp')), may hold values from 1703.936 to 27525.12
- proj_second: float32 [32, 8192], P(('dp', 'fsdp')), may hold values from 163.84 to 655.36
- up_second: float32 [32, 32768], P(('dp', 'fsdp')), may hold values from 340.7872 to 5505.024
- down_second: float32 [32, 32768], P(('dp', 'fsdp')), may hold values from 340.7872 to 5505.024
- vector_second: float32 [32, 208], P(('dp', 'fsdp')), may hold values from 851.968 to 13762.56
- qkv_average: float32 [32, 24576], P(('dp', 'fsdp')), may hold values from -0.25 to 0.25
- proj_average: float32 [32, 8192], P(('dp', 'fsdp')), may hold values from -0.375 to 0.375
- up_average: float32 [32, 32768], P(('dp', 'fsdp')), may hold values from -0.25 to 0.25
- down_average: float32 [32, 32768], P(('dp', 'fsdp')), may hold values from -0.125 to 0.125
- vector_average: float32 [32, 208], P(('dp', 'fsdp')), may hold values from 0.5 to 1.5
Outputs:
- output: bfloat16 [65536, 512], P(('dp', 'fsdp'))
- input_grad: float32 [65536, 512], P(('dp', 'fsdp'))
- qkv_first_new: float32 [32, 24576], P(('dp', 'fsdp'))
- qkv_second_new: float32 [32, 24576], P(('dp', 'fsdp'))
- qkv_weight_new: float32 [32, 24576], P(('dp', 'fsdp'))
- qkv_average_new: float32 [32, 24576], P(('dp', 'fsdp'))
- proj_first_new: float32 [32, 8192], P(('dp', 'fsdp'))
- proj_second_new: float32 [32, 8192], P(('dp', 'fsdp'))
- proj_weight_new: float32 [32, 8192], P(('dp', 'fsdp'))
- proj_average_new: float32 [32, 8192], P(('dp', 'fsdp'))
- up_first_new: float32 [32, 32768], P(('dp', 'fsdp'))
- up_second_new: float32 [32, 32768], P(('dp', 'fsdp'))
- up_weight_new: float32 [32, 32768], P(('dp', 'fsdp'))
- up_average_new: float32 [32, 32768], P(('dp', 'fsdp'))
- down_first_new: float32 [32, 32768], P(('dp', 'fsdp'))
- down_second_new: float32 [32, 32768], P(('dp', 'fsdp'))
- down_weight_new: float32 [32, 32768], P(('dp', 'fsdp'))
- down_average_new: float32 [32, 32768], P(('dp', 'fsdp'))
- vector_first_new: float32 [32, 208], P(('dp', 'fsdp'))
- vector_second_new: float32 [32, 208], P(('dp', 'fsdp'))
- vector_new: float32 [32, 208], P(('dp', 'fsdp'))
- vector_average_new: float32 [32, 208], P(('dp', 'fsdp'))
The draws below stay inside these ranges and needn't reach their ends.
Inputs may be any that keep to these rules, and one draw needn't show every extreme that they name: `cond_frames`: each clip's first frame is always conditioning. `vectors`: entries of g1 and g2 are gains, the others biases.
All inputs are finite; a program needn't handle non-finite values.
Results may differ from the reference program's by a relative error of at most 0.0093.
Values may be sent and summed in bfloat16 or wider, within the bound.
A program may use at most 192 MiB of HBM per device.

```python
import math
import jax
import jax.numpy as jnp
from jax import lax

D = 512
FF = 2048
HEADS = 8
HEAD_DIM = 64
FRAME_TOK = 64
STEP = 10
CLIP_LEN = 1024
SHARDS = 32
CLIPS = 64
TOKENS = 65536
VEC = 6656


def draw_vectors(key, part):
    key = jax.random.fold_in(key, 5)
    gain_key, shift_key = jax.random.split(key)
    place = jnp.arange(VEC)
    gains_all = jax.random.uniform(gain_key, (VEC,), jnp.float32, 0.6, 1.4)
    shifts_all = 0.2 * jax.random.truncated_normal(shift_key, -3.0, 3.0, (VEC,), jnp.float32)
    is_gain = (place < D) | (place >= 6 * D) & (place < 7 * D)
    return jnp.where(is_gain, gains_all, shifts_all).reshape(SHARDS, VEC // SHARDS)


def plant(result, stream_key, smallest, top_value):
    dims = result.shape
    index_at = [jax.random.randint(jax.random.fold_in(stream_key, axis), (), 0, dims[axis]) for axis in range(len(dims))]
    result = result.at[tuple(index_at)].set(smallest)
    longest = dims.index(max(dims))
    index_at[longest] = (index_at[longest] + 1) % dims[longest]
    return result.at[tuple(index_at)].set(top_value)


def level_of(stream_key, shape, cuts, least, top_value):
    gain, own = 1.0, jax.random.fold_in(stream_key, 6)
    for dim, parts in cuts:
        heights = jnp.exp(jax.random.uniform(jax.random.fold_in(own, dim), (parts,), jnp.float32, least / len(cuts), top_value / len(cuts)))
        gain = gain * jnp.repeat(heights, shape[dim] // parts).reshape([-1 if axis == dim else 1 for axis in range(len(shape))])
    return gain


def gaussian(key, shape, scale, bound, shards=(), kind=jnp.bfloat16):
    entries = jax.random.normal(key, shape, jnp.float32) * scale
    if len(shards) > 0:
        entries = level_of(key, shape, shards, -0.22, 0.18) * entries
    return jnp.clip(entries, min=-bound, max=bound).astype(kind)


def setup_inputs(seed: int = 0) -> dict:
    key_of = jax.random.split(jax.random.key(seed), 24)
    tokens = gaussian(key_of[0], (TOKENS, D), 1.0, 6.0, ((0, 32),))
    cotangent = gaussian(key_of[1], (TOKENS, D), 1.0, 6.0, ((0, 32),))
    cond_frames = plant(jax.random.randint(key_of[2], (CLIPS,), 1, 4), jax.random.fold_in(key_of[2], 1), 1, 3).astype(jnp.int32)
    qkv_weight = gaussian(key_of[3], (SHARDS, 3 * D * D // SHARDS), D ** -0.5, 0.25, ((0, 32),), jnp.float32)
    proj_weight = gaussian(key_of[4], (SHARDS, D * D // SHARDS), (max(1, D // 2)) ** -0.5, 0.375, ((0, 32),), jnp.float32)
    up_weight = gaussian(key_of[5], (SHARDS, D * FF // SHARDS), D ** -0.5, 0.25, ((0, 32),), jnp.float32)
    down_weight = gaussian(key_of[6], (SHARDS, D * FF // SHARDS), FF ** -0.5, 0.125, ((0, 32),), jnp.float32)
    vectors = draw_vectors(jax.random.fold_in(key_of[23], 71), 0)
    qkv_first = gaussian(key_of[8], (SHARDS, 3 * D * D // SHARDS), (0.11 * TOKENS ** 0.5), 160.0, ((0, 32),), jnp.float32)
    proj_first = gaussian(key_of[9], (SHARDS, D * D // SHARDS), (0.025 * TOKENS ** 0.5), 40.0, ((0, 32),), jnp.float32)
    up_first = gaussian(key_of[10], (SHARDS, D * FF // SHARDS), (0.049 * TOKENS ** 0.5), 80.0, ((0, 32),), jnp.float32)
    down_first = gaussian(key_of[11], (SHARDS, D * FF // SHARDS), (0.049 * TOKENS ** 0.5), 80.0, ((0, 32),), jnp.float32)
    vector_first = gaussian(key_of[12], (SHARDS, VEC // SHARDS), (0.078 * TOKENS ** 0.5), 128.0, ((0, 32),), jnp.float32)
    qkv_second = jnp.clip(jnp.exp(math.log(27525.12) - 2.7821581 * jax.random.uniform(key_of[13], (SHARDS, 3 * D * D // SHARDS), jnp.float32) ** level_of(key_of[13], (SHARDS, 3 * D * D // SHARDS), ((0, 32),), -0.2, 0.2)), 1703.936, 27525.12)
    proj_second = jnp.clip(jnp.exp(math.log(655.36) - 1.3862944 * jax.random.uniform(key_of[14], (SHARDS, D * D // SHARDS), jnp.float32) ** level_of(key_of[14], (SHARDS, D * D // SHARDS), ((0, 32),), -0.2, 0.2)), 163.84, 655.36)
    up_second = jnp.clip(jnp.exp(math.log(5505.024) - 2.7821582 * jax.random.uniform(key_of[15], (SHARDS, D * FF // SHARDS), jnp.float32) ** level_of(key_of[15], (SHARDS, D * FF // SHARDS), ((0, 32),), -0.2, 0.2)), 340.7872, 5505.024)
    down_second = jnp.clip(jnp.exp(math.log(5505.024) - 2.7821582 * jax.random.uniform(key_of[16], (SHARDS, D * FF // SHARDS), jnp.float32) ** level_of(key_of[16], (SHARDS, D * FF // SHARDS), ((0, 32),), -0.2, 0.2)), 340.7872, 5505.024)
    vector_second = jnp.clip(jnp.exp(math.log(13762.56) - 2.7821581 * jax.random.uniform(key_of[17], (SHARDS, VEC // SHARDS), jnp.float32) ** level_of(key_of[17], (SHARDS, VEC // SHARDS), ((0, 32),), -0.2, 0.2)), 851.968, 13762.56)
    qkv_average = gaussian(key_of[18], (SHARDS, 3 * D * D // SHARDS), D ** -0.5, 0.25, ((0, 32),), jnp.float32)
    proj_average = gaussian(key_of[19], (SHARDS, D * D // SHARDS), (max(1, D // 2)) ** -0.5, 0.375, ((0, 32),), jnp.float32)
    up_average = gaussian(key_of[20], (SHARDS, D * FF // SHARDS), D ** -0.5, 0.25, ((0, 32),), jnp.float32)
    down_average = gaussian(key_of[21], (SHARDS, D * FF // SHARDS), FF ** -0.5, 0.125, ((0, 32),), jnp.float32)
    vector_average = jnp.clip(1.0 + 0.1 * jax.random.normal(key_of[22], (SHARDS, VEC // SHARDS), jnp.float32), 0.5, 1.5)
    return dict(tokens=tokens, cotangent=cotangent, cond_frames=cond_frames, qkv_weight=qkv_weight, proj_weight=proj_weight, up_weight=up_weight, down_weight=down_weight, vectors=vectors, qkv_first=qkv_first, proj_first=proj_first, up_first=up_first, down_first=down_first, vector_first=vector_first, qkv_second=qkv_second, proj_second=proj_second, up_second=up_second, down_second=down_second, vector_second=vector_second, qkv_average=qkv_average, proj_average=proj_average, up_average=up_average, down_average=down_average, vector_average=vector_average)


EPS = 1e-05
BETA_ONE = 0.9
BETA_TWO = 0.95
ADAM_EPS = 1e-08
RATE_MATRIX = 0.02
RATE_VECTOR = 0.2
WEIGHT_DECAY = 0.1
EMA_KEEP = 0.9
NEG = -1e+30

@jax.custom_vjp
def low(v):
    return lax.optimization_barrier(v.astype(jnp.bfloat16)).astype(jnp.float32)

@jax.custom_vjp
def low_back(v):
    return v

def low_keep(v):
    return (low(v), None)

def low_pass(kept, grad):
    return (grad,)

def back_keep(v):
    return (v, None)

def back_low(kept, grad):
    return (low(grad),)
low.defvjp(low_keep, low_pass)
low_back.defvjp(back_keep, back_low)

def layer_norm(inputs, gain_vec, shifts):
    row_mean = lax.optimization_barrier(jnp.mean(inputs, axis=-1, keepdims=True))
    centred = inputs - row_mean
    variance = lax.optimization_barrier(jnp.mean(centred * centred, axis=-1, keepdims=True))
    return centred * lax.rsqrt(variance + EPS) * gain_vec + shifts

def matmul(left_op, right_op):
    return jnp.dot(left_op, right_op, precision=lax.Precision.HIGHEST)

def split_vectors(packed):
    bounds = [0, D, 2 * D, 5 * D, 6 * D, 7 * D, 8 * D, 8 * D + FF, 9 * D + FF]
    return [packed[bounds[i]:bounds[i + 1]] for i in range(8)]

def clip_attention(qkv_clip):
    length = qkv_clip.shape[0]
    queries = qkv_clip[:, :D].reshape(length, HEADS, HEAD_DIM)
    keys_part = qkv_clip[:, D:2 * D].reshape(length, HEADS, HEAD_DIM)
    values_part = qkv_clip[:, 2 * D:].reshape(length, HEADS, HEAD_DIM)
    scores = jnp.einsum('qhd,khd->hqk', queries, keys_part, precision=lax.Precision.HIGHEST) * HEAD_DIM ** (-0.5)
    scores = low_back(scores)
    row_index = jnp.arange(length)[:, None]
    col_index = jnp.arange(length)[None, :]
    scores = jnp.where(col_index <= row_index, scores, NEG)
    row_top = lax.optimization_barrier(jnp.max(scores, axis=-1, keepdims=True))
    exponent = jnp.exp(scores - row_top)
    attn_probs = exponent / lax.optimization_barrier(jnp.sum(exponent, axis=-1, keepdims=True))
    mixed = jnp.einsum('hqk,khd->qhd', low(attn_probs), values_part, precision=lax.Precision.HIGHEST)
    return mixed.reshape(length, D)

def forward(inputs, qkv_weight, proj_weight, up_weight, down_weight, vectors):
    gain_one, shift_one, qkv_bias, proj_bias, gain_two, shift_two, up_bias, down_bias = split_vectors(low(vectors).reshape(-1))
    qkv_mat = low(qkv_weight).reshape(D, 3 * D)
    proj_mat = low(proj_weight).reshape(D, D)
    up_mat = low(up_weight).reshape(D, FF)
    down_mat = low(down_weight).reshape(FF, D)
    normed = low(layer_norm(inputs, gain_one, shift_one))
    qkv_all = low(low_back(matmul(normed, qkv_mat) + qkv_bias))
    attended = lax.map(jax.checkpoint(clip_attention), qkv_all.reshape(CLIPS, CLIP_LEN, 3 * D)).reshape(TOKENS, D)
    attended = low(low_back(attended))
    branch = low_back(matmul(attended, proj_mat) + proj_bias)
    hidden_res = inputs + branch
    normed_two = low(layer_norm(hidden_res, gain_two, shift_two))
    pre_act = low_back(matmul(normed_two, up_mat) + up_bias)
    activ = low(jax.nn.gelu(pre_act))
    return hidden_res + matmul(activ, down_mat) + down_bias

def adamw(weight, grad, first, second, average, rate, decay):
    first_new = BETA_ONE * first + (1.0 - BETA_ONE) * grad
    second_new = BETA_TWO * second + (1.0 - BETA_TWO) * grad * grad
    first_hat = first_new / (1.0 - BETA_ONE ** STEP)
    second_hat = second_new / (1.0 - BETA_TWO ** STEP)
    weight_new = weight - rate * (first_hat / (jnp.sqrt(second_hat) + ADAM_EPS) + decay * weight)
    average_new = EMA_KEEP * average + (1.0 - EMA_KEEP) * weight_new
    return (first_new, second_new, weight_new, average_new)

def reference(tokens, cotangent, cond_frames, qkv_weight, proj_weight, up_weight, down_weight, vectors, qkv_first, proj_first, up_first, down_first, vector_first, qkv_second, proj_second, up_second, down_second, vector_second, qkv_average, proj_average, up_average, down_average, vector_average):
    inputs = tokens.astype(jnp.float32)
    output, pullback = jax.vjp(forward, inputs, qkv_weight, proj_weight, up_weight, down_weight, vectors)
    positions = jnp.arange(TOKENS)
    frame_of = positions % CLIP_LEN // FRAME_TOK
    clip_of = positions // CLIP_LEN
    keep_rows = (frame_of >= cond_frames[clip_of]).astype(jnp.float32)
    back = cotangent.astype(jnp.float32) * keep_rows[:, None]
    grads = pullback(back)
    qkv_f, qkv_s, qkv_w, qkv_e = adamw(qkv_weight, grads[1], qkv_first, qkv_second, qkv_average, RATE_MATRIX, WEIGHT_DECAY)
    proj_f, proj_s, proj_w, proj_e = adamw(proj_weight, grads[2], proj_first, proj_second, proj_average, RATE_MATRIX, WEIGHT_DECAY)
    up_f, up_s, up_w, up_e = adamw(up_weight, grads[3], up_first, up_second, up_average, RATE_MATRIX, WEIGHT_DECAY)
    down_f, down_s, down_w, down_e = adamw(down_weight, grads[4], down_first, down_second, down_average, RATE_MATRIX, WEIGHT_DECAY)
    vec_f, vec_s, vec_w, vec_e = adamw(vectors, grads[5], vector_first, vector_second, vector_average, RATE_VECTOR, 0.0)
    return (output.astype(jnp.bfloat16), grads[0], qkv_f, qkv_s, qkv_w, qkv_e, proj_f, proj_s, proj_w, proj_e, up_f, up_s, up_w, up_e, down_f, down_s, down_w, down_e, vec_f, vec_s, vec_w, vec_e)
```

```python
import functools
from types import SimpleNamespace

import jax
import jax.numpy as jnp
from jax import lax
from jax.experimental import pallas as pl
from jax.experimental.pallas import tpu as pltpu
from jax.sharding import PartitionSpec as P

D = 512
FF = 2048
HEADS = 8
HEAD_DIM = 64
FRAME_TOK = 64
STEP = 10
CLIP_LEN = 1024
VEC = 9 * D + FF

EPS = 1e-05
BETA_ONE = 0.9
BETA_TWO = 0.95
ADAM_EPS = 1e-08
RATE_MATRIX = 0.02
RATE_VECTOR = 0.2
WEIGHT_DECAY = 0.1
EMA_KEEP = 0.9
NEG = -1e30

AXES = ("dp", "fsdp")
MESH = pl.DeviceIdType.MESH
BF16 = jnp.bfloat16
F32 = jnp.float32
NN = (((1,), (0,)), ((), ()))
NT = (((1,), (1,)), ((), ()))
TN = (((0,), (0,)), ((), ()))
PAIRS = HEADS // 2
QB = 256
TILE = 512
CHUNK = 512
VROWS = 56
G1, S1, BQKV, BO, G2, S2, B1, B2 = 0, 4, 8, 20, 24, 28, 32, 48
GELU_A = 0.7978845608028654
GELU_B = 0.044715


def dot(left, right, dims=NN):
    return lax.dot_general(left, right, dims, preferred_element_type=F32)


def place(dp, fs):
    hi, lo = dp.bit_length() - 1, fs.bit_length() - 1
    i, f = lax.axis_index("dp"), lax.axis_index("fsdp")
    me = [(i // 2 ** (hi - 1 - t)) % 2 for t in range(hi)]
    me += [(f // 2 ** (lo - 1 - t)) % 2 for t in range(lo)]

    def partner(t):
        if t < hi:
            step = 2 ** (hi - 1 - t)
            return (i + step - 2 * step * me[t], f)
        step = 2 ** (hi + lo - 1 - t)
        return (i, f + step - 2 * step * me[t])

    return me, partner


def remote(src, dst, send, recv, device):
    return pltpu.make_async_remote_copy(
        src_ref=src, dst_ref=dst, send_sem=send, recv_sem=recv, device_id=device, device_id_type=MESH
    )


class Gather:
    def __init__(self, me, partner, order, buf, cols, send, recv):
        self.copies = []
        done = set()
        for k, t in enumerate(order):
            at = tuple(slice(None) if u in done else me[u] for u in range(len(me)))
            ref = buf.at[at + (slice(None), cols)]
            self.copies.append(remote(ref, ref, send.at[k], recv.at[k], partner(t)))
            done.add(t)

    def step(self, k):
        if k:
            self.copies[k - 1].wait_recv()
        if k < len(self.copies):
            self.copies[k].start()
        else:
            for copy in self.copies:
                copy.wait_send()


class Sum:
    def __init__(self, partner, order, held, come, send, recv):
        self.held, self.come = held, come
        self.copies = [
            remote(held.at[k], come.at[k], send.at[k], recv.at[k], partner(t))
            for k, t in enumerate(order)
        ]

    def step(self, k):
        if k:
            self.copies[k - 1].wait_recv()
            self.held[k] = self.held[k - 1] + self.come[k - 1]
        if k < len(self.copies):
            self.copies[k].start()
        else:
            for copy in self.copies:
                copy.wait_send()


class Scatter:
    def __init__(self, me, partner, order, stage, cols, come, come_cols, send, recv, finish):
        self.finish = finish
        self.copies, self.kept, self.landed = [], [], []
        left = list(range(len(me)))
        source, source_cols = stage, cols
        for k, t in enumerate(order):
            pos = left.index(t)
            every = [slice(None)] * len(left)
            keep, give = list(every), list(every)
            keep[pos], give[pos] = me[t], 1 - me[t]
            left.remove(t)
            landing = (slice(None),) * (len(left) + 1) + (come_cols,)
            self.copies.append(
                remote(
                    source.at[tuple(give) + (slice(None), source_cols)],
                    come[k].at[landing],
                    send.at[k],
                    recv.at[k],
                    partner(t),
                )
            )
            self.kept.append((source, tuple(keep) + (slice(None), source_cols)))
            self.landed.append((come[k], landing))
            source, source_cols = come[k], come_cols

    def step(self, k):
        if k:
            self.copies[k - 1].wait_recv()
            kept, kept_at = self.kept[k - 1]
            land, land_at = self.landed[k - 1]
            total = kept[kept_at].astype(F32) + land[land_at].astype(F32)
            if k < len(self.copies):
                land[land_at] = total.astype(BF16)
            else:
                self.finish(total)
        if k < len(self.copies):
            self.copies[k].start()
        else:
            for copy in self.copies:
                copy.wait_send()


ORDER = ((0, 1, 2, 3, 4), (0, 1, 3, 2, 4))
LINK = ("z", "z", "y", "x", "core")


def streams_of():
    gathers = [("vec", 0, VROWS * 512, 0)]
    gathers += [(f"q{p}", 16 * 384 * 2, 0, p % 2) for p in range(PAIRS)]
    gathers += [("o", 16 * 512 * 2, 0, 0)]
    gathers += [(f"d{i}", 64 * 256 * 2, 0, i % 2) for i in range(2)]
    gathers += [(f"u{i}", 16 * 512 * 2, 0, (i + 1) % 2) for i in range(4)]
    return gathers


def steps_of():
    steps = [("norm", 0, 3.0, [], []), ("affine", 0, 0.8, ["vec"], [])]
    steps += [("fwd", t, 2.2 + (t % 2 == 0), [f"q{t // 2}"], []) for t in range(2 * PAIRS)]
    steps += [("mid", 0, 3.0, ["o"], [])]
    for c in range(FF // CHUNK):
        steps += [("ffa", c, 7.5, ["d0", "d1", f"u{c}"], []), ("ffb", c, 2.5, [], [f"u{c}"])]
    steps[-1][4].extend(["d0", "d1"])
    steps += [("ln2", 0, 5.0, [], ["o"])]
    steps += [("bwd", t, 3.8 + (t % 2), [], [f"q{t // 2}"] if t % 2 else []) for t in range(2 * PAIRS)]
    steps += [("ln1", t, 1.6, [], ["vec"] if t == 3 else []) for t in range(4)]
    steps += [("end", 0, 0.0, ["all"], [])]
    return steps


def plan_of():
    latency = {"z": 2.2, "y": 2.2, "x": 2.2, "core": 0.8}
    rate = {"z": 45e3, "y": 45e3, "x": 45e3, "core": 250e3}
    free = dict.fromkeys(rate, 0.0)
    streams = streams_of()
    info = {name: (share, fixed, ORDER[which]) for name, share, fixed, which in streams}
    bits = len(LINK)
    pending = [("g", name, 0, 0.0) for name, *_ in streams]
    rank = {("g", s[0]): i for i, s in enumerate(streams)}
    plan = {}
    now = 0.0

    def cost(kind, name, k):
        share, fixed, order = info[name]
        bit = (order if kind == "g" else order[::-1])[k]
        size = fixed or share * 2 ** (k if kind == "g" else bits - 1 - k)
        return LINK[bit], size * (2 if bit == 0 else 1) / rate[LINK[bit]]

    def start_of(item):
        kind, name, k, ready = item
        if k == bits:
            return ready
        return max(ready, free[cost(kind, name, k)[0]])

    def issue(item, at):
        kind, name, k, ready = item
        pending.remove(item)
        if k == bits:
            return
        link, time = cost(kind, name, k)
        begin = max(at, free[link])
        free[link] = begin + time
        pending.append((kind, name, k + 1, begin + time + latency[link]))

    for name, index, time, needs, feeds in steps_of():
        taken = plan.setdefault((name, index), [])

        def open_needs():
            if "all" in needs:
                return list(pending)
            return [i for i in pending if i[0] == "g" and i[1] in needs]

        while True:
            ready = [i for i in pending if start_of(i) <= now + 0.3 and i[3] <= now]
            if ready:
                item = min(ready, key=lambda i: (start_of(i), rank.get(i[:2], 99)))
            elif open_needs():
                item = min(pending, key=lambda i: (start_of(i), rank.get(i[:2], 99)))
                now = max(now, start_of(item), item[3])
            else:
                break
            taken.append(item[:3])
            issue(item, now)
        now += time
        for fed in feeds:
            pending.append(("s", fed, 0, now))
    return plan


def norm(values):
    mean = jnp.mean(values, axis=-1, keepdims=True)
    centred = values - mean
    scale = lax.rsqrt(jnp.mean(centred * centred, axis=-1, keepdims=True) + EPS)
    return centred * scale, scale


def norm_back(grad, hat, scale, gain):
    inner = grad * gain
    return scale * (
        inner
        - jnp.mean(inner, axis=-1, keepdims=True)
        - hat * jnp.mean(inner * hat, axis=-1, keepdims=True)
    )


def gelu_both(pre):
    square = pre * pre
    tanh = jnp.tanh(pre * (GELU_A + (GELU_A * GELU_B) * square))
    half = 0.5 + 0.5 * tanh
    act = pre * half
    return act, half + act * (1.0 - tanh) * (GELU_A + (3 * GELU_A * GELU_B) * square)


def column_sum(values):
    return jnp.sum(values, axis=0, keepdims=True)


def attend_forward(qkv, mixed, lse, row0, pair):
    rows = lambda start, size: pl.ds(pl.multiple_of(row0 + start, QB), size)
    cols = lambda part: pl.ds(pl.multiple_of(pair * 384 + part * 128, 128), 128)
    out_cols = pl.ds(pl.multiple_of(pair * 128, 128), 128)
    low_all = lax.broadcasted_iota(jnp.int32, (CLIP_LEN, 128), 1) < 64
    lane = lax.broadcasted_iota(jnp.int32, (QB, 128), 1)
    low = lane < 64
    spare = lane & 63
    causal = lax.broadcasted_iota(jnp.int32, (QB, QB), 1) <= lax.broadcasted_iota(
        jnp.int32, (QB, QB), 0
    )
    one, zero = jnp.ones((), BF16), jnp.zeros((), BF16)
    queries = qkv[rows(0, CLIP_LEN), cols(0)] * jnp.asarray(HEAD_DIM**-0.5, BF16)
    keys = qkv[rows(0, CLIP_LEN), cols(1)]
    values = qkv[rows(0, CLIP_LEN), cols(2)]
    head_q = [jnp.where(low_all, queries, zero), jnp.where(low_all, zero, queries)]
    head_v = [jnp.where(low_all, values, one), jnp.where(low_all, one, values)]

    def scores(item):
        block, head = item
        n = QB * block
        s = dot(head_q[head][n : n + QB], keys[: n + QB], NT)
        diagonal = jnp.where(causal, s[:, n:], NEG)
        return jnp.concatenate([s[:, :n], diagonal], axis=1) if n else diagonal

    items = [(block, head) for block in reversed(range(CLIP_LEN // QB)) for head in range(2)]
    ahead = 3
    ready = {t: scores(items[t]) for t in range(ahead)}
    sums, tops = {}, {}
    for t, (block, head) in enumerate(items):
        s = ready.pop(t)
        top = jnp.max(s, axis=1, keepdims=True)
        if t + ahead < len(items):
            ready[t + ahead] = scores(items[t + ahead])
        weights = jnp.exp(s - top).astype(BF16)
        sums[head] = dot(weights, head_v[head][: QB * (block + 1)])
        tops[head] = top
        if head == 1:
            at = rows(QB * block, QB)
            top_sum = jnp.where(low, sums[0], sums[1])
            total = jnp.where(low, sums[1], sums[0])
            mixed[at, out_cols] = (top_sum / pltpu.roll(total, 64, 1)).astype(BF16)
            log_sum = jnp.where(low, tops[1], tops[0]) + jnp.log(total)
            high = log_sum.astype(BF16).astype(F32)
            lse[at, out_cols] = jnp.where(
                spare == 0, -high, jnp.where(spare == 1, high - log_sum, 0.0)
            ).astype(BF16)


def attend_backward(qkv, grad, lse, dots, grad_qkv, grad_qt, row0, pair):
    rows = lambda start, size: pl.ds(pl.multiple_of(row0 + start, QB), size)
    cols = lambda part: pl.ds(pl.multiple_of(pair * 384 + part * 128, 128), 128)
    one_cols = pl.ds(pl.multiple_of(pair * 128, 128), 128)
    low = lax.broadcasted_iota(jnp.int32, (CLIP_LEN, 128), 1) < 64
    causal = lax.broadcasted_iota(jnp.int32, (QB, QB), 0) <= lax.broadcasted_iota(
        jnp.int32, (QB, QB), 1
    )
    one, zero = jnp.ones((), BF16), jnp.zeros((), BF16)
    every = rows(0, CLIP_LEN)
    queries = qkv[every, cols(0)] * jnp.asarray(HEAD_DIM**-0.5, BF16)
    keys = qkv[every, cols(1)]
    values = qkv[every, cols(2)]
    out_grad = grad[every, one_cols]
    shift = lse[every, one_cols]
    row_dot = dots[every, one_cols]
    pick = lambda head, a, b: jnp.where(low, a, b) if head == 0 else jnp.where(low, b, a)
    q_shift = [pick(h, queries, shift) for h in range(2)]
    k_one = [pick(h, keys, one) for h in range(2)]
    v_one = [pick(h, values, one) for h in range(2)]
    g_shift = [pick(h, out_grad, row_dot) for h in range(2)]
    q_zero = [pick(h, queries, zero) for h in range(2)]
    g_zero = [pick(h, out_grad, zero) for h in range(2)]
    keys_t = keys.T
    items = [(block, head) for block in range(CLIP_LEN // QB) for head in range(2)]

    def products(item):
        block, head = item
        n = QB * block
        return (
            dot(k_one[head][n : n + QB], q_shift[head][n:], NT),
            dot(v_one[head][n : n + QB], g_shift[head][n:], NT),
        )

    ahead = 2
    ready = {t: products(items[t]) for t in range(ahead)}
    kept = {}
    for t, (block, head) in enumerate(items):
        n = QB * block
        s, grad_p = ready.pop(t)
        if t + ahead < len(items):
            ready[t + ahead] = products(items[t + ahead])
        probs = jnp.exp(s)
        diagonal = jnp.where(causal, probs[:, :QB], 0.0)
        probs = jnp.concatenate([diagonal, probs[:, QB:]], axis=1) if n + QB < CLIP_LEN else diagonal
        grad_s = (probs * grad_p).astype(BF16)
        kept[head] = (dot(grad_s, q_zero[head][n:]), dot(probs.astype(BF16), g_zero[head][n:]))
        half = slice(64 * head, 64 * head + 64)
        part = dot(keys_t[half, n : n + QB], grad_s)
        if block == 0:
            grad_qt[half, :] = part
        else:
            grad_qt[half, n:] = grad_qt[half, n:] + part
        if head == 1:
            at = rows(n, QB)
            grad_qkv[at, cols(1)] = (kept[0][0] + kept[1][0]).astype(BF16)
            grad_qkv[at, cols(2)] = (kept[0][1] + kept[1][1]).astype(BF16)
    grad_qkv[every, cols(0)] = (grad_qt[...].T * HEAD_DIM**-0.5).astype(BF16)


def block_kernel(dp, fs, tokens_n, linked, names, *refs):
    r = SimpleNamespace(**dict(zip(names, refs)))
    clips = tokens_n // CLIP_LEN
    tiles = tokens_n // TILE
    chunks = FF // CHUNK
    bits = len(LINK) if linked else 0
    lead = (slice(None),) * bits

    load_x = pltpu.make_async_copy(r.tokens, r.x, r.local.at[0])
    load_cot = pltpu.make_async_copy(r.cotangent, r.dy, r.local.at[1])
    load_x.start()
    load_cot.start()

    if linked:
        me, partner = place(dp, fs)
        barrier = pltpu.get_barrier_semaphore()
        for t in range(bits):
            pl.semaphore_signal(barrier, inc=1, device_id=partner(t), device_id_type=MESH)
        own = tuple(me)

        def share(flat, buf, rows, width, place_of):
            for j in range(width):
                part = flat[pl.ds(j, rows, stride=width), :].astype(BF16)
                buf[own + (slice(None), slice(128 * place_of(j), 128 * place_of(j) + 128))] = part

        per = VEC // (dp * fs)
        start = (lax.axis_index("dp") * fs + lax.axis_index("fsdp")) * per
        row, lane0 = start // 128, start % 128
        part = r.vectors[...].astype(BF16).astype(F32)
        lane = lax.broadcasted_iota(jnp.int32, (1, 128), 1)
        first = pltpu.roll(part[:, :128], lane0, 1)
        tail = jnp.concatenate([part[:, 128:], jnp.zeros((1, 256 - per), F32)], axis=1)
        second = pltpu.roll(tail, lane0, 1)
        r.vec[0] = jnp.zeros((VROWS, 128), F32)
        r.vec[0, pl.ds(row, 1), :] = jnp.where(lane >= lane0, first, 0.0)
        r.vec[0, pl.ds(row + 1, 1), :] = jnp.where(lane < lane0, first, second)
        r.vec[0, pl.ds(row + 2, 1), :] = jnp.where(lane < lane0, second, 0.0)
        share(r.qkv_weight, r.wq, 16, 12, lambda j: (j % PAIRS) * 3 + j // PAIRS)
        share(r.proj_weight, r.wo, 16, 4, lambda j: j)
        share(r.up_weight, r.w1, 16, 16, lambda j: j)
        share(r.down_weight, r.w2, 64, 4, lambda j: j)

        jobs = {}
        for n, (name, _, _, which) in enumerate(streams_of()):
            order = ORDER[which]
            gs, gr, ss, sr = r.gather_send.at[n], r.gather_recv.at[n], r.sum_send.at[n], r.sum_recv.at[n]
            kind, number = name[0], int(name[1:]) if name[1:].isdigit() else 0
            back = order[::-1]
            if name == "vec":
                jobs["g", name] = Sum(partner, order, r.vec, r.vec_come, gs, gr)
                jobs["s", name] = Sum(partner, back, r.gvec, r.gvec_come, ss, sr)
                continue
            rows, width, base, matrix, stage, come, come0 = {
                "q": (16, 384, 0, r.wq, r.sq, r.come, 0),
                "o": (16, 512, 192, r.wo, r.wo, r.come, 1536),
                "u": (16, 512, 256, r.w1, r.w1, r.come, 2048),
                "d": (64, 256, 512, r.w2, r.w2, r.come_down, 0),
            }[kind]
            cols = slice(number * width, number * width + width)
            come_cols = slice(come0 + number * width, come0 + number * width + width)

            def finish(total, kind=kind, number=number, rows=rows, width=width, base=base):
                for j in range(width // 128):
                    col = j * PAIRS + number if kind == "q" else number * (width // 128) + j
                    stride = {"q": 12, "o": 4, "u": 16, "d": 4}[kind]
                    r.total[pl.ds(base + col, rows, stride=stride), :] = total[:, 128 * j : 128 * j + 128]

            jobs["g", name] = Gather(me, partner, order, matrix, cols, gs, gr)
            jobs["s", name] = Scatter(
                me, partner, back, stage, cols, come, come_cols, ss, sr, finish
            )
        plan = plan_of()
        pl.semaphore_wait(barrier, bits)
    else:
        loads = [
            pltpu.make_async_copy(src, dst, r.local.at[3 + n])
            for n, (src, dst) in enumerate(
                [(r.qkv_mat, r.wq), (r.proj_mat, r.wo), (r.up_mat, r.w1), (r.down_mat, r.w2)]
            )
        ]
        for load in loads:
            load.start()
        r.vec[0] = r.vec_in[...]
        for load in loads:
            load.wait()

    def exchange(name, index):
        if not linked:
            return
        for (step, at), taken in plan.items():
            if step != name or not taken:
                continue

            def act(taken=taken):
                for kind, stream, k in taken:
                    jobs[kind, stream].step(k)

            if isinstance(index, int):
                if index == at:
                    act()
            else:
                pl.when(index == at)(act)

    vec = r.vec.at[bits]
    gvec = r.gvec.at[0]
    gvec[...] = jnp.zeros((VROWS, 128), F32)

    def vector(first, count):
        return jnp.concatenate([vec[first + n : first + n + 1, :] for n in range(count)], axis=1)

    def add_vector(first, values):
        for n in range(values.shape[1] // 128):
            gvec[first + n : first + n + 1, :] += values[:, 128 * n : 128 * n + 128]

    def whole(ref, cols):
        got = ref[lead + (slice(None), cols)]
        return got.reshape(-1, got.shape[-1])

    def down_chunk(c):
        if linked:
            return r.w2[c // 2, c % 2].reshape(CHUNK, D)
        return r.w2[pl.ds(pl.multiple_of(c * CHUNK, CHUNK), CHUNK), :]

    rows_of = lambda i, size: pl.ds(pl.multiple_of(i * size, size), size)
    act = lambda rows: r.big.at[rows, pl.ds(0, 512)]
    grad_pre = lambda rows: r.big.at[rows, pl.ds(512, 512)]
    normed_two = lambda rows: r.big.at[rows, pl.ds(1024, 512)]
    everything = pl.ds(0, tokens_n)

    exchange("norm", 0)
    load_x.wait()

    def norm_one(i, carry):
        rows = rows_of(i, 256)
        r.hat[rows, :] = norm(r.x[rows, :].astype(F32))[0]
        return carry

    lax.fori_loop(0, tokens_n // 256, norm_one, 0)
    exchange("affine", 0)

    def affine_one(i, carry):
        rows = rows_of(i, 256)
        r.a[rows, :] = (r.hat[rows, :] * vector(G1, 4) + vector(S1, 4)).astype(BF16)
        return carry

    lax.fori_loop(0, tokens_n // 256, affine_one, 0)

    def forward(t, carry):
        exchange("fwd", t)
        pair, clip = t // clips, t % clips

        @pl.when(clip == 0)
        def _():
            cols = pl.ds(pl.multiple_of(pair * 384, 128), 384)
            matrix = whole(r.wq, cols)
            bias = jnp.concatenate([vec[pl.ds(BQKV + 4 * n + pair, 1), :] for n in range(3)], axis=1)
            for i in range(tiles):
                rows = slice(i * TILE, i * TILE + TILE)
                r.qkv[rows, cols] = (dot(r.a[rows, :], matrix) + bias).astype(BF16)

        attend_forward(r.qkv, r.mixed, r.lse, clip * CLIP_LEN, pair)
        return carry

    lax.fori_loop(0, PAIRS * clips, forward, 0)

    exchange("mid", 0)
    load_cot.wait()

    def middle(i, carry):
        rows = rows_of(i, TILE)
        h = r.x[rows, :].astype(F32) + dot(r.mixed[rows, :], whole(r.wo, slice(None))) + vector(BO, 4)
        hat, scale = norm(h)
        r.hat[rows, :] = hat
        r.scale[rows, :] = jnp.broadcast_to(scale, (TILE, 128))
        normed_two(rows)[...] = (hat * vector(G2, 4) + vector(S2, 4)).astype(BF16)
        r.total_out[rows, :] = h + vector(B2, 4)
        r.grad_h[rows, :] = jnp.zeros((TILE, D), F32)
        per = CLIP_LEN // TILE
        place_in = (i % per) * TILE + lax.broadcasted_iota(jnp.int32, (TILE, 1), 0)
        dy = jnp.where(place_in >= r.cond_frames[i // per] * FRAME_TOK, r.dy[rows, :].astype(F32), 0.0)
        add_vector(B2, column_sum(dy))
        r.dy[rows, :] = dy.astype(BF16)
        return carry

    lax.fori_loop(0, tiles, middle, 0)

    def feed(c, carry):
        exchange("ffa", c)
        cols = pl.ds(pl.multiple_of(c * CHUNK, CHUNK), CHUNK)
        up, down = whole(r.w1, cols), down_chunk(c)
        bias = jnp.concatenate([vec[pl.ds(B1 + 4 * c + n, 1), :] for n in range(4)], axis=1)
        spans = [slice(i * TILE, i * TILE + TILE) for i in range(tiles)]

        def products(rows):
            return dot(normed_two(rows)[...], up), dot(r.dy[rows, :], down, NT)

        ready = products(spans[0])
        bias_grad = jnp.zeros((1, CHUNK), F32)
        for i, rows in enumerate(spans):
            pre, grad_act = ready
            if i + 1 < tiles:
                ready = products(spans[i + 1])
            value, slope = gelu_both(pre + bias)
            value = value.astype(BF16)
            grad = (slope * grad_act).astype(BF16)
            bias_grad = bias_grad + column_sum(grad.astype(F32))
            act(rows)[...] = value
            grad_pre(rows)[...] = grad
            r.total_out[rows, :] += dot(value, down)
            r.grad_h[rows, :] += dot(grad, up, NT)
        for n in range(4):
            gvec[pl.ds(B1 + 4 * c + n, 1), :] = bias_grad[:, 128 * n : 128 * n + 128]
        exchange("ffb", c)
        grad_up = dot(normed_two(everything)[...], grad_pre(everything)[...], TN).astype(BF16)
        grad_down = dot(act(everything)[...], r.dy[...], TN).astype(BF16)
        if linked:
            r.w1[lead + (slice(None), cols)] = grad_up.reshape((2,) * bits + (16, CHUNK))
            r.w2[c // 2, c % 2] = grad_down.reshape((2,) * (bits - 2) + (64, D))
        else:
            r.w1[:, cols] = grad_up
            r.w2[rows_of(c, CHUNK), :] = grad_down
        return carry

    lax.fori_loop(0, chunks, feed, 0)

    exchange("ln2", 0)
    ri = lax.broadcasted_iota(jnp.int32, (128, 128), 0)
    ci = lax.broadcasted_iota(jnp.int32, (128, 128), 1)
    other_half = jnp.where((ri < 64) != (ci < 64), 1.0, 0.0).astype(BF16)
    spare = lax.broadcasted_iota(jnp.int32, (TILE, 128), 1) & 63
    proj = whole(r.wo, slice(None))
    grad_proj = jnp.zeros((D, D), F32)
    for i in range(tiles):
        rows = slice(i * TILE, i * TILE + TILE)
        r.out_low[rows, :] = r.total_out[rows, :].astype(BF16)
        grad, hat, scale = r.grad_h[rows, :], r.hat[rows, :], r.scale[rows, :1]
        add_vector(G2, column_sum(grad * hat))
        add_vector(S2, column_sum(grad))
        grad = r.dy[rows, :].astype(F32) + norm_back(grad, hat, scale, vector(G2, 4))
        r.grad_h[rows, :] = grad
        low = grad.astype(BF16)
        add_vector(BO, column_sum(low.astype(F32)))
        mixed = r.mixed[rows, :]
        grad_proj = grad_proj + dot(mixed, low, TN)
        grad_mixed = dot(low, proj, NT).astype(BF16)
        r.dy[rows, :] = grad_mixed
        product = grad_mixed.astype(F32) * mixed.astype(F32)
        high = product.astype(BF16)
        rest = (product - high.astype(F32)).astype(BF16)
        for p in range(PAIRS):
            cols = slice(128 * p, 128 * p + 128)
            row_dot = dot(high[:, cols], other_half) + dot(rest[:, cols], other_half)
            top = row_dot.astype(BF16).astype(F32)
            r.mixed[rows, cols] = jnp.where(
                spare == 0, -top, jnp.where(spare == 1, top - row_dot, 0.0)
            ).astype(BF16)
    grad_proj = grad_proj.astype(BF16)
    if linked:
        r.wo[...] = grad_proj.reshape((2,) * bits + (16, D))
    else:
        r.wo[...] = grad_proj
    store_out = pltpu.make_async_copy(r.out_low, r.output, r.local.at[2])
    store_out.start()

    def backward(t, carry):
        exchange("bwd", t)
        pair, clip = t // clips, t % clips
        attend_backward(r.qkv, r.dy, r.lse, r.mixed, r.big, r.grad_qt, clip * CLIP_LEN, pair)

        @pl.when(clip == clips - 1)
        def _():
            cols = pl.ds(pl.multiple_of(pair * 384, 128), 384)
            grad = r.big[:, cols]
            sums = column_sum(grad.astype(F32))
            for n in range(3):
                gvec[pl.ds(BQKV + 4 * n + pair, 1), :] = sums[:, 128 * n : 128 * n + 128]
            matrix = dot(r.a[...], grad, TN).astype(BF16)
            if linked:
                r.sq[lead + (slice(None), cols)] = matrix.reshape((2,) * bits + (16, 384))
            else:
                r.sq[:, cols] = matrix

        return carry

    lax.fori_loop(0, PAIRS * clips, backward, 0)

    def first_back(i, carry):
        exchange("ln1", i)
        rows = rows_of(i, TILE)
        grad = dot(r.big[rows, :], whole(r.wq, slice(None)), NT)
        hat, scale = norm(r.x[rows, :].astype(F32))
        add_vector(G1, column_sum(grad * hat))
        add_vector(S1, column_sum(grad))
        r.grad_h[rows, :] += norm_back(grad, hat, scale, vector(G1, 4))
        return carry

    lax.fori_loop(0, tiles, first_back, 0)
    store_grad = pltpu.make_async_copy(r.grad_h, r.input_grad, r.local.at[3])
    store_grad.start()
    exchange("end", 0)
    if linked:
        r.total_vec[...] = r.gvec[bits]
    else:
        stores = [
            pltpu.make_async_copy(src, dst, r.local.at[4 + n])
            for n, (src, dst) in enumerate(
                [(r.sq, r.qkv_grad), (r.wo, r.proj_grad), (r.w1, r.up_grad), (r.w2, r.down_grad)]
            )
        ]
        for store in stores:
            store.start()
        for store in stores:
            store.wait()
        r.total_vec[...] = gvec[...]
    store_out.wait()
    store_grad.wait()


def run_block(dp, fs, linked, tokens, cotangent, cond_frames, weights):
    n = tokens.shape[0]
    shape = jax.ShapeDtypeStruct
    vmem, smem, any_ = (
        pl.BlockSpec(memory_space=pltpu.VMEM),
        pl.BlockSpec(memory_space=pltpu.SMEM),
        pl.BlockSpec(memory_space=pl.ANY),
    )
    bits = len(LINK) if linked else 0
    ins = ["tokens", "cotangent", "cond_frames"]
    in_specs = [any_, any_, smem]
    outs = {"output": ((n, D), BF16, any_), "input_grad": ((n, D), F32, any_)}
    outs["total_vec"] = ((VROWS, 128), F32, vmem)
    if linked:
        ins += ["qkv_weight", "proj_weight", "up_weight", "down_weight", "vectors"]
        in_specs += [vmem] * 5
        outs["total"] = ((768, 128), F32, vmem)
        matrix = lambda rows, cols: pltpu.VMEM((2,) * bits + (rows // 2**bits, cols), BF16)
    else:
        ins += ["qkv_mat", "proj_mat", "up_mat", "down_mat", "vec_in"]
        in_specs += [any_] * 4 + [vmem]
        outs["qkv_grad"] = ((D, 3 * D), BF16, any_)
        outs["proj_grad"] = ((D, D), BF16, any_)
        outs["up_grad"] = ((D, FF), BF16, any_)
        outs["down_grad"] = ((FF, D), BF16, any_)
        matrix = lambda rows, cols: pltpu.VMEM((rows, cols), BF16)
    scratch = {
        "x": pltpu.VMEM((n, D), BF16),
        "a": pltpu.VMEM((n, D), BF16),
        "dy": pltpu.VMEM((n, D), BF16),
        "qkv": pltpu.VMEM((n, 3 * D), BF16),
        "mixed": pltpu.VMEM((n, D), BF16),
        "lse": pltpu.VMEM((n, D), BF16),
        "hat": pltpu.VMEM((n, D), F32),
        "total_out": pltpu.VMEM((n, D), F32),
        "grad_h": pltpu.VMEM((n, D), F32),
        "scale": pltpu.VMEM((n, 128), F32),
        "big": pltpu.VMEM((n, 3 * D), BF16),
        "out_low": pltpu.VMEM((n, D), BF16),
        "grad_qt": pltpu.VMEM((128, CLIP_LEN), F32),
        "wq": matrix(D, 3 * D),
        "sq": matrix(D, 3 * D),
        "wo": matrix(D, D),
        "w1": matrix(D, FF),
        "w2": matrix(FF, D),
        "vec": pltpu.VMEM((bits + 1, VROWS, 128), F32),
        "gvec": pltpu.VMEM((bits + 1, VROWS, 128), F32),
        "local": pltpu.SemaphoreType.DMA((8,)),
    }
    names = ins + list(outs) + list(scratch)
    shapes = list(scratch.values())
    if linked:
        count = len(streams_of())
        for name in ("vec_come", "gvec_come"):
            names.append(name)
            shapes.append(pltpu.VMEM((bits, VROWS, 128), F32))
        for name in ("gather_send", "gather_recv", "sum_send", "sum_recv"):
            names.append(name)
            shapes.append(pltpu.SemaphoreType.DMA((count, bits)))
        for k in range(bits):
            names.append(f"come{k}")
            shapes.append(pltpu.VMEM((2,) * (bits - 1 - k) + (16, 8 * D), BF16))
        for k in range(bits):
            names.append(f"come_down{k}")
            shapes.append(pltpu.VMEM((2,) * (bits - 1 - k) + (64, D), BF16))

    def body(*refs):
        table = dict(zip(names, refs))
        if linked:
            table["come"] = [table.pop(f"come{k}") for k in range(bits)]
            table["come_down"] = [table.pop(f"come_down{k}") for k in range(bits)]
        block_kernel(dp, fs, n, linked, list(table), *table.values())

    params = dict(vmem_limit_bytes=64 << 20)
    if linked:
        params.update(collective_id=0, has_side_effects=True)
    return pl.pallas_call(
        body,
        out_shape=[shape(s, t) for s, t, _ in outs.values()],
        in_specs=in_specs,
        out_specs=[spec for *_, spec in outs.values()],
        scratch_shapes=shapes,
        compiler_params=pltpu.CompilerParams(**params),
        name="block",
    )(tokens, cotangent, cond_frames, *weights)


def adamw(weight, grad, first, second, average, rate, decay):
    first_new = BETA_ONE * first + (1.0 - BETA_ONE) * grad
    second_new = BETA_TWO * second + (1.0 - BETA_TWO) * grad * grad
    first_hat = first_new / (1.0 - BETA_ONE**STEP)
    second_hat = second_new / (1.0 - BETA_TWO**STEP)
    weight_new = weight - rate * (first_hat / (jnp.sqrt(second_hat) + ADAM_EPS) + decay * weight)
    average_new = EMA_KEEP * average + (1.0 - EMA_KEEP) * weight_new
    return (first_new, second_new, weight_new, average_new)


def adam_kernel(dp, fs, *refs):
    total, total_vec = refs[:2]
    ins, outs = refs[2:22], refs[22:]
    base = 0
    for m in range(4):
        weight, first, second, average = ins[4 * m : 4 * m + 4]
        size = weight.shape[0]
        new = adamw(
            weight[...], total[base : base + size, :], first[...], second[...], average[...],
            RATE_MATRIX, WEIGHT_DECAY,
        )
        for ref, value in zip(outs[4 * m : 4 * m + 4], new):
            ref[...] = value
        base += size
    per = VEC // (dp * fs)
    start = (lax.axis_index("dp") * fs + lax.axis_index("fsdp")) * per
    row, lane0 = start // 128, start % 128
    lane = lax.broadcasted_iota(jnp.int32, (1, 128), 1)
    back = lax.rem(128 - lane0, 128)
    parts = [pltpu.roll(total_vec[pl.ds(row + n, 1), :], back, 1) for n in range(3)]
    keep = 128 - lane0
    grad = jnp.concatenate(
        [jnp.where(lane < keep, parts[0], parts[1]), jnp.where(lane < keep, parts[1], parts[2])], axis=1
    )[:, :per]
    weight, first, second, average = ins[16:]
    new = adamw(
        weight[...], grad, first[...], second[...], average[...], RATE_VECTOR, 0.0
    )
    for ref, value in zip(outs[16:], new):
        ref[...] = value


def run_adam(dp, fs, total, total_vec, state):
    flat = [a.reshape(-1, 128) for a in state[:16]] + list(state[16:])
    vmem = pl.BlockSpec(memory_space=pltpu.VMEM)
    new = pl.pallas_call(
        functools.partial(adam_kernel, dp, fs),
        out_shape=[jax.ShapeDtypeStruct(a.shape, F32) for a in flat],
        in_specs=[vmem] * 22,
        out_specs=[vmem] * 20,
        compiler_params=pltpu.CompilerParams(vmem_limit_bytes=64 << 20),
        name="adam",
    )(total, total_vec, *flat)
    return [a.reshape(b.shape) for a, b in zip(new, state)]


def local(dp, fs, tokens, cotangent, cond_frames, *state):
    weights, firsts, seconds, averages = (state[5 * n : 5 * n + 5] for n in range(4))
    shards = dp * fs
    linked = shards == 2 ** len(LINK) and not (dp & (dp - 1))
    if linked:
        shares = [w.reshape(-1, 128) for w in weights[:4]] + [weights[4]]
        output, input_grad, total_vec, total = run_block(
            dp, fs, True, tokens, cotangent, cond_frames, shares
        )
    else:
        gathered = [
            lax.all_gather(w.astype(BF16), AXES, axis=0, tiled=True) for w in weights
        ]
        qkv = gathered[0].reshape(D, 3, PAIRS, 128).swapaxes(1, 2).reshape(D, 3 * D)
        vec = jnp.pad(gathered[4].astype(F32).reshape(-1, 128), ((0, VROWS - VEC // 128), (0, 0)))
        mats = [qkv] + [g.reshape(-1, c) for g, c in zip(gathered[1:4], (D, FF, D))] + [vec]
        output, input_grad, total_vec, *grads = run_block(
            dp, fs, False, tokens, cotangent, cond_frames, mats
        )
        grads[0] = grads[0].reshape(D, PAIRS, 3, 128).swapaxes(1, 2).reshape(D, 3 * D)
        scatter = lambda g: lax.psum_scatter(
            g.astype(F32).reshape(shards, -1), AXES, scatter_dimension=0, tiled=True
        )
        total = jnp.concatenate([scatter(g).reshape(-1, 128) for g in grads], axis=0)
        total_vec = lax.psum(total_vec, AXES)
    order = [group[m] for m in range(5) for group in (weights, firsts, seconds, averages)]
    new = run_adam(dp, fs, total, total_vec, order)
    return (output, input_grad, *new)


def solution(mesh):
    dp, fs = mesh.shape["dp"], mesh.shape["fsdp"]
    split = P(AXES, None)
    return jax.shard_map(
        functools.partial(local, dp, fs),
        mesh=mesh,
        in_specs=(split, split, P(AXES)) + (split,) * 20,
        out_specs=(split,) * 22,
        check_vma=False,
    )
```

```python
import functools
from types import SimpleNamespace

import jax
import jax.numpy as jnp
from jax import lax
from jax.experimental import pallas as pl
from jax.experimental.pallas import tpu as pltpu
from jax.sharding import PartitionSpec as P

D = 512
FF = 2048
HEADS = 8
HEAD_DIM = 64
FRAME_TOK = 64
STEP = 10
CLIP_LEN = 1024
VEC = 9 * D + FF

EPS = 1e-05
BETA_ONE = 0.9
BETA_TWO = 0.95
ADAM_EPS = 1e-08
RATE_MATRIX = 0.02
RATE_VECTOR = 0.2
WEIGHT_DECAY = 0.1
EMA_KEEP = 0.9
NEG = -1e30

AXES = ("dp", "fsdp")
MESH = pl.DeviceIdType.MESH
BF16 = jnp.bfloat16
F32 = jnp.float32
NN = (((1,), (0,)), ((), ()))
NT = (((1,), (1,)), ((), ()))
TN = (((0,), (0,)), ((), ()))
PAIRS = HEADS // 2
QB = 256
TILE = 512
CHUNK = 512
VROWS = 56
G1, S1, BQKV, BO, G2, S2, B1, B2 = 0, 4, 8, 20, 24, 28, 32, 48
GELU_A = 0.7978845608028654
GELU_B = 0.044715


def dot(left, right, dims=NN):
    return lax.dot_general(left, right, dims, preferred_element_type=F32)


BITS = 5
Z, Y, X, XY, CORE = (0, 1), (2,), (3,), (2, 3), (4,)
LINK = {0: "z", 1: "z", 2: "y", 3: "x", 4: "core"}


def masks_of(hop):
    return [(hop[0],)] if len(hop) == 1 else [(hop[1],), (hop[0],), hop]


def place(dp, fs):
    hi, lo = dp.bit_length() - 1, fs.bit_length() - 1
    i, f = lax.axis_index("dp"), lax.axis_index("fsdp")
    me = [(i // 2 ** (hi - 1 - t)) % 2 for t in range(hi)]
    me += [(f // 2 ** (lo - 1 - t)) % 2 for t in range(lo)]

    def partner(mask):
        at_i, at_f = i, f
        for t in mask:
            if t < hi:
                step = 2 ** (hi - 1 - t)
                at_i = at_i + step - 2 * step * me[t]
            else:
                step = 2 ** (hi + lo - 1 - t)
                at_f = at_f + step - 2 * step * me[t]
        return (at_i, at_f)

    return me, partner


def remote(src, dst, send, recv, device):
    return pltpu.make_async_remote_copy(
        src_ref=src, dst_ref=dst, send_sem=send, recv_sem=recv, device_id=device, device_id_type=MESH
    )


def split_bits(n):
    return tuple(n >> (BITS - 1 - t) & 1 for t in range(BITS))


class Transfer:
    def step(self, k):
        if k:
            for copy in self.hops[k - 1]:
                copy.wait_recv()
            self.arrived(k - 1)
        if k < len(self.hops):
            for copy in self.hops[k]:
                copy.start()
        else:
            for hop in self.hops:
                for copy in hop:
                    copy.wait_send()

    def arrived(self, k):
        pass


class Gather(Transfer):
    def __init__(self, me, partner, hops, left, buf, cols, send, recv):
        self.hops = []
        done, n = set(), 0
        for hop in hops:
            at = tuple(slice(None) if t in done else me[t] for t in left)
            ref = buf.at[at + (slice(None), cols)]
            copies = []
            for mask in masks_of(hop):
                copies.append(remote(ref, ref, send(n), recv(n), partner(mask)))
                n += 1
            self.hops.append(copies)
            done.update(hop)


class Scatter(Transfer):
    def __init__(self, me, partner, hops, left, stage, cols, come, send, recv, finish):
        self.hops, self.sums = [], []
        self.finish = finish
        left, n = list(left), 0
        source, source_cols = stage, cols
        for k, hop in enumerate(hops):

            def part(mask):
                at = [(1 - me[t] if t in mask else me[t]) if t in hop else slice(None) for t in left]
                return tuple(at) + (slice(None), source_cols)

            copies = []
            for slot, mask in enumerate(masks_of(hop)):
                copies.append(
                    remote(source.at[part(mask)], come[k].at[slot], send(n), recv(n), partner(mask))
                )
                n += 1
            self.hops.append(copies)
            self.sums.append((source, part(()), come[k], len(copies)))
            left = [t for t in left if t not in hop]
            source, source_cols = come[k].at[0], slice(None)

    def arrived(self, k):
        source, at, come, count = self.sums[k]
        total = source[at].astype(F32)
        for slot in range(count):
            total = total + come[slot].astype(F32)
        if k + 1 < len(self.hops):
            come[0] = total.astype(come.dtype)
        else:
            self.finish(total)


def streams_of():
    first, second = (Z, Y, X, CORE), (Z, X, Y, CORE)
    every = (0, 1, 2, 3, 4)
    streams = {"vec": ((Z, XY, CORE), every, 8, 128, 4)}
    for p in range(PAIRS):
        hops = (Z, XY, CORE) if p in (0, PAIRS - 1) else (first, second)[p % 2]
        streams[f"q{p}"] = (hops, every, 16, 384, 2)
    streams["o"] = (first, every, 16, 512, 2)
    streams["u0"] = (second, every, 16, 512, 2)
    streams["dz"] = ((Z,), every, 64, 512, 2)
    streams["d0"] = (first[1:], every[2:], 64, 512, 2)
    for c in range(1, FF // CHUNK):
        streams[f"u{c}"] = ((second, first)[c % 2], every, 16, 512, 2)
        streams[f"d{c}"] = ((first, second)[c % 2][1:], every[2:], 64, 512, 2)
    return streams


def steps_of():
    steps = [("norm", 0, 3.0, [], []), ("affine", 0, 0.8, ["vec"], [])]
    steps += [("fwd", t, 2.0 + (t % 2 == 0), [f"q{t // 2}"], []) for t in range(2 * PAIRS)]
    steps += [("mid", 0, 3.0, ["o"], [])]
    for c in range(FF // CHUNK):
        steps += [("ffa", c, 7.5, ["dz", f"d{c}", f"u{c}"], []), ("ffb", c, 2.5, [], [f"u{c}", f"d{c}"])]
    steps += [("ln2", 0, 5.0, [], ["o"])]
    steps += [("bwd", t, 3.5 + (t % 2), [], [f"q{t // 2}"] if t % 2 else []) for t in range(2 * PAIRS)]
    steps += [("sums", t, 1.0, [], ["vec"] if t == 3 else []) for t in range(4)]
    steps += [("ln1", t, 0.6, [], []) for t in range(4)]
    steps += [("end", 0, 0.0, ["all"], [])]
    return steps


def plan_of():
    latency = {"z": 2.0, "y": 2.0, "x": 2.0, "core": 0.8}
    rate = {"z": 45e3, "y": 45e3, "x": 45e3, "core": 250e3}
    free = dict.fromkeys(rate, 0.0)
    streams = streams_of()
    rank = {("g", s): n for n, s in enumerate(streams)}
    rank.update({("s", s): 50 + n for n, s in enumerate(streams)})
    rank["s", f"q{PAIRS - 1}"], rank["s", "vec"] = 1, 0
    arrived = {}
    after = {("g", f"d{c}"): [("g", "dz")] for c in range(4)}
    after["s", "dz"] = [("s", f"d{c}") for c in range(4)]
    pending = [("g", s, 0, 0.0) for s in streams if ("g", s) not in after]
    plan, model = {}, []
    now = 0.0

    def cost(kind, name, k):
        hops, bits, rows, cols, size = streams[name]
        hop = (hops if kind == "g" else hops[::-1])[k]
        done = [t for h in (hops[:k] if kind == "g" else hops[: len(hops) - 1 - k]) for t in h]
        held = rows * cols * size * 2 ** len(done)
        if hop == Z:
            return {"z": 4 * held / rate["z"]}
        if hop == XY:
            return {"x": 2 * held / rate["x"], "y": 2 * held / rate["y"]}
        return {LINK[hop[0]]: held / rate[LINK[hop[0]]]}

    def start_of(item):
        kind, name, k, ready = item
        if k == len(streams[name][0]):
            return ready
        return max([ready] + [free[link] for link in cost(kind, name, k)])

    def issue(item, at):
        kind, name, k, ready = item
        pending.remove(item)
        if k == len(streams[name][0]):
            arrived[kind, name] = max(at, ready)
            for other, needs in after.items():
                if (kind, name) in needs and all(n in arrived for n in needs):
                    pending.append((*other, 0, max(at, ready)))
            return
        begin, end = max(at, start_of(item)), 0.0
        for link, time in cost(kind, name, k).items():
            free[link] = begin + time
            end = max(end, begin + time + latency[link])
        pending.append((kind, name, k + 1, end))

    for name, index, time, needs, feeds in steps_of():
        taken = plan.setdefault((name, index), [])

        def missing():
            if "all" in needs:
                return bool(pending)
            return any(("g", n) not in arrived for n in needs)

        begun = now
        while True:
            ready = [i for i in pending if i[3] <= now and start_of(i) <= now + max(1.0, 0.5 * time)]
            if ready:
                item = min(ready, key=lambda i: rank[i[:2]])
            elif missing():
                item = min(pending, key=lambda i: (max(start_of(i), i[3]), rank[i[:2]]))
                now = max(now, item[3], start_of(item))
            else:
                break
            taken.append(item[:3])
            issue(item, now)
        model.append((begun, now, name, index, taken))
        now += time
        for fed in feeds:
            pending.append(("s", fed, 0, now))
    return plan, model


def norm(values):
    mean = jnp.mean(values, axis=-1, keepdims=True)
    centred = values - mean
    scale = lax.rsqrt(jnp.mean(centred * centred, axis=-1, keepdims=True) + EPS)
    return centred * scale, scale


def norm_back(grad, hat, scale, gain):
    inner = grad * gain
    return scale * (
        inner
        - jnp.mean(inner, axis=-1, keepdims=True)
        - hat * jnp.mean(inner * hat, axis=-1, keepdims=True)
    )


def gelu_both(pre):
    square = pre * pre
    tanh = jnp.tanh(pre * (GELU_A + (GELU_A * GELU_B) * square))
    half = 0.5 + 0.5 * tanh
    act = pre * half
    return act, half + act * (1.0 - tanh) * (GELU_A + (3 * GELU_A * GELU_B) * square)


def column_sum(values):
    return jnp.sum(values, axis=0, keepdims=True)


def attend_forward(qkv, mixed, lse, row0, pair):
    rows = lambda start, size: pl.ds(pl.multiple_of(row0 + start, QB), size)
    cols = lambda part: pl.ds(pl.multiple_of(pair * 384 + part * 128, 128), 128)
    out_cols = pl.ds(pl.multiple_of(pair * 128, 128), 128)
    low_all = lax.broadcasted_iota(jnp.int32, (CLIP_LEN, 128), 1) < 64
    lane = lax.broadcasted_iota(jnp.int32, (QB, 128), 1)
    low = lane < 64
    spare = lane & 63
    causal = lax.broadcasted_iota(jnp.int32, (QB, QB), 1) <= lax.broadcasted_iota(
        jnp.int32, (QB, QB), 0
    )
    one, zero = jnp.ones((), BF16), jnp.zeros((), BF16)
    queries = qkv[rows(0, CLIP_LEN), cols(0)] * jnp.asarray(HEAD_DIM**-0.5, BF16)
    keys = qkv[rows(0, CLIP_LEN), cols(1)]
    values = qkv[rows(0, CLIP_LEN), cols(2)]
    head_q = [jnp.where(low_all, queries, zero), jnp.where(low_all, zero, queries)]
    head_v = [jnp.where(low_all, values, one), jnp.where(low_all, one, values)]

    def scores(item):
        block, head = item
        n = QB * block
        s = dot(head_q[head][n : n + QB], keys[: n + QB], NT)
        diagonal = jnp.where(causal, s[:, n:], NEG)
        return jnp.concatenate([s[:, :n], diagonal], axis=1) if n else diagonal

    items = [(block, head) for block in reversed(range(CLIP_LEN // QB)) for head in range(2)]
    ahead = 3
    ready = {t: scores(items[t]) for t in range(ahead)}
    sums, tops = {}, {}
    for t, (block, head) in enumerate(items):
        s = ready.pop(t)
        top = jnp.max(s, axis=1, keepdims=True)
        if t + ahead < len(items):
            ready[t + ahead] = scores(items[t + ahead])
        weights = jnp.exp(s - top).astype(BF16)
        sums[head] = dot(weights, head_v[head][: QB * (block + 1)])
        tops[head] = top
        if head == 1:
            at = rows(QB * block, QB)
            top_sum = jnp.where(low, sums[0], sums[1])
            total = jnp.where(low, sums[1], sums[0])
            mixed[at, out_cols] = (top_sum / pltpu.roll(total, 64, 1)).astype(BF16)
            log_sum = jnp.where(low, tops[1], tops[0]) + jnp.log(total)
            high = log_sum.astype(BF16).astype(F32)
            lse[at, out_cols] = jnp.where(
                spare == 0, -high, jnp.where(spare == 1, high - log_sum, 0.0)
            ).astype(BF16)


def attend_backward(qkv, grad, lse, dots, grad_qkv, grad_qt, row0, pair):
    rows = lambda start, size: pl.ds(pl.multiple_of(row0 + start, QB), size)
    cols = lambda part: pl.ds(pl.multiple_of(pair * 384 + part * 128, 128), 128)
    one_cols = pl.ds(pl.multiple_of(pair * 128, 128), 128)
    low = lax.broadcasted_iota(jnp.int32, (CLIP_LEN, 128), 1) < 64
    causal = lax.broadcasted_iota(jnp.int32, (QB, QB), 0) <= lax.broadcasted_iota(
        jnp.int32, (QB, QB), 1
    )
    one, zero = jnp.ones((), BF16), jnp.zeros((), BF16)
    every = rows(0, CLIP_LEN)
    queries = qkv[every, cols(0)] * jnp.asarray(HEAD_DIM**-0.5, BF16)
    keys = qkv[every, cols(1)]
    values = qkv[every, cols(2)]
    out_grad = grad[every, one_cols]
    shift = lse[every, one_cols]
    row_dot = dots[every, one_cols]
    pick = lambda head, a, b: jnp.where(low, a, b) if head == 0 else jnp.where(low, b, a)
    q_shift = [pick(h, queries, shift) for h in range(2)]
    k_one = [pick(h, keys, one) for h in range(2)]
    v_one = [pick(h, values, one) for h in range(2)]
    g_shift = [pick(h, out_grad, row_dot) for h in range(2)]
    q_zero = [pick(h, queries, zero) for h in range(2)]
    g_zero = [pick(h, out_grad, zero) for h in range(2)]
    keys_t = keys.T
    items = [(block, head) for block in range(CLIP_LEN // QB) for head in range(2)]

    def products(item):
        block, head = item
        n = QB * block
        return (
            dot(k_one[head][n : n + QB], q_shift[head][n:], NT),
            dot(v_one[head][n : n + QB], g_shift[head][n:], NT),
        )

    ahead = 2
    ready = {t: products(items[t]) for t in range(ahead)}
    kept = {}
    for t, (block, head) in enumerate(items):
        n = QB * block
        s, grad_p = ready.pop(t)
        if t + ahead < len(items):
            ready[t + ahead] = products(items[t + ahead])
        probs = jnp.exp(s)
        diagonal = jnp.where(causal, probs[:, :QB], 0.0)
        probs = jnp.concatenate([diagonal, probs[:, QB:]], axis=1) if n + QB < CLIP_LEN else diagonal
        grad_s = (probs * grad_p).astype(BF16)
        kept[head] = (dot(grad_s, q_zero[head][n:]), dot(probs.astype(BF16), g_zero[head][n:]))
        half = slice(64 * head, 64 * head + 64)
        part = dot(keys_t[half, n : n + QB], grad_s)
        if block == 0:
            grad_qt[half, :] = part
        else:
            grad_qt[half, n:] = grad_qt[half, n:] + part
        if head == 1:
            at = rows(n, QB)
            grad_qkv[at, cols(1)] = (kept[0][0] + kept[1][0]).astype(BF16)
            grad_qkv[at, cols(2)] = (kept[0][1] + kept[1][1]).astype(BF16)
    grad_qkv[every, cols(0)] = (grad_qt[...].T * HEAD_DIM**-0.5).astype(BF16)


def block_kernel(dp, fs, tokens_n, linked, names, *refs):
    r = SimpleNamespace(**dict(zip(names, refs)))
    clips = tokens_n // CLIP_LEN
    tiles = tokens_n // TILE
    chunks = FF // CHUNK
    bits = BITS if linked else 0
    lead = (slice(None),) * bits
    base_of, stride_of = {}, {}

    load_x = pltpu.make_async_copy(r.tokens, r.x, r.local.at[0])
    load_cot = pltpu.make_async_copy(r.cotangent, r.dy, r.local.at[1])
    load_x.start()
    load_cot.start()

    if linked:
        me, partner = place(dp, fs)
        barrier = pltpu.get_barrier_semaphore()
        friends = [mask for hop in (Z, XY, CORE) for mask in masks_of(hop)]
        for mask in friends:
            pl.semaphore_signal(barrier, inc=1, device_id=partner(mask), device_id_type=MESH)
        own = tuple(me)

        def share(flat, buf, rows, width, place_of):
            for j in range(width):
                part = flat[pl.ds(j, rows, stride=width), :].astype(BF16)
                buf[own + (slice(None), slice(128 * place_of(j), 128 * place_of(j) + 128))] = part

        per = VEC // (dp * fs)
        lane0 = (lax.axis_index("dp") * fs + lax.axis_index("fsdp")) * per % 128
        part = r.vectors[...].astype(BF16).astype(F32)
        lane = lax.broadcasted_iota(jnp.int32, (1, 128), 1)
        first = pltpu.roll(part[:, :128], lane0, 1)
        tail = jnp.concatenate([part[:, 128:], jnp.zeros((1, 256 - per), F32)], axis=1)
        second = pltpu.roll(tail, lane0, 1)
        r.vec_parts[own] = jnp.concatenate(
            [
                jnp.where(lane >= lane0, first, 0.0),
                jnp.where(lane < lane0, first, second),
                jnp.where(lane < lane0, second, 0.0),
                jnp.zeros((5, 128), F32),
            ],
            axis=0,
        )
        share(r.qkv_weight, r.wq, 16, 12, lambda j: (j % PAIRS) * 3 + j // PAIRS)
        share(r.proj_weight, r.wo, 16, 4, lambda j: j)
        share(r.up_weight, r.w1, 16, 16, lambda j: j)
        share(r.down_weight, r.w2, 64, 4, lambda j: j)

        jobs = {}
        for n, (name, (hops, left, rows, width, _)) in enumerate(streams_of().items()):
            sems = [lambda k, ref=ref, n=n: ref.at[n, k] for ref in r.sems]
            kind, number = name[0], int(name[1:]) if name[1:].isdigit() else 0
            cols = slice(number * width, number * width + width)
            if name == "vec":
                matrix, stage, cols, base, stride = r.vec_parts, r.gvec_parts, slice(None), 0, 0
            elif kind == "q":
                matrix, stage, base, stride = r.wq, r.sq, 0, 12
            elif kind == "o":
                matrix, stage, base, stride = r.wo, r.wo, 192, 4
            elif kind == "u":
                matrix, stage, base, stride = r.w1, r.w1, 256, 16
            elif name == "dz":
                matrix, stage, cols, base, stride = r.w2, r.down_part, slice(None), 512, 4
            else:
                matrix = stage = r.w2.at[number // 2, number % 2]
                cols = slice(None)

            def finish(total, name=name, kind=kind, number=number, rows=rows, width=width):
                if name == "vec":
                    r.total_vec[...] = total
                elif kind == "d" and name != "dz":
                    r.down_part[number // 2, number % 2] = total.astype(BF16)
                else:
                    for j in range(width // 128):
                        col = j * PAIRS + number if kind == "q" else number * (width // 128) + j
                        at = pl.ds(base_of[name] + col, rows, stride=stride_of[name])
                        r.total[at, :] = total[:, 128 * j : 128 * j + 128]

            if name == "vec" or name == "dz" or kind != "d":
                base_of[name], stride_of[name] = base, stride
            jobs["g", name] = Gather(me, partner, hops, left, matrix, cols, *sems[:2])
            sum_left = left if name != "dz" else Z
            jobs["s", name] = Scatter(
                me, partner, hops[::-1], sum_left, stage, cols, r.come[name], *sems[2:], finish
            )
        plan = plan_of()[0]
        pl.semaphore_wait(barrier, len(friends))
    else:
        loads = [
            pltpu.make_async_copy(src, dst, r.local.at[3 + n])
            for n, (src, dst) in enumerate(
                [(r.qkv_mat, r.wq), (r.proj_mat, r.wo), (r.up_mat, r.w1), (r.down_mat, r.w2)]
            )
        ]
        for load in loads:
            load.start()
        r.vec[...] = r.vec_in[...]
        for load in loads:
            load.wait()

    def exchange(name, index):
        if not linked:
            return
        for (step, at), taken in plan.items():
            if step != name or not taken:
                continue

            def act(taken=taken):
                for kind, stream, k in taken:
                    jobs[kind, stream].step(k)

            if isinstance(index, int):
                if index == at:
                    act()
            else:
                pl.when(index == at)(act)

    vec, gvec = r.vec, r.gvec
    gvec[...] = jnp.zeros((VROWS, 128), F32)

    def vector(first, count):
        return jnp.concatenate([vec[first + n : first + n + 1, :] for n in range(count)], axis=1)

    def add_vector(first, values):
        for n in range(values.shape[1] // 128):
            gvec[first + n : first + n + 1, :] += values[:, 128 * n : 128 * n + 128]

    def whole(ref, cols):
        got = ref[lead + (slice(None), cols)]
        return got.reshape(-1, got.shape[-1])

    def down_chunk(c):
        if linked:
            return r.w2[c // 2, c % 2].reshape(CHUNK, D)
        return r.w2[pl.ds(pl.multiple_of(c * CHUNK, CHUNK), CHUNK), :]

    rows_of = lambda i, size: pl.ds(pl.multiple_of(i * size, size), size)
    act = lambda rows: r.big.at[rows, pl.ds(0, 512)]
    grad_pre = lambda rows: r.big.at[rows, pl.ds(512, 512)]
    normed_two = lambda rows: r.big.at[rows, pl.ds(1024, 512)]
    everything = pl.ds(0, tokens_n)

    exchange("norm", 0)
    load_x.wait()

    def norm_one(i, carry):
        rows = rows_of(i, 256)
        r.hat[rows, :] = norm(r.x[rows, :].astype(F32))[0]
        return carry

    lax.fori_loop(0, tokens_n // 256, norm_one, 0)
    exchange("affine", 0)
    if linked:
        vec[...] = jnp.zeros((VROWS, 128), F32)
        for n in range(dp * fs):
            row = n * per // 128
            vec[row : row + 3, :] += r.vec_parts[split_bits(n) + (slice(0, 3),)]

    def affine_one(i, carry):
        rows = rows_of(i, 256)
        r.a[rows, :] = (r.hat[rows, :] * vector(G1, 4) + vector(S1, 4)).astype(BF16)
        return carry

    lax.fori_loop(0, tokens_n // 256, affine_one, 0)

    def forward(t, carry):
        exchange("fwd", t)
        pair, clip = t // clips, t % clips

        @pl.when(clip == 0)
        def _():
            cols = pl.ds(pl.multiple_of(pair * 384, 128), 384)
            matrix = whole(r.wq, cols)
            bias = jnp.concatenate([vec[pl.ds(BQKV + 4 * n + pair, 1), :] for n in range(3)], axis=1)
            for i in range(tiles):
                rows = slice(i * TILE, i * TILE + TILE)
                r.qkv[rows, cols] = (dot(r.a[rows, :], matrix) + bias).astype(BF16)

        attend_forward(r.qkv, r.mixed, r.lse, clip * CLIP_LEN, pair)
        return carry

    lax.fori_loop(0, PAIRS * clips, forward, 0)

    exchange("mid", 0)
    load_cot.wait()

    def middle(i, carry):
        rows = rows_of(i, TILE)
        h = r.x[rows, :].astype(F32) + dot(r.mixed[rows, :], whole(r.wo, slice(None))) + vector(BO, 4)
        hat, scale = norm(h)
        r.hat[rows, :] = hat
        r.scale[rows, :] = jnp.broadcast_to(scale, (TILE, 128))
        normed_two(rows)[...] = (hat * vector(G2, 4) + vector(S2, 4)).astype(BF16)
        r.total_out[rows, :] = h + vector(B2, 4)
        r.grad_h[rows, :] = jnp.zeros((TILE, D), F32)
        per = CLIP_LEN // TILE
        place_in = (i % per) * TILE + lax.broadcasted_iota(jnp.int32, (TILE, 1), 0)
        dy = jnp.where(place_in >= r.cond_frames[i // per] * FRAME_TOK, r.dy[rows, :].astype(F32), 0.0)
        add_vector(B2, column_sum(dy))
        r.dy[rows, :] = dy.astype(BF16)
        return carry

    lax.fori_loop(0, tiles, middle, 0)

    def feed(c, carry):
        exchange("ffa", c)
        cols = pl.ds(pl.multiple_of(c * CHUNK, CHUNK), CHUNK)
        up, down = whole(r.w1, cols), down_chunk(c)
        bias = jnp.concatenate([vec[pl.ds(B1 + 4 * c + n, 1), :] for n in range(4)], axis=1)
        spans = [slice(i * TILE, i * TILE + TILE) for i in range(tiles)]

        def products(rows):
            return dot(normed_two(rows)[...], up), dot(r.dy[rows, :], down, NT)

        ready = products(spans[0])
        bias_grad = jnp.zeros((1, CHUNK), F32)
        for i, rows in enumerate(spans):
            pre, grad_act = ready
            if i + 1 < tiles:
                ready = products(spans[i + 1])
            value, slope = gelu_both(pre + bias)
            value = value.astype(BF16)
            grad = (slope * grad_act).astype(BF16)
            bias_grad = bias_grad + column_sum(grad.astype(F32))
            act(rows)[...] = value
            grad_pre(rows)[...] = grad
            r.total_out[rows, :] += dot(value, down)
            r.grad_h[rows, :] += dot(grad, up, NT)
        for n in range(4):
            gvec[pl.ds(B1 + 4 * c + n, 1), :] = bias_grad[:, 128 * n : 128 * n + 128]
        exchange("ffb", c)
        grad_up = dot(normed_two(everything)[...], grad_pre(everything)[...], TN).astype(BF16)
        grad_down = dot(act(everything)[...], r.dy[...], TN).astype(BF16)
        if linked:
            r.w1[lead + (slice(None), cols)] = grad_up.reshape((2,) * bits + (16, CHUNK))
            r.w2[c // 2, c % 2] = grad_down.reshape((2,) * (bits - 2) + (64, D))
        else:
            r.w1[:, cols] = grad_up
            r.w2[rows_of(c, CHUNK), :] = grad_down
        return carry

    lax.fori_loop(0, chunks, feed, 0)

    exchange("ln2", 0)
    ri = lax.broadcasted_iota(jnp.int32, (128, 128), 0)
    ci = lax.broadcasted_iota(jnp.int32, (128, 128), 1)
    other_half = jnp.where((ri < 64) != (ci < 64), 1.0, 0.0).astype(BF16)
    spare = lax.broadcasted_iota(jnp.int32, (TILE, 128), 1) & 63
    proj = whole(r.wo, slice(None))
    grad_proj = jnp.zeros((D, D), F32)
    for i in range(tiles):
        rows = slice(i * TILE, i * TILE + TILE)
        r.out_low[rows, :] = r.total_out[rows, :].astype(BF16)
        grad, hat, scale = r.grad_h[rows, :], r.hat[rows, :], r.scale[rows, :1]
        add_vector(G2, column_sum(grad * hat))
        add_vector(S2, column_sum(grad))
        grad = r.dy[rows, :].astype(F32) + norm_back(grad, hat, scale, vector(G2, 4))
        r.grad_h[rows, :] = grad
        low = grad.astype(BF16)
        add_vector(BO, column_sum(low.astype(F32)))
        mixed = r.mixed[rows, :]
        grad_proj = grad_proj + dot(mixed, low, TN)
        grad_mixed = dot(low, proj, NT).astype(BF16)
        r.dy[rows, :] = grad_mixed
        product = grad_mixed.astype(F32) * mixed.astype(F32)
        high = product.astype(BF16)
        rest = (product - high.astype(F32)).astype(BF16)
        for p in range(PAIRS):
            cols = slice(128 * p, 128 * p + 128)
            row_dot = dot(high[:, cols], other_half) + dot(rest[:, cols], other_half)
            top = row_dot.astype(BF16).astype(F32)
            r.mixed[rows, cols] = jnp.where(
                spare == 0, -top, jnp.where(spare == 1, top - row_dot, 0.0)
            ).astype(BF16)
    grad_proj = grad_proj.astype(BF16)
    if linked:
        r.wo[...] = grad_proj.reshape((2,) * bits + (16, D))
    else:
        r.wo[...] = grad_proj
    store_out = pltpu.make_async_copy(r.out_low, r.output, r.local.at[2])
    store_out.start()

    def backward(t, carry):
        exchange("bwd", t)
        pair, clip = t // clips, t % clips
        attend_backward(r.qkv, r.dy, r.lse, r.mixed, r.big, r.grad_qt, clip * CLIP_LEN, pair)

        @pl.when(clip == clips - 1)
        def _():
            cols = pl.ds(pl.multiple_of(pair * 384, 128), 384)
            grad = r.big[:, cols]
            sums = column_sum(grad.astype(F32))
            for n in range(3):
                gvec[pl.ds(BQKV + 4 * n + pair, 1), :] = sums[:, 128 * n : 128 * n + 128]
            matrix = dot(r.a[...], grad, TN).astype(BF16)
            if linked:
                r.sq[lead + (slice(None), cols)] = matrix.reshape((2,) * bits + (16, 384))
            else:
                r.sq[:, cols] = matrix

        return carry

    lax.fori_loop(0, PAIRS * clips, backward, 0)

    def first_sums(i, carry):
        exchange("sums", i)
        rows = rows_of(i, TILE)
        grad = dot(r.big[rows, :], whole(r.wq, slice(None)), NT)
        hat, scale = norm(r.x[rows, :].astype(F32))
        add_vector(G1, column_sum(grad * hat))
        add_vector(S1, column_sum(grad))
        r.total_out[rows, :] = grad
        r.hat[rows, :] = hat
        r.scale[rows, :] = jnp.broadcast_to(scale, (TILE, 128))
        return carry

    lax.fori_loop(0, tiles, first_sums, 0)
    if linked:
        for n in range(dp * fs):
            row = n * per // 128
            r.gvec_parts[split_bits(n)] = jnp.concatenate(
                [gvec[row : row + 3, :], jnp.zeros((5, 128), F32)], axis=0
            )

    def first_back(i, carry):
        exchange("ln1", i)
        rows = rows_of(i, TILE)
        r.grad_h[rows, :] += norm_back(
            r.total_out[rows, :], r.hat[rows, :], r.scale[rows, :1], vector(G1, 4)
        )
        return carry

    lax.fori_loop(0, tiles, first_back, 0)
    store_grad = pltpu.make_async_copy(r.grad_h, r.input_grad, r.local.at[3])
    store_grad.start()
    exchange("end", 0)
    if not linked:
        stores = [
            pltpu.make_async_copy(src, dst, r.local.at[4 + n])
            for n, (src, dst) in enumerate(
                [(r.sq, r.qkv_grad), (r.wo, r.proj_grad), (r.w1, r.up_grad), (r.w2, r.down_grad)]
            )
        ]
        for store in stores:
            store.start()
        for store in stores:
            store.wait()
        r.total_vec[...] = gvec[...]
    store_out.wait()
    store_grad.wait()


def run_block(dp, fs, linked, tokens, cotangent, cond_frames, weights):
    n = tokens.shape[0]
    shape = jax.ShapeDtypeStruct
    vmem, smem, any_ = (
        pl.BlockSpec(memory_space=pltpu.VMEM),
        pl.BlockSpec(memory_space=pltpu.SMEM),
        pl.BlockSpec(memory_space=pl.ANY),
    )
    bits = BITS if linked else 0
    ins = ["tokens", "cotangent", "cond_frames"]
    in_specs = [any_, any_, smem]
    outs = {"output": ((n, D), BF16, any_), "input_grad": ((n, D), F32, any_)}
    outs["total_vec"] = ((8 if linked else VROWS, 128), F32, vmem)
    if linked:
        ins += ["qkv_weight", "proj_weight", "up_weight", "down_weight", "vectors"]
        in_specs += [vmem] * 5
        outs["total"] = ((768, 128), F32, vmem)
        matrix = lambda rows, cols: pltpu.VMEM((2,) * bits + (rows // 2**bits, cols), BF16)
    else:
        ins += ["qkv_mat", "proj_mat", "up_mat", "down_mat", "vec_in"]
        in_specs += [any_] * 4 + [vmem]
        outs["qkv_grad"] = ((D, 3 * D), BF16, any_)
        outs["proj_grad"] = ((D, D), BF16, any_)
        outs["up_grad"] = ((D, FF), BF16, any_)
        outs["down_grad"] = ((FF, D), BF16, any_)
        matrix = lambda rows, cols: pltpu.VMEM((rows, cols), BF16)
    scratch = {
        "x": pltpu.VMEM((n, D), BF16),
        "a": pltpu.VMEM((n, D), BF16),
        "dy": pltpu.VMEM((n, D), BF16),
        "qkv": pltpu.VMEM((n, 3 * D), BF16),
        "mixed": pltpu.VMEM((n, D), BF16),
        "lse": pltpu.VMEM((n, D), BF16),
        "hat": pltpu.VMEM((n, D), F32),
        "total_out": pltpu.VMEM((n, D), F32),
        "grad_h": pltpu.VMEM((n, D), F32),
        "scale": pltpu.VMEM((n, 128), F32),
        "big": pltpu.VMEM((n, 3 * D), BF16),
        "out_low": pltpu.VMEM((n, D), BF16),
        "grad_qt": pltpu.VMEM((128, CLIP_LEN), F32),
        "wq": matrix(D, 3 * D),
        "sq": matrix(D, 3 * D),
        "wo": matrix(D, D),
        "w1": matrix(D, FF),
        "w2": matrix(FF, D),
        "vec": pltpu.VMEM((VROWS, 128), F32),
        "gvec": pltpu.VMEM((VROWS, 128), F32),
        "local": pltpu.SemaphoreType.DMA((8,)),
    }
    names = ins + list(outs) + list(scratch)
    shapes = list(scratch.values())
    come_names = []
    if linked:
        streams = streams_of()
        for name in ("vec_parts", "gvec_parts"):
            names.append(name)
            shapes.append(pltpu.VMEM((2,) * bits + (8, 128), F32))
        names.append("down_part")
        shapes.append(pltpu.VMEM((2, 2, 64, D), BF16))
        for name in ("gather_send", "gather_recv", "sum_send", "sum_recv"):
            names.append(name)
            shapes.append(pltpu.SemaphoreType.DMA((len(streams), 7)))
        for name, (hops, left, rows, width, size) in streams.items():
            held = len(left) if name != "dz" else 2
            for k, hop in enumerate(hops[::-1]):
                held -= len(hop)
                come_names.append((name, f"{name}_{k}"))
                names.append(f"{name}_{k}")
                kind = BF16 if size == 2 else F32
                shapes.append(pltpu.VMEM((len(masks_of(hop)),) + (2,) * held + (rows, width), kind))

    def body(*refs):
        table = dict(zip(names, refs))
        if linked:
            table["come"] = {}
            for name, key in come_names:
                table["come"].setdefault(name, []).append(table.pop(key))
            keys = ("gather_send", "gather_recv", "sum_send", "sum_recv")
            table["sems"] = [table.pop(key) for key in keys]
        block_kernel(dp, fs, n, linked, list(table), *table.values())

    params = dict(vmem_limit_bytes=64 << 20)
    if linked:
        params.update(collective_id=0, has_side_effects=True)
    return pl.pallas_call(
        body,
        out_shape=[shape(s, t) for s, t, _ in outs.values()],
        in_specs=in_specs,
        out_specs=[spec for *_, spec in outs.values()],
        scratch_shapes=shapes,
        compiler_params=pltpu.CompilerParams(**params),
        name="block",
    )(tokens, cotangent, cond_frames, *weights)


def adamw(weight, grad, first, second, average, rate, decay):
    first_new = BETA_ONE * first + (1.0 - BETA_ONE) * grad
    second_new = BETA_TWO * second + (1.0 - BETA_TWO) * grad * grad
    first_hat = first_new / (1.0 - BETA_ONE**STEP)
    second_hat = second_new / (1.0 - BETA_TWO**STEP)
    weight_new = weight - rate * (first_hat / (jnp.sqrt(second_hat) + ADAM_EPS) + decay * weight)
    average_new = EMA_KEEP * average + (1.0 - EMA_KEEP) * weight_new
    return (first_new, second_new, weight_new, average_new)


def adam_kernel(dp, fs, linked, *refs):
    total, total_vec, output, input_grad = refs[:4]
    ins, outs, (output_new, input_grad_new) = refs[4:24], refs[24:44], refs[44:46]
    held, made, passing = refs[46:66], refs[66:86], refs[86:88]
    fetched, moved, loaded, stored = refs[88:]
    loads = [pltpu.make_async_copy(a, b, loaded.at[n]) for n, (a, b) in enumerate(zip(ins, held))]
    stores = [pltpu.make_async_copy(a, b, stored.at[n]) for n, (a, b) in enumerate(zip(made, outs))]
    fetches, moves = [], []
    for a, b, c in ((input_grad, passing[0], input_grad_new), (output, passing[1], output_new)):
        size = a.shape[0] // 4
        for n in range(4):
            rows, at = pl.ds(n * size, size), len(moves)
            fetches.append(pltpu.make_async_copy(a.at[rows, :], b.at[rows, :], fetched.at[at]))
            moves.append(pltpu.make_async_copy(b.at[rows, :], c.at[rows, :], moved.at[at]))
    for load in fetches + loads:
        load.start()
    for fetch, move in zip(fetches, moves):
        fetch.wait()
        move.start()

    def update(m, grad, rate, decay):
        for load in loads[4 * m : 4 * m + 4]:
            load.wait()
        weight, first, second, average = (ref[...] for ref in held[4 * m : 4 * m + 4])
        new = adamw(weight, grad, first, second, average, rate, decay)
        for ref, value in zip(made[4 * m : 4 * m + 4], new):
            ref[...] = value
        for store in stores[4 * m : 4 * m + 4]:
            store.start()

    base = 0
    for m in range(4):
        size = held[4 * m].shape[0]
        update(m, total[base : base + size, :], RATE_MATRIX, WEIGHT_DECAY)
        base += size
    per = VEC // (dp * fs)
    start = (lax.axis_index("dp") * fs + lax.axis_index("fsdp")) * per
    lane0 = start % 128
    lane = lax.broadcasted_iota(jnp.int32, (1, 128), 1)
    back = lax.rem(128 - lane0, 128)
    row = 0 if linked else start // 128
    parts = [pltpu.roll(total_vec[pl.ds(row + n, 1), :], back, 1) for n in range(3)]
    keep = 128 - lane0
    grad = jnp.concatenate(
        [jnp.where(lane < keep, parts[0], parts[1]), jnp.where(lane < keep, parts[1], parts[2])], axis=1
    )[:, :per]
    update(4, grad, RATE_VECTOR, 0.0)
    for copy in stores + moves:
        copy.wait()


def run_adam(dp, fs, linked, total, total_vec, output, input_grad, state):
    flat = [a.reshape(-1, 128) for a in state[:16]] + list(state[16:])
    vmem, any_ = pl.BlockSpec(memory_space=pltpu.VMEM), pl.BlockSpec(memory_space=pl.ANY)
    shapes = [jax.ShapeDtypeStruct(a.shape, F32) for a in flat]
    shapes += [jax.ShapeDtypeStruct(a.shape, a.dtype) for a in (output, input_grad)]
    new = pl.pallas_call(
        functools.partial(adam_kernel, dp, fs, linked),
        out_shape=shapes,
        in_specs=[vmem] * 2 + [any_] * 22,
        out_specs=[any_] * 22,
        scratch_shapes=[pltpu.VMEM(a.shape, F32) for a in flat] * 2
        + [pltpu.VMEM(a.shape, a.dtype) for a in (input_grad, output)]
        + [pltpu.SemaphoreType.DMA((n,)) for n in (8, 8, 20, 20)],
        compiler_params=pltpu.CompilerParams(vmem_limit_bytes=64 << 20),
        name="adam",
    )(total, total_vec, output, input_grad, *flat)
    return list(new[20:]) + [a.reshape(b.shape) for a, b in zip(new, state)]


def local(dp, fs, tokens, cotangent, cond_frames, *state):
    weights, firsts, seconds, averages = (state[5 * n : 5 * n + 5] for n in range(4))
    shards = dp * fs
    linked = shards == 2**BITS and not (dp & (dp - 1))
    if linked:
        shares = [w.reshape(-1, 128) for w in weights[:4]] + [weights[4]]
        output, input_grad, total_vec, total = run_block(
            dp, fs, True, tokens, cotangent, cond_frames, shares
        )
    else:
        gathered = [
            lax.all_gather(w.astype(BF16), AXES, axis=0, tiled=True) for w in weights
        ]
        qkv = gathered[0].reshape(D, 3, PAIRS, 128).swapaxes(1, 2).reshape(D, 3 * D)
        vec = jnp.pad(gathered[4].astype(F32).reshape(-1, 128), ((0, VROWS - VEC // 128), (0, 0)))
        mats = [qkv] + [g.reshape(-1, c) for g, c in zip(gathered[1:4], (D, FF, D))] + [vec]
        output, input_grad, total_vec, *grads = run_block(
            dp, fs, False, tokens, cotangent, cond_frames, mats
        )
        grads[0] = grads[0].reshape(D, PAIRS, 3, 128).swapaxes(1, 2).reshape(D, 3 * D)
        scatter = lambda g: lax.psum_scatter(
            g.astype(F32).reshape(shards, -1), AXES, scatter_dimension=0, tiled=True
        )
        total = jnp.concatenate([scatter(g).reshape(-1, 128) for g in grads], axis=0)
        total_vec = lax.psum(total_vec, AXES)
    order = [group[m] for m in range(5) for group in (weights, firsts, seconds, averages)]
    return tuple(run_adam(dp, fs, linked, total, total_vec, output, input_grad, order))


def solution(mesh):
    dp, fs = mesh.shape["dp"], mesh.shape["fsdp"]
    split = P(AXES, None)
    return jax.shard_map(
        functools.partial(local, dp, fs),
        mesh=mesh,
        in_specs=(split, split, P(AXES)) + (split,) * 20,
        out_specs=(split,) * 22,
        check_vma=False,
    )
```

```python
import functools
from types import SimpleNamespace

import jax
import jax.numpy as jnp
from jax import lax
from jax.experimental import pallas as pl
from jax.experimental.pallas import tpu as pltpu
from jax.sharding import PartitionSpec as P

D = 512
FF = 2048
HEADS = 8
HEAD_DIM = 64
FRAME_TOK = 64
STEP = 10
CLIP_LEN = 1024
VEC = 9 * D + FF

EPS = 1e-05
BETA_ONE = 0.9
BETA_TWO = 0.95
ADAM_EPS = 1e-08
RATE_MATRIX = 0.02
RATE_VECTOR = 0.2
WEIGHT_DECAY = 0.1
EMA_KEEP = 0.9
NEG = -1e30

AXES = ("dp", "fsdp")
MESH = pl.DeviceIdType.MESH
BF16 = jnp.bfloat16
F32 = jnp.float32
NN = (((1,), (0,)), ((), ()))
NT = (((1,), (1,)), ((), ()))
TN = (((0,), (0,)), ((), ()))
PAIRS = HEADS // 2
QB = 256
TILE = 512
CHUNK = 512
VROWS = 56
G1, S1, BQKV, BO, G2, S2, B1, B2 = 0, 4, 8, 20, 24, 28, 32, 48
GELU_A = 0.7978845608028654
GELU_B = 0.044715


def dot(left, right, dims=NN):
    return lax.dot_general(left, right, dims, preferred_element_type=F32)


BITS = 5
Z, Y, X, XY, CORE = (0, 1), (2,), (3,), (2, 3), (4,)
LINK = {0: "z", 1: "z", 2: "y", 3: "x", 4: "core"}


def masks_of(hop):
    return [(hop[0],)] if len(hop) == 1 else [(hop[1],), (hop[0],), hop]


def place(dp, fs):
    hi, lo = dp.bit_length() - 1, fs.bit_length() - 1
    i, f = lax.axis_index("dp"), lax.axis_index("fsdp")
    me = [(i // 2 ** (hi - 1 - t)) % 2 for t in range(hi)]
    me += [(f // 2 ** (lo - 1 - t)) % 2 for t in range(lo)]

    def partner(mask):
        at_i, at_f = i, f
        for t in mask:
            if t < hi:
                step = 2 ** (hi - 1 - t)
                at_i = at_i + step - 2 * step * me[t]
            else:
                step = 2 ** (hi + lo - 1 - t)
                at_f = at_f + step - 2 * step * me[t]
        return (at_i, at_f)

    return me, partner


def remote(src, dst, send, recv, device):
    return pltpu.make_async_remote_copy(
        src_ref=src, dst_ref=dst, send_sem=send, recv_sem=recv, device_id=device, device_id_type=MESH
    )


def split_bits(n):
    return tuple(n >> (BITS - 1 - t) & 1 for t in range(BITS))


class Transfer:
    def step(self, k):
        if k:
            for copy in self.hops[k - 1]:
                copy.wait_recv()
            self.arrived(k - 1)
        if k < len(self.hops):
            for copy in self.hops[k]:
                copy.start()
        else:
            for hop in self.hops:
                for copy in hop:
                    copy.wait_send()

    def arrived(self, k):
        pass


class Gather(Transfer):
    def __init__(self, me, partner, hops, left, buf, cols, send, recv):
        self.hops = []
        done, n = set(), 0
        for hop in hops:
            at = tuple(slice(None) if t in done else me[t] for t in left)
            ref = buf.at[at + (slice(None), cols)]
            copies = []
            for mask in masks_of(hop):
                copies.append(remote(ref, ref, send(n), recv(n), partner(mask)))
                n += 1
            self.hops.append(copies)
            done.update(hop)


class Scatter(Transfer):
    def __init__(self, me, partner, hops, left, stage, cols, come, send, recv, finish):
        self.hops, self.sums = [], []
        self.finish = finish
        left, n = list(left), 0
        source, source_cols = stage, cols
        for k, hop in enumerate(hops):

            def part(mask):
                at = [(1 - me[t] if t in mask else me[t]) if t in hop else slice(None) for t in left]
                return tuple(at) + (slice(None), source_cols)

            copies = []
            for slot, mask in enumerate(masks_of(hop)):
                copies.append(
                    remote(source.at[part(mask)], come[k].at[slot], send(n), recv(n), partner(mask))
                )
                n += 1
            self.hops.append(copies)
            self.sums.append((source, part(()), come[k], len(copies)))
            left = [t for t in left if t not in hop]
            source, source_cols = come[k].at[0], slice(None)

    def arrived(self, k):
        source, at, come, count = self.sums[k]
        if k + 1 < len(self.hops) and count == 1:
            come[0] = source[at] + come[0]
            return
        total = source[at].astype(F32)
        for slot in range(count):
            total = total + come[slot].astype(F32)
        if k + 1 < len(self.hops):
            come[0] = total.astype(come.dtype)
        else:
            self.finish(total)


def streams_of():
    first, second = (Z, Y, X, CORE), (Z, X, Y, CORE)
    every = (0, 1, 2, 3, 4)
    streams = {"vec": ((Z, XY, CORE), every, 8, 128, 4)}
    for p in range(PAIRS):
        hops = (Z, XY, CORE) if p in (0, PAIRS - 1) else (first, second)[p % 2]
        streams[f"q{p}"] = (hops, every, 16, 384, 2)
    streams["o"] = (first, every, 16, 512, 2)
    streams["u0"] = (second, every, 16, 512, 2)
    streams["dz"] = ((Z,), every, 64, 512, 2)
    streams["d0"] = (first[1:], every[2:], 64, 512, 2)
    for c in range(1, FF // CHUNK):
        streams[f"u{c}"] = ((second, first)[c % 2], every, 16, 512, 2)
        streams[f"d{c}"] = ((first, second)[c % 2][1:], every[2:], 64, 512, 2)
    return streams


def steps_of():
    steps = [("first", 0, 0.6, [], []), ("norm", 0, 1.5, [], []), ("affine", 0, 0.8, ["vec"], [])]
    steps += [("fwd", t, 2.1 + (t % 2 == 0), [f"q{t // 2}"], []) for t in range(2 * PAIRS)]
    steps += [("mid", 0, 3.1, ["o"], [])]
    for c in range(FF // CHUNK):
        steps += [("ffa", c, 4.4, ["dz", f"d{c}", f"u{c}"], []), ("ffb", c, 2.4, [], [f"u{c}", f"d{c}"])]
    steps += [("ln2", 0, 5.5, [], ["o"])]
    steps += [("bwd", t, 3.5 + (t % 2), [], [f"q{t // 2}"] if t % 2 else []) for t in range(2 * PAIRS)]
    steps += [("sums", t, 1.0, [], ["vec"] if t == 3 else []) for t in range(4)]
    steps += [("ln1", t, 0.6, [], []) for t in range(4)]
    steps += [("out", t, 1.1, [], []) for t in range(4)]
    steps += [("end", 0, 0.0, ["all"], [])]
    return steps


def plan_of():
    latency = {"z": 2.5, "y": 2.2, "x": 2.2, "core": 0.8}
    rate = {"z": 45e3, "y": 45e3, "x": 45e3, "core": 250e3}
    free = dict.fromkeys(rate, 0.0)
    streams = streams_of()
    rank = {("g", s): n for n, s in enumerate(streams)}
    rank.update({("s", s): 50 + n for n, s in enumerate(streams)})
    rank["s", f"q{PAIRS - 1}"], rank["s", "vec"] = 1, 0
    arrived = {}
    after = {("g", f"d{c}"): [("g", "dz")] for c in range(4)}
    after["s", "dz"] = [("s", f"d{c}") for c in range(4)]
    early = ("vec", "q0")
    pending = [("g", s, 0, 0.0 if s in early else 0.5) for s in streams if ("g", s) not in after]
    plan, model = {}, []
    now = 0.0

    def cost(kind, name, k):
        hops, bits, rows, cols, size = streams[name]
        hop = (hops if kind == "g" else hops[::-1])[k]
        done = [t for h in (hops[:k] if kind == "g" else hops[: len(hops) - 1 - k]) for t in h]
        held = rows * cols * size * 2 ** len(done)
        if hop == Z:
            return {"z": 4 * held / rate["z"]}
        if hop == XY:
            return {"x": 2 * held / rate["x"], "y": 2 * held / rate["y"]}
        return {LINK[hop[0]]: held / rate[LINK[hop[0]]]}

    def start_of(item):
        kind, name, k, ready = item
        if k == len(streams[name][0]):
            return ready
        return max([ready] + [free[link] for link in cost(kind, name, k)])

    def issue(item, at):
        kind, name, k, ready = item
        pending.remove(item)
        if k == len(streams[name][0]):
            arrived[kind, name] = max(at, ready)
            for other, needs in after.items():
                if (kind, name) in needs and all(n in arrived for n in needs):
                    pending.append((*other, 0, max(at, ready)))
            return
        begin, end = max(at, start_of(item)), 0.0
        for link, time in cost(kind, name, k).items():
            free[link] = begin + time
            end = max(end, begin + time + latency[link])
        pending.append((kind, name, k + 1, end))

    for name, index, time, needs, feeds in steps_of():
        taken = plan.setdefault((name, index), [])

        def missing():
            if "all" in needs:
                return bool(pending)
            return any(("g", n) not in arrived for n in needs)

        begun = now
        while True:
            ready = [
                i
                for i in pending
                if i[3] <= now and start_of(i) <= now + max(1.0, 0.5 * time)
            ]
            if ready:
                item = min(ready, key=lambda i: rank[i[:2]])
            elif missing():
                item = min(pending, key=lambda i: (max(start_of(i), i[3]), rank[i[:2]]))
                now = max(now, item[3], start_of(item))
            else:
                break
            taken.append(item[:3])
            issue(item, now)
        model.append((begun, now, name, index, taken))
        now += time
        for fed in feeds:
            pending.append(("s", fed, 0, now))
    return plan, model


def norm(values):
    mean = jnp.mean(values, axis=-1, keepdims=True)
    centred = values - mean
    scale = lax.rsqrt(jnp.mean(centred * centred, axis=-1, keepdims=True) + EPS)
    return centred * scale, scale


def norm_back(grad, hat, scale, gain):
    inner = grad * gain
    return scale * (
        inner
        - jnp.mean(inner, axis=-1, keepdims=True)
        - hat * jnp.mean(inner * hat, axis=-1, keepdims=True)
    )


def gelu_both(pre):
    square = pre * pre
    half = 0.5 + 0.5 * jnp.tanh(pre * (GELU_A + (GELU_A * GELU_B) * square))
    act = pre * half
    return act, half + (act - act * half) * (2 * GELU_A + (6 * GELU_A * GELU_B) * square)


def column_sum(values):
    return jnp.sum(values, axis=0, keepdims=True)


def attend_forward(qkv, mixed, lse, row0, pair):
    rows = lambda start, size: pl.ds(pl.multiple_of(row0 + start, QB), size)
    cols = lambda part: pl.ds(pl.multiple_of(pair * 384 + part * 128, 128), 128)
    out_cols = pl.ds(pl.multiple_of(pair * 128, 128), 128)
    low_all = lax.broadcasted_iota(jnp.int32, (CLIP_LEN, 128), 1) < 64
    lane = lax.broadcasted_iota(jnp.int32, (QB, 128), 1)
    low = lane < 64
    spare = lane & 63
    causal = lax.broadcasted_iota(jnp.int32, (QB, QB), 1) <= lax.broadcasted_iota(
        jnp.int32, (QB, QB), 0
    )
    one, zero = jnp.ones((), BF16), jnp.zeros((), BF16)
    queries = qkv[rows(0, CLIP_LEN), cols(0)] * jnp.asarray(HEAD_DIM**-0.5, BF16)
    keys = qkv[rows(0, CLIP_LEN), cols(1)]
    values = qkv[rows(0, CLIP_LEN), cols(2)]
    head_q = [jnp.where(low_all, queries, zero), jnp.where(low_all, zero, queries)]
    head_v = [jnp.where(low_all, values, one), jnp.where(low_all, one, values)]

    def scores(item):
        block, head = item
        n = QB * block
        s = dot(head_q[head][n : n + QB], keys[: n + QB], NT)
        diagonal = jnp.where(causal, s[:, n:], NEG)
        return jnp.concatenate([s[:, :n], diagonal], axis=1) if n else diagonal

    items = [(block, head) for block in reversed(range(CLIP_LEN // QB)) for head in range(2)]
    ahead = 3
    ready = {t: scores(items[t]) for t in range(ahead)}
    sums, tops = {}, {}
    for t, (block, head) in enumerate(items):
        s = ready.pop(t)
        top = jnp.max(s, axis=1, keepdims=True)
        if t + ahead < len(items):
            ready[t + ahead] = scores(items[t + ahead])
        weights = jnp.exp(s - top).astype(BF16)
        sums[head] = dot(weights, head_v[head][: QB * (block + 1)])
        tops[head] = top
        if head == 1:
            at = rows(QB * block, QB)
            top_sum = jnp.where(low, sums[0], sums[1])
            total = jnp.where(low, sums[1], sums[0])
            mixed[at, out_cols] = (top_sum / pltpu.roll(total, 64, 1)).astype(BF16)
            log_sum = jnp.where(low, tops[1], tops[0]) + jnp.log(total)
            high = log_sum.astype(BF16).astype(F32)
            lse[at, out_cols] = jnp.where(
                spare == 0, -high, jnp.where(spare == 1, high - log_sum, 0.0)
            ).astype(BF16)


def attend_backward(qkv, grad, lse, dots, grad_qkv, grad_qt, row0, pair):
    rows = lambda start, size: pl.ds(pl.multiple_of(row0 + start, QB), size)
    cols = lambda part: pl.ds(pl.multiple_of(pair * 384 + part * 128, 128), 128)
    one_cols = pl.ds(pl.multiple_of(pair * 128, 128), 128)
    low = lax.broadcasted_iota(jnp.int32, (CLIP_LEN, 128), 1) < 64
    causal = lax.broadcasted_iota(jnp.int32, (QB, QB), 0) <= lax.broadcasted_iota(
        jnp.int32, (QB, QB), 1
    )
    one, zero = jnp.ones((), BF16), jnp.zeros((), BF16)
    every = rows(0, CLIP_LEN)
    queries = qkv[every, cols(0)] * jnp.asarray(HEAD_DIM**-0.5, BF16)
    keys = qkv[every, cols(1)]
    values = qkv[every, cols(2)]
    out_grad = grad[every, one_cols]
    shift = lse[every, one_cols]
    row_dot = dots[every, one_cols]
    pick = lambda head, a, b: jnp.where(low, a, b) if head == 0 else jnp.where(low, b, a)
    q_shift = [pick(h, queries, shift) for h in range(2)]
    k_one = [pick(h, keys, one) for h in range(2)]
    v_one = [pick(h, values, one) for h in range(2)]
    g_shift = [pick(h, out_grad, row_dot) for h in range(2)]
    q_zero = [pick(h, queries, zero) for h in range(2)]
    g_zero = [pick(h, out_grad, zero) for h in range(2)]
    keys_t = keys.T
    items = [(block, head) for block in range(CLIP_LEN // QB) for head in range(2)]

    def products(item):
        block, head = item
        n = QB * block
        return (
            dot(k_one[head][n : n + QB], q_shift[head][n:], NT),
            dot(v_one[head][n : n + QB], g_shift[head][n:], NT),
        )

    ahead = 2
    ready = {t: products(items[t]) for t in range(ahead)}
    kept = {}
    for t, (block, head) in enumerate(items):
        n = QB * block
        s, grad_p = ready.pop(t)
        if t + ahead < len(items):
            ready[t + ahead] = products(items[t + ahead])
        probs = jnp.exp(s)
        diagonal = jnp.where(causal, probs[:, :QB], 0.0)
        probs = jnp.concatenate([diagonal, probs[:, QB:]], axis=1) if n + QB < CLIP_LEN else diagonal
        grad_s = (probs * grad_p).astype(BF16)
        kept[head] = (dot(grad_s, q_zero[head][n:]), dot(probs.astype(BF16), g_zero[head][n:]))
        half = slice(64 * head, 64 * head + 64)
        part = dot(keys_t[half, n : n + QB], grad_s)
        if block == 0:
            grad_qt[half, :] = part
        else:
            grad_qt[half, n:] = grad_qt[half, n:] + part
        if head == 1:
            at = rows(n, QB)
            grad_qkv[at, cols(1)] = (kept[0][0] + kept[1][0]).astype(BF16)
            grad_qkv[at, cols(2)] = (kept[0][1] + kept[1][1]).astype(BF16)
    grad_qkv[every, cols(0)] = (grad_qt[...].T * HEAD_DIM**-0.5).astype(BF16)


def block_kernel(dp, fs, tokens_n, linked, names, *refs):
    r = SimpleNamespace(**dict(zip(names, refs)))
    clips = tokens_n // CLIP_LEN
    tiles = tokens_n // TILE
    chunks = FF // CHUNK
    bits = BITS if linked else 0
    lead = (slice(None),) * bits
    base_of, stride_of = {}, {}

    load_x = pltpu.make_async_copy(r.tokens, r.x, r.local.at[0])
    load_cot = pltpu.make_async_copy(r.cotangent, r.dy, r.local.at[1])

    if linked:
        me, partner = place(dp, fs)
        barrier = pltpu.get_barrier_semaphore()
        friends = [mask for hop in (Z, XY, CORE) for mask in masks_of(hop)]
        for mask in friends:
            pl.semaphore_signal(barrier, inc=1, device_id=partner(mask), device_id_type=MESH)
        own = tuple(me)
        loads = {}
        for n, name in enumerate(("vectors", "qkv_weight", "proj_weight", "up_weight", "down_weight")):
            loads[name] = pltpu.make_async_copy(getattr(r, name), getattr(r, "my_" + name), r.local.at[3 + n])
            loads[name].start()
        load_x.start()
        load_cot.start()

        def share(flat, buf, rows, width, place_of):
            for j in range(width):
                part = flat[pl.ds(j, rows, stride=width), :].astype(BF16)
                buf[own + (slice(None), slice(128 * place_of(j), 128 * place_of(j) + 128))] = part

        per = VEC // (dp * fs)
        lane0 = (lax.axis_index("dp") * fs + lax.axis_index("fsdp")) * per % 128
        loads["vectors"].wait()
        part = r.my_vectors[...].astype(BF16).astype(F32)
        lane = lax.broadcasted_iota(jnp.int32, (1, 128), 1)
        first = pltpu.roll(part[:, :128], lane0, 1)
        tail = jnp.concatenate([part[:, 128:], jnp.zeros((1, 256 - per), F32)], axis=1)
        second = pltpu.roll(tail, lane0, 1)
        r.vec_parts[own] = jnp.concatenate(
            [
                jnp.where(lane >= lane0, first, 0.0),
                jnp.where(lane < lane0, first, second),
                jnp.where(lane < lane0, second, 0.0),
                jnp.zeros((5, 128), F32),
            ],
            axis=0,
        )
        loads["qkv_weight"].wait()
        share(r.my_qkv_weight, r.wq, 16, 12, lambda j: (j % PAIRS) * 3 + j // PAIRS)

        jobs = {}
        for n, (name, (hops, left, rows, width, _)) in enumerate(streams_of().items()):
            sems = [lambda k, ref=ref, n=n: ref.at[n, k] for ref in r.sems]
            kind, number = name[0], int(name[1:]) if name[1:].isdigit() else 0
            cols = slice(number * width, number * width + width)
            if name == "vec":
                matrix, stage, cols, base, stride = r.vec_parts, r.gvec_parts, slice(None), 0, 0
            elif kind == "q":
                matrix, stage, base, stride = r.wq, r.sq, 0, 12
            elif kind == "o":
                matrix, stage, base, stride = r.wo, r.wo, 192, 4
            elif kind == "u":
                matrix, stage, base, stride = r.w1, r.w1, 256, 16
            elif name == "dz":
                matrix, stage, cols, base, stride = r.w2, r.down_part, slice(None), 512, 4
            else:
                matrix, stage = r.w2.at[number // 2, number % 2], r.sd.at[number // 2, number % 2]
                cols = slice(None)

            def finish(total, name=name, kind=kind, number=number, rows=rows, width=width):
                if name == "vec":
                    r.total_vec[...] = total
                elif kind == "d" and name != "dz":
                    r.down_part[number // 2, number % 2] = total.astype(BF16)
                else:
                    for j in range(width // 128):
                        col = j * PAIRS + number if kind == "q" else number * (width // 128) + j
                        at = pl.ds(base_of[name] + col, rows, stride=stride_of[name])
                        r.total[at, :] = total[:, 128 * j : 128 * j + 128]

            if name == "vec" or name == "dz" or kind != "d":
                base_of[name], stride_of[name] = base, stride
            jobs["g", name] = Gather(me, partner, hops, left, matrix, cols, *sems[:2])
            sum_left = left if name != "dz" else Z
            jobs["s", name] = Scatter(
                me, partner, hops[::-1], sum_left, stage, cols, r.come[name], *sems[2:], finish
            )
        plan = plan_of()[0]
        pl.semaphore_wait(barrier, len(friends))
    else:
        load_x.start()
        load_cot.start()
        loads = [
            pltpu.make_async_copy(src, dst, r.local.at[3 + n])
            for n, (src, dst) in enumerate(
                [(r.qkv_mat, r.wq), (r.proj_mat, r.wo), (r.up_mat, r.w1), (r.down_mat, r.w2)]
            )
        ]
        for load in loads:
            load.start()
        r.vec[...] = r.vec_in[...]
        for load in loads:
            load.wait()

    def exchange(name, index):
        if not linked:
            return
        for (step, at), taken in plan.items():
            if step != name or not taken:
                continue

            def act(taken=taken):
                for kind, stream, k in taken:
                    jobs[kind, stream].step(k)

            if isinstance(index, int):
                if index == at:
                    act()
            else:
                pl.when(index == at)(act)

    vec, gvec = r.vec, r.gvec
    gvec[...] = jnp.zeros((VROWS, 128), F32)

    def vector(first, count):
        return jnp.concatenate([vec[first + n : first + n + 1, :] for n in range(count)], axis=1)

    def add_vector(first, values):
        for n in range(values.shape[1] // 128):
            gvec[first + n : first + n + 1, :] += values[:, 128 * n : 128 * n + 128]

    def whole(ref, cols):
        got = ref[lead + (slice(None), cols)]
        return got.reshape(-1, got.shape[-1])

    def down_chunk(c):
        if linked:
            return r.w2[c // 2, c % 2].reshape(CHUNK, D)
        return r.w2[pl.ds(pl.multiple_of(c * CHUNK, CHUNK), CHUNK), :]

    rows_of = lambda i, size: pl.ds(pl.multiple_of(i * size, size), size)
    act = lambda rows: r.big.at[rows, pl.ds(0, 512)]
    grad_pre = lambda rows: r.big.at[rows, pl.ds(512, 512)]
    normed_two = lambda rows: r.big.at[rows, pl.ds(1024, 512)]
    everything = pl.ds(0, tokens_n)

    exchange("first", 0)
    if linked:
        for name, buf, rows, width in (
            ("proj_weight", r.wo, 16, 4),
            ("up_weight", r.w1, 16, 16),
            ("down_weight", r.w2, 64, 4),
        ):
            loads[name].wait()
            share(getattr(r, "my_" + name), buf, rows, width, lambda j: j)
    exchange("norm", 0)
    load_x.wait()

    def norm_one(i, carry):
        rows = rows_of(i, 256)
        r.grad_h[rows, :] = norm(r.x[rows, :].astype(F32))[0]
        return carry

    lax.fori_loop(0, tokens_n // 256, norm_one, 0)
    exchange("affine", 0)
    if linked:
        vec[...] = jnp.zeros((VROWS, 128), F32)
        for n in range(dp * fs):
            row = n * per // 128
            vec[row : row + 3, :] += r.vec_parts[split_bits(n) + (slice(0, 3),)]

    def affine_one(i, carry):
        rows = rows_of(i, 256)
        r.a[rows, :] = (r.grad_h[rows, :] * vector(G1, 4) + vector(S1, 4)).astype(BF16)
        return carry

    lax.fori_loop(0, tokens_n // 256, affine_one, 0)

    def forward(t, carry):
        exchange("fwd", t)
        pair, clip = t // clips, t % clips

        @pl.when(clip == 0)
        def _():
            cols = pl.ds(pl.multiple_of(pair * 384, 128), 384)
            matrix = whole(r.wq, cols)
            bias = jnp.concatenate([vec[pl.ds(BQKV + 4 * n + pair, 1), :] for n in range(3)], axis=1)
            for i in range(tiles):
                rows = slice(i * TILE, i * TILE + TILE)
                r.qkv[rows, cols] = (dot(r.a[rows, :], matrix) + bias).astype(BF16)

        attend_forward(r.qkv, r.mixed, r.lse, clip * CLIP_LEN, pair)
        return carry

    lax.fori_loop(0, PAIRS * clips, forward, 0)

    exchange("mid", 0)
    load_cot.wait()

    def middle(i, carry):
        rows = rows_of(i, TILE)
        h = r.x[rows, :].astype(F32) + dot(r.mixed[rows, :], whole(r.wo, slice(None))) + vector(BO, 4)
        hat, scale = norm(h)
        r.hat[rows, :] = hat.astype(BF16)
        r.scale[rows, :] = jnp.broadcast_to(scale, (TILE, 128))
        normed_two(rows)[...] = (hat * vector(G2, 4) + vector(S2, 4)).astype(BF16)
        r.h_low[rows, :] = (h + vector(B2, 4)).astype(BF16)
        r.grad_h[rows, :] = jnp.zeros((TILE, D), F32)
        per = CLIP_LEN // TILE
        place_in = (i % per) * TILE + lax.broadcasted_iota(jnp.int32, (TILE, 1), 0)
        dy = jnp.where(place_in >= r.cond_frames[i // per] * FRAME_TOK, r.dy[rows, :].astype(F32), 0.0)
        add_vector(B2, column_sum(dy))
        r.dy[rows, :] = dy.astype(BF16)
        return carry

    lax.fori_loop(0, tiles, middle, 0)

    def park_of(c):
        cols = pl.ds(pl.multiple_of(c * CHUNK, CHUNK), CHUNK)
        return pltpu.make_async_copy(act(everything), r.parked.at[:, cols], r.local.at[2])

    def feed(c, carry):
        exchange("ffa", c)
        cols = pl.ds(pl.multiple_of(c * CHUNK, CHUNK), CHUNK)
        up, down = whole(r.w1, cols), down_chunk(c)
        bias = jnp.concatenate([vec[pl.ds(B1 + 4 * c + n, 1), :] for n in range(4)], axis=1)
        spans = [slice(i * TILE, i * TILE + TILE) for i in range(tiles)]

        def products(rows):
            return dot(normed_two(rows)[...], up), dot(r.dy[rows, :], down, NT)

        park = park_of(c)

        @pl.when(c > 0)
        def _():
            park.wait()

        ready, late = products(spans[0]), None
        bias_grad = jnp.zeros((1, CHUNK), F32)
        for i, rows in enumerate(spans):
            pre, grad_act = ready
            if i + 1 < tiles:
                ready = products(spans[i + 1])
            value, slope = gelu_both(pre + bias)
            value = value.astype(BF16)
            grad = slope * grad_act
            bias_grad = bias_grad + column_sum(grad)
            grad = grad.astype(BF16)
            act(rows)[...] = value
            grad_pre(rows)[...] = grad
            if late:
                r.grad_h[late[0], :] += dot(late[1], up, NT)
            late = (rows, grad)
        r.grad_h[late[0], :] += dot(late[1], up, NT)
        for n in range(4):
            gvec[pl.ds(B1 + 4 * c + n, 1), :] = bias_grad[:, 128 * n : 128 * n + 128]
        exchange("ffb", c)
        park.start()
        grad_up = dot(normed_two(everything)[...], grad_pre(everything)[...], TN).astype(BF16)
        grad_down = dot(act(everything)[...], r.dy[...], TN).astype(BF16)
        if linked:
            r.w1[lead + (slice(None), cols)] = grad_up.reshape((2,) * bits + (16, CHUNK))
            r.sd[c // 2, c % 2] = grad_down.reshape((2,) * (bits - 2) + (64, D))
        else:
            r.w1[:, cols] = grad_up
            r.sd[rows_of(c, CHUNK), :] = grad_down
        return carry

    lax.fori_loop(0, chunks, feed, 0)
    park_of(0).wait()

    exchange("ln2", 0)
    ri = lax.broadcasted_iota(jnp.int32, (128, 128), 0)
    ci = lax.broadcasted_iota(jnp.int32, (128, 128), 1)
    other_half = jnp.where((ri < 64) != (ci < 64), 1.0, 0.0).astype(BF16)
    other_half = jnp.concatenate([other_half, other_half], axis=0)
    spare = lax.broadcasted_iota(jnp.int32, (TILE, 128), 1) & 63
    proj = whole(r.wo, slice(None))

    def norm_part(rows):
        grad, hat, scale = r.grad_h[rows, :], r.hat[rows, :].astype(F32), r.scale[rows, :1]
        add_vector(G2, column_sum(grad * hat))
        add_vector(S2, column_sum(grad))
        grad = r.dy[rows, :].astype(F32) + norm_back(grad, hat, scale, vector(G2, 4))
        r.grad_h[rows, :] = grad
        low = grad.astype(BF16)
        add_vector(BO, column_sum(low.astype(F32)))
        return low

    def proj_part(rows, low):
        mixed = r.mixed[rows, :]
        part = dot(mixed, low, TN)
        grad_mixed = dot(low, proj, NT).astype(BF16)
        r.dy[rows, :] = grad_mixed
        product = grad_mixed.astype(F32) * mixed.astype(F32)
        high = product.astype(BF16)
        rest = (product - high.astype(F32)).astype(BF16)
        for p in range(PAIRS):
            cols = slice(128 * p, 128 * p + 128)
            row_dot = dot(jnp.concatenate([high[:, cols], rest[:, cols]], axis=1), other_half)
            top = row_dot.astype(BF16).astype(F32)
            r.mixed[rows, cols] = jnp.where(
                spare == 0, -top, jnp.where(spare == 1, top - row_dot, 0.0)
            ).astype(BF16)
        return part

    spans = [slice(i * TILE, i * TILE + TILE) for i in range(tiles)]
    grad_proj = jnp.zeros((D, D), F32)
    low = norm_part(spans[0])
    for i, rows in enumerate(spans):
        after = norm_part(spans[i + 1]) if i + 1 < tiles else None
        grad_proj = grad_proj + proj_part(rows, low)
        low = after
    grad_proj = grad_proj.astype(BF16)
    if linked:
        r.wo[...] = grad_proj.reshape((2,) * bits + (16, D))
    else:
        r.wo[...] = grad_proj

    def backward(t, carry):
        exchange("bwd", t)
        pair, clip = t // clips, t % clips
        attend_backward(r.qkv, r.dy, r.lse, r.mixed, r.big, r.grad_qt, clip * CLIP_LEN, pair)

        @pl.when(clip == clips - 1)
        def _():
            cols = pl.ds(pl.multiple_of(pair * 384, 128), 384)
            grad = r.big[:, cols]
            sums = column_sum(grad.astype(F32))
            for n in range(3):
                gvec[pl.ds(BQKV + 4 * n + pair, 1), :] = sums[:, 128 * n : 128 * n + 128]
            hat, scale = norm(r.x[rows_of(pair, tokens_n // PAIRS), :].astype(F32))
            r.hat[rows_of(pair, tokens_n // PAIRS), :] = hat.astype(BF16)
            r.scale[rows_of(pair, tokens_n // PAIRS), :] = jnp.broadcast_to(scale, (tokens_n // PAIRS, 128))
            matrix = dot(r.a[...], grad, TN).astype(BF16)
            if linked:
                r.sq[lead + (slice(None), cols)] = matrix.reshape((2,) * bits + (16, 384))
            else:
                r.sq[:, cols] = matrix

        return carry

    lax.fori_loop(0, PAIRS * clips, backward, 0)

    fetches = []
    for c in range(chunks):
        dst = r.qkv.at[:, c * CHUNK : c * CHUNK + CHUNK] if c < 3 else r.dy
        src = r.parked.at[:, c * CHUNK : c * CHUNK + CHUNK]
        fetches.append(pltpu.make_async_copy(src, dst, r.local.at[c]))
        fetches[-1].start()
    matrix = whole(r.wq, slice(None))
    spans = [slice(i * TILE, i * TILE + TILE) for i in range(tiles)]
    for i, rows in enumerate(spans):
        exchange("sums", i)
        grad = dot(r.big[rows, :], matrix, NT)
        add_vector(G1, column_sum(grad * r.hat[rows, :].astype(F32)))
        add_vector(S1, column_sum(grad))
        r.a[rows, :] = grad.astype(BF16)
    if linked:
        for n in range(dp * fs):
            row = n * per // 128
            r.gvec_parts[split_bits(n)] = jnp.concatenate(
                [gvec[row : row + 3, :], jnp.zeros((5, 128), F32)], axis=0
            )
    stores = []
    for i, rows in enumerate(spans):
        exchange("ln1", i)
        grad = norm_back(r.a[rows, :].astype(F32), r.hat[rows, :].astype(F32), r.scale[rows, :1], vector(G1, 4))
        r.lse[rows, :] = (r.grad_h[rows, :] + grad).astype(BF16)
        stores.append(pltpu.make_async_copy(r.lse.at[rows, :], r.input_grad.at[rows, :], r.local.at[4 + i]))
        stores[-1].start()

    for fetch in fetches:
        fetch.wait()
    down = whole(r.w2, slice(None))
    for i, rows in enumerate(spans):
        exchange("out", i)
        value = jnp.concatenate([r.qkv[rows, :], r.dy[rows, :]], axis=1)
        r.mixed[rows, :] = (r.h_low[rows, :].astype(F32) + dot(value, down)).astype(BF16)
        stores.append(pltpu.make_async_copy(r.mixed.at[rows, :], r.output.at[rows, :], r.local.at[8 + i]))
        stores[-1].start()
    exchange("end", 0)
    if not linked:
        for n, (src, dst) in enumerate(
            [(r.sq, r.qkv_grad), (r.wo, r.proj_grad), (r.w1, r.up_grad), (r.sd, r.down_grad)]
        ):
            stores.append(pltpu.make_async_copy(src, dst, r.local.at[n]))
            stores[-1].start()
        r.total_vec[...] = gvec[...]
    for store in stores:
        store.wait()


def run_block(dp, fs, linked, tokens, cotangent, cond_frames, weights):
    n = tokens.shape[0]
    shape = jax.ShapeDtypeStruct
    vmem, smem, any_ = (
        pl.BlockSpec(memory_space=pltpu.VMEM),
        pl.BlockSpec(memory_space=pltpu.SMEM),
        pl.BlockSpec(memory_space=pl.ANY),
    )
    bits = BITS if linked else 0
    ins = ["tokens", "cotangent", "cond_frames"]
    in_specs = [any_, any_, smem]
    outs = {"output": ((n, D), BF16, any_), "input_grad": ((n, D), BF16, any_)}
    outs["parked"] = ((n, FF), BF16, any_)
    outs["total_vec"] = ((8 if linked else VROWS, 128), F32, vmem)
    if linked:
        ins += ["qkv_weight", "proj_weight", "up_weight", "down_weight", "vectors"]
        in_specs += [any_] * 5
        outs["total"] = ((768, 128), F32, vmem)
        matrix = lambda rows, cols: pltpu.VMEM((2,) * bits + (rows // 2**bits, cols), BF16)
    else:
        ins += ["qkv_mat", "proj_mat", "up_mat", "down_mat", "vec_in"]
        in_specs += [any_] * 4 + [vmem]
        outs["qkv_grad"] = ((D, 3 * D), BF16, any_)
        outs["proj_grad"] = ((D, D), BF16, any_)
        outs["up_grad"] = ((D, FF), BF16, any_)
        outs["down_grad"] = ((FF, D), BF16, any_)
        matrix = lambda rows, cols: pltpu.VMEM((rows, cols), BF16)
    scratch = {
        "x": pltpu.VMEM((n, D), BF16),
        "a": pltpu.VMEM((n, D), BF16),
        "dy": pltpu.VMEM((n, D), BF16),
        "qkv": pltpu.VMEM((n, 3 * D), BF16),
        "mixed": pltpu.VMEM((n, D), BF16),
        "lse": pltpu.VMEM((n, D), BF16),
        "hat": pltpu.VMEM((n, D), BF16),
        "h_low": pltpu.VMEM((n, D), BF16),
        "grad_h": pltpu.VMEM((n, D), F32),
        "scale": pltpu.VMEM((n, 128), F32),
        "big": pltpu.VMEM((n, 3 * D), BF16),
        "grad_qt": pltpu.VMEM((128, CLIP_LEN), F32),
        "wq": matrix(D, 3 * D),
        "sq": matrix(D, 3 * D),
        "wo": matrix(D, D),
        "w1": matrix(D, FF),
        "w2": matrix(FF, D),
        "sd": matrix(FF, D),
        "vec": pltpu.VMEM((VROWS, 128), F32),
        "gvec": pltpu.VMEM((VROWS, 128), F32),
        "local": pltpu.SemaphoreType.DMA((12,)),
    }
    names = ins + list(outs) + list(scratch)
    shapes = list(scratch.values())
    come_names = []
    if linked:
        streams = streams_of()
        for name in ("vec_parts", "gvec_parts"):
            names.append(name)
            shapes.append(pltpu.VMEM((2,) * bits + (8, 128), F32))
        for name, held in zip(ins[3:], weights):
            names.append("my_" + name)
            shapes.append(pltpu.VMEM(held.shape, F32))
        names.append("down_part")
        shapes.append(pltpu.VMEM((2, 2, 64, D), BF16))
        for name in ("gather_send", "gather_recv", "sum_send", "sum_recv"):
            names.append(name)
            shapes.append(pltpu.SemaphoreType.DMA((len(streams), 7)))
        for name, (hops, left, rows, width, size) in streams.items():
            held = len(left) if name != "dz" else 2
            for k, hop in enumerate(hops[::-1]):
                held -= len(hop)
                come_names.append((name, f"{name}_{k}"))
                names.append(f"{name}_{k}")
                kind = BF16 if size == 2 else F32
                shapes.append(pltpu.VMEM((len(masks_of(hop)),) + (2,) * held + (rows, width), kind))

    def body(*refs):
        table = dict(zip(names, refs))
        if linked:
            table["come"] = {}
            for name, key in come_names:
                table["come"].setdefault(name, []).append(table.pop(key))
            keys = ("gather_send", "gather_recv", "sum_send", "sum_recv")
            table["sems"] = [table.pop(key) for key in keys]
        block_kernel(dp, fs, n, linked, list(table), *table.values())

    params = dict(vmem_limit_bytes=64 << 20)
    if linked:
        params.update(collective_id=0, has_side_effects=True)
    return pl.pallas_call(
        body,
        out_shape=[shape(s, t) for s, t, _ in outs.values()],
        in_specs=in_specs,
        out_specs=[spec for *_, spec in outs.values()],
        scratch_shapes=shapes,
        compiler_params=pltpu.CompilerParams(**params),
        name="block",
    )(tokens, cotangent, cond_frames, *weights)


def adamw(weight, grad, first, second, average, rate, decay):
    first_new = BETA_ONE * first + (1.0 - BETA_ONE) * grad
    second_new = BETA_TWO * second + (1.0 - BETA_TWO) * grad * grad
    first_hat = first_new / (1.0 - BETA_ONE**STEP)
    second_hat = second_new / (1.0 - BETA_TWO**STEP)
    weight_new = weight - rate * (first_hat / (jnp.sqrt(second_hat) + ADAM_EPS) + decay * weight)
    average_new = EMA_KEEP * average + (1.0 - EMA_KEEP) * weight_new
    return (first_new, second_new, weight_new, average_new)


def adam_kernel(dp, fs, linked, *refs):
    total, total_vec, output, input_grad = refs[:4]
    ins, outs, (output_new, input_grad_new) = refs[4:24], refs[24:44], refs[44:46]
    held, made = refs[46:66], refs[66:86]
    low_grad, full_grad, out_low, fetched, moved, loaded, stored = refs[86:]
    loads = [pltpu.make_async_copy(a, b, loaded.at[n]) for n, (a, b) in enumerate(zip(ins, held))]
    stores = [pltpu.make_async_copy(a, b, stored.at[n]) for n, (a, b) in enumerate(zip(made, outs))]
    fetches, moves = [], []
    for a, b, c, d in ((input_grad, low_grad, full_grad, input_grad_new), (output, out_low, out_low, output_new)):
        size = a.shape[0] // 4
        for n in range(4):
            rows, at = pl.ds(n * size, size), len(moves)
            fetches.append(pltpu.make_async_copy(a.at[rows, :], b.at[rows, :], fetched.at[at]))
            moves.append(pltpu.make_async_copy(c.at[rows, :], d.at[rows, :], moved.at[at]))
    for load in fetches + loads:
        load.start()
    for n, (fetch, move) in enumerate(zip(fetches, moves)):
        fetch.wait()
        if n < 4:
            rows = slice(n * size, n * size + size)
            full_grad[rows, :] = low_grad[rows, :].astype(F32)
        move.start()

    def update(m, grad, rate, decay):
        for load in loads[4 * m : 4 * m + 4]:
            load.wait()
        weight, first, second, average = (ref[...] for ref in held[4 * m : 4 * m + 4])
        new = adamw(weight, grad, first, second, average, rate, decay)
        for ref, value in zip(made[4 * m : 4 * m + 4], new):
            ref[...] = value
        for store in stores[4 * m : 4 * m + 4]:
            store.start()

    base = 0
    for m in range(4):
        size = held[4 * m].shape[0]
        update(m, total[base : base + size, :], RATE_MATRIX, WEIGHT_DECAY)
        base += size
    per = VEC // (dp * fs)
    start = (lax.axis_index("dp") * fs + lax.axis_index("fsdp")) * per
    lane0 = start % 128
    lane = lax.broadcasted_iota(jnp.int32, (1, 128), 1)
    back = lax.rem(128 - lane0, 128)
    row = 0 if linked else start // 128
    parts = [pltpu.roll(total_vec[pl.ds(row + n, 1), :], back, 1) for n in range(3)]
    keep = 128 - lane0
    grad = jnp.concatenate(
        [jnp.where(lane < keep, parts[0], parts[1]), jnp.where(lane < keep, parts[1], parts[2])], axis=1
    )[:, :per]
    update(4, grad, RATE_VECTOR, 0.0)
    for copy in stores + moves:
        copy.wait()


def run_adam(dp, fs, linked, total, total_vec, output, input_grad, state):
    flat = [a.reshape(-1, 128) for a in state[:16]] + list(state[16:])
    vmem, any_ = pl.BlockSpec(memory_space=pltpu.VMEM), pl.BlockSpec(memory_space=pl.ANY)
    shapes = [jax.ShapeDtypeStruct(a.shape, F32) for a in flat]
    shapes += [jax.ShapeDtypeStruct(output.shape, BF16), jax.ShapeDtypeStruct(output.shape, F32)]
    new = pl.pallas_call(
        functools.partial(adam_kernel, dp, fs, linked),
        out_shape=shapes,
        in_specs=[vmem] * 2 + [any_] * 22,
        out_specs=[any_] * 22,
        scratch_shapes=[pltpu.VMEM(a.shape, F32) for a in flat] * 2
        + [pltpu.VMEM(output.shape, t) for t in (BF16, F32, BF16)]
        + [pltpu.SemaphoreType.DMA((n,)) for n in (8, 8, 20, 20)],
        compiler_params=pltpu.CompilerParams(vmem_limit_bytes=64 << 20),
        name="adam",
    )(total, total_vec, output, input_grad, *flat)
    return list(new[20:]) + [a.reshape(b.shape) for a, b in zip(new, state)]


def local(dp, fs, tokens, cotangent, cond_frames, *state):
    weights, firsts, seconds, averages = (state[5 * n : 5 * n + 5] for n in range(4))
    shards = dp * fs
    linked = shards == 2**BITS and not (dp & (dp - 1))
    if linked:
        shares = [w.reshape(-1, 128) for w in weights[:4]] + [weights[4]]
        output, input_grad, _, total_vec, total = run_block(
            dp, fs, True, tokens, cotangent, cond_frames, shares
        )
    else:
        gathered = [
            lax.all_gather(w.astype(BF16), AXES, axis=0, tiled=True) for w in weights
        ]
        qkv = gathered[0].reshape(D, 3, PAIRS, 128).swapaxes(1, 2).reshape(D, 3 * D)
        vec = jnp.pad(gathered[4].astype(F32).reshape(-1, 128), ((0, VROWS - VEC // 128), (0, 0)))
        mats = [qkv] + [g.reshape(-1, c) for g, c in zip(gathered[1:4], (D, FF, D))] + [vec]
        output, input_grad, _, total_vec, *grads = run_block(
            dp, fs, False, tokens, cotangent, cond_frames, mats
        )
        grads[0] = grads[0].reshape(D, PAIRS, 3, 128).swapaxes(1, 2).reshape(D, 3 * D)
        scatter = lambda g: lax.psum_scatter(
            g.astype(F32).reshape(shards, -1), AXES, scatter_dimension=0, tiled=True
        )
        total = jnp.concatenate([scatter(g).reshape(-1, 128) for g in grads], axis=0)
        total_vec = lax.psum(total_vec, AXES)
    order = [group[m] for m in range(5) for group in (weights, firsts, seconds, averages)]
    return tuple(run_adam(dp, fs, linked, total, total_vec, output, input_grad, order))


def solution(mesh):
    dp, fs = mesh.shape["dp"], mesh.shape["fsdp"]
    split = P(AXES, None)
    return jax.shard_map(
        functools.partial(local, dp, fs),
        mesh=mesh,
        in_specs=(split, split, P(AXES)) + (split,) * 20,
        out_specs=(split,) * 22,
        check_vma=False,
    )
```

```python
import functools
from types import SimpleNamespace

import jax
import jax.numpy as jnp
from jax import lax
from jax.experimental import pallas as pl
from jax.experimental.pallas import tpu as pltpu
from jax.sharding import PartitionSpec as P

D = 512
FF = 2048
HEADS = 8
HEAD_DIM = 64
FRAME_TOK = 64
STEP = 10
CLIP_LEN = 1024
VEC = 9 * D + FF

EPS = 1e-05
BETA_ONE = 0.9
BETA_TWO = 0.95
ADAM_EPS = 1e-08
RATE_MATRIX = 0.02
RATE_VECTOR = 0.2
WEIGHT_DECAY = 0.1
EMA_KEEP = 0.9
NEG = -1e30

AXES = ("dp", "fsdp")
MESH = pl.DeviceIdType.MESH
BF16 = jnp.bfloat16
F32 = jnp.float32
NN = (((1,), (0,)), ((), ()))
NT = (((1,), (1,)), ((), ()))
TN = (((0,), (0,)), ((), ()))
PAIRS = HEADS // 2
QB = 256
TILE = 512
CHUNK = 512
VROWS = 56
G1, S1, BQKV, BO, G2, S2, B1, B2 = 0, 4, 8, 20, 24, 28, 32, 48
GELU_A = 0.7978845608028654
GELU_B = 0.044715


def dot(left, right, dims=NN):
    return lax.dot_general(left, right, dims, preferred_element_type=F32)


BITS = 5
Z, Y, X, XY, CORE = (0, 1), (2,), (3,), (2, 3), (4,)
LINK = {0: "z", 1: "z", 2: "y", 3: "x", 4: "core"}


def masks_of(hop):
    return [(hop[0],)] if len(hop) == 1 else [(hop[1],), (hop[0],), hop]


def place(dp, fs):
    hi, lo = dp.bit_length() - 1, fs.bit_length() - 1
    i, f = lax.axis_index("dp"), lax.axis_index("fsdp")
    me = [(i // 2 ** (hi - 1 - t)) % 2 for t in range(hi)]
    me += [(f // 2 ** (lo - 1 - t)) % 2 for t in range(lo)]

    def partner(mask):
        at_i, at_f = i, f
        for t in mask:
            if t < hi:
                step = 2 ** (hi - 1 - t)
                at_i = at_i + step - 2 * step * me[t]
            else:
                step = 2 ** (hi + lo - 1 - t)
                at_f = at_f + step - 2 * step * me[t]
        return (at_i, at_f)

    return me, partner


def remote(src, dst, send, recv, device):
    return pltpu.make_async_remote_copy(
        src_ref=src, dst_ref=dst, send_sem=send, recv_sem=recv, device_id=device, device_id_type=MESH
    )


def split_bits(n):
    return tuple(n >> (BITS - 1 - t) & 1 for t in range(BITS))


class Transfer:
    def step(self, k):
        if k:
            for copy in self.hops[k - 1]:
                copy.wait_recv()
            self.arrived(k - 1)
        if k < len(self.hops):
            for copy in self.hops[k]:
                copy.start()
        else:
            for hop in self.hops:
                for copy in hop:
                    copy.wait_send()

    def arrived(self, k):
        pass


class Gather(Transfer):
    def __init__(self, me, partner, hops, left, buf, cols, send, recv):
        self.hops = []
        done, n = set(), 0
        for hop in hops:
            at = tuple(slice(None) if t in done else me[t] for t in left)
            ref = buf.at[at + (slice(None), cols)]
            copies = []
            for mask in masks_of(hop):
                copies.append(remote(ref, ref, send(n), recv(n), partner(mask)))
                n += 1
            self.hops.append(copies)
            done.update(hop)


class Scatter(Transfer):
    def __init__(self, me, partner, hops, left, stage, cols, come, send, recv, finish):
        self.hops, self.sums = [], []
        self.finish = finish
        left, n = list(left), 0
        source, source_cols = stage, cols
        for k, hop in enumerate(hops):

            def part(mask):
                at = [(1 - me[t] if t in mask else me[t]) if t in hop else slice(None) for t in left]
                return tuple(at) + (slice(None), source_cols)

            copies = []
            for slot, mask in enumerate(masks_of(hop)):
                copies.append(
                    remote(source.at[part(mask)], come[k].at[slot], send(n), recv(n), partner(mask))
                )
                n += 1
            self.hops.append(copies)
            self.sums.append((source, part(()), come[k], len(copies)))
            left = [t for t in left if t not in hop]
            source, source_cols = come[k].at[0], slice(None)

    def arrived(self, k):
        source, at, come, count = self.sums[k]
        if k + 1 < len(self.hops) and count == 1:
            come[0] = source[at] + come[0]
            return
        total = source[at].astype(F32)
        for slot in range(count):
            total = total + come[slot].astype(F32)
        if k + 1 < len(self.hops):
            come[0] = total.astype(come.dtype)
        else:
            self.finish(total)


def streams_of():
    first, second = (Z, Y, X, CORE), (Z, X, Y, CORE)
    every = (0, 1, 2, 3, 4)
    streams = {"vec": ((Z, XY, CORE), every, 8, 128, 4)}
    for p in range(PAIRS):
        hops = (Z, XY, CORE) if p in (0, 1, PAIRS - 1) else (first, second)[p % 2]
        streams[f"q{p}"] = (hops, every, 16, 384, 2)
    streams["o"] = (first, every, 16, 512, 2)
    streams["u0"] = (second, every, 16, 512, 2)
    streams["dz"] = ((Z,), every, 64, 512, 2)
    streams["d0"] = (first[1:], every[2:], 64, 512, 2)
    for c in range(1, FF // CHUNK):
        streams[f"u{c}"] = ((second, first)[c % 2], every, 16, 512, 2)
        streams[f"d{c}"] = ((first, second)[c % 2][1:], every[2:], 64, 512, 2)
    return streams


def steps_of():
    steps = [("first", 0, 0.6, [], []), ("norm", 0, 1.5, [], []), ("affine", 0, 0.8, ["vec"], [])]
    steps += [("fwd", t, 2.1 + (t % 2 == 0), [f"q{t // 2}"], []) for t in range(2 * PAIRS)]
    steps += [("mid", 0, 3.1, ["o"], [])]
    for c in range(FF // CHUNK):
        steps += [("ffa", c, 4.4, ["dz", f"d{c}", f"u{c}"], []), ("ffb", c, 2.4, [], [f"u{c}", f"d{c}"])]
    steps += [("ln2", 0, 5.5, [], ["o"])]
    steps += [("bwd", t, 3.5 + (t % 2), [], [f"q{t // 2}"] if t % 2 else []) for t in range(2 * PAIRS)]
    steps += [("sums", t, 1.2, [], ["vec"] if t == 3 else []) for t in range(4)]
    steps += [("ln1", t, 0.6, [], []) for t in range(4)]
    steps += [("out", t, 1.1, [], []) for t in range(4)]
    steps += [("end", 0, 0.0, ["all"], [])]
    return steps


def plan_of():
    latency = {"z": 2.5, "y": 2.2, "x": 2.2, "core": 0.8}
    rate = {"z": 45e3, "y": 45e3, "x": 45e3, "core": 250e3}
    free = dict.fromkeys(rate, 0.0)
    streams = streams_of()
    rank = {("g", s): n for n, s in enumerate(streams)}
    rank.update({("s", s): 50 + n for n, s in enumerate(streams)})
    rank["s", f"q{PAIRS - 1}"], rank["s", "vec"] = 1, 0
    arrived = {}
    after = {("g", f"d{c}"): [("g", "dz")] for c in range(4)}
    after["s", "dz"] = [("s", f"d{c}") for c in range(4)]
    early = ("vec", "q0")
    pending = [("g", s, 0, 0.0 if s in early else 0.5) for s in streams if ("g", s) not in after]
    plan, model = {}, []
    now = 0.0

    def cost(kind, name, k):
        hops, bits, rows, cols, size = streams[name]
        hop = (hops if kind == "g" else hops[::-1])[k]
        done = [t for h in (hops[:k] if kind == "g" else hops[: len(hops) - 1 - k]) for t in h]
        held = rows * cols * size * 2 ** len(done)
        if hop == Z:
            return {"z": 4 * held / rate["z"]}
        if hop == XY:
            return {"x": 2 * held / rate["x"], "y": 2 * held / rate["y"]}
        return {LINK[hop[0]]: held / rate[LINK[hop[0]]]}

    def start_of(item):
        kind, name, k, ready = item
        if k == len(streams[name][0]):
            return ready
        return max([ready] + [free[link] for link in cost(kind, name, k)])

    def issue(item, at):
        kind, name, k, ready = item
        pending.remove(item)
        if k == len(streams[name][0]):
            arrived[kind, name] = max(at, ready)
            for other, needs in after.items():
                if (kind, name) in needs and all(n in arrived for n in needs):
                    pending.append((*other, 0, max(at, ready)))
            return
        begin, end = max(at, start_of(item)), 0.0
        for link, time in cost(kind, name, k).items():
            free[link] = begin + time
            end = max(end, begin + time + latency[link])
        pending.append((kind, name, k + 1, end))

    for name, index, time, needs, feeds in steps_of():
        taken = plan.setdefault((name, index), [])

        def missing():
            if "all" in needs:
                return bool(pending)
            return any(("g", n) not in arrived for n in needs)

        begun = now
        while True:
            ready = [
                i
                for i in pending
                if i[3] <= now and start_of(i) <= now + max(1.0, 0.5 * time)
            ]
            if ready:
                item = min(ready, key=lambda i: rank[i[:2]])
            elif missing():
                item = min(pending, key=lambda i: (max(start_of(i), i[3]), rank[i[:2]]))
                now = max(now, item[3], start_of(item))
            else:
                break
            taken.append(item[:3])
            issue(item, now)
        model.append((begun, now, name, index, taken))
        now += time
        for fed in feeds:
            pending.append(("s", fed, 0, now))
    return plan, model


def norm(values):
    mean = jnp.mean(values, axis=-1, keepdims=True)
    centred = values - mean
    scale = lax.rsqrt(jnp.mean(centred * centred, axis=-1, keepdims=True) + EPS)
    return centred * scale, scale


def norm_back(grad, hat, scale, gain):
    inner = grad * gain
    return scale * (
        inner
        - jnp.mean(inner, axis=-1, keepdims=True)
        - hat * jnp.mean(inner * hat, axis=-1, keepdims=True)
    )


def gelu_both(pre):
    square = pre * pre
    half = 0.5 + 0.5 * jnp.tanh(pre * (GELU_A + (GELU_A * GELU_B) * square))
    act = pre * half
    return act, half + (act - act * half) * (2 * GELU_A + (6 * GELU_A * GELU_B) * square)


def column_sum(values):
    return jnp.sum(values, axis=0, keepdims=True)


def attend_forward(qkv, mixed, lse, row0, pair):
    rows = lambda start, size: pl.ds(pl.multiple_of(row0 + start, QB), size)
    cols = lambda part: pl.ds(pl.multiple_of(pair * 384 + part * 128, 128), 128)
    out_cols = pl.ds(pl.multiple_of(pair * 128, 128), 128)
    low_all = lax.broadcasted_iota(jnp.int32, (CLIP_LEN, 128), 1) < 64
    lane = lax.broadcasted_iota(jnp.int32, (QB, 128), 1)
    low = lane < 64
    spare = lane & 63
    causal = lax.broadcasted_iota(jnp.int32, (QB, QB), 1) <= lax.broadcasted_iota(
        jnp.int32, (QB, QB), 0
    )
    one, zero = jnp.ones((), BF16), jnp.zeros((), BF16)
    queries = qkv[rows(0, CLIP_LEN), cols(0)] * jnp.asarray(HEAD_DIM**-0.5, BF16)
    keys = qkv[rows(0, CLIP_LEN), cols(1)]
    values = qkv[rows(0, CLIP_LEN), cols(2)]
    head_q = [jnp.where(low_all, queries, zero), jnp.where(low_all, zero, queries)]
    head_v = [jnp.where(low_all, values, one), jnp.where(low_all, one, values)]

    def scores(item):
        block, head = item
        n = QB * block
        s = dot(head_q[head][n : n + QB], keys[: n + QB], NT)
        diagonal = jnp.where(causal, s[:, n:], NEG)
        return jnp.concatenate([s[:, :n], diagonal], axis=1) if n else diagonal

    items = [(block, head) for block in reversed(range(CLIP_LEN // QB)) for head in range(2)]
    ahead = 3
    ready = {t: scores(items[t]) for t in range(ahead)}
    sums, tops = {}, {}
    for t, (block, head) in enumerate(items):
        s = ready.pop(t)
        top = jnp.max(s, axis=1, keepdims=True)
        if t + ahead < len(items):
            ready[t + ahead] = scores(items[t + ahead])
        weights = jnp.exp(s - top).astype(BF16)
        sums[head] = dot(weights, head_v[head][: QB * (block + 1)])
        tops[head] = top
        if head == 1:
            at = rows(QB * block, QB)
            top_sum = jnp.where(low, sums[0], sums[1])
            total = jnp.where(low, sums[1], sums[0])
            mixed[at, out_cols] = (top_sum / pltpu.roll(total, 64, 1)).astype(BF16)
            log_sum = jnp.where(low, tops[1], tops[0]) + jnp.log(total)
            high = log_sum.astype(BF16).astype(F32)
            lse[at, out_cols] = jnp.where(
                spare == 0, -high, jnp.where(spare == 1, high - log_sum, 0.0)
            ).astype(BF16)


def attend_backward(qkv, grad, lse, dots, grad_qkv, grad_qt, row0, pair):
    rows = lambda start, size: pl.ds(pl.multiple_of(row0 + start, QB), size)
    cols = lambda part: pl.ds(pl.multiple_of(pair * 384 + part * 128, 128), 128)
    one_cols = pl.ds(pl.multiple_of(pair * 128, 128), 128)
    low = lax.broadcasted_iota(jnp.int32, (CLIP_LEN, 128), 1) < 64
    causal = lax.broadcasted_iota(jnp.int32, (QB, QB), 0) <= lax.broadcasted_iota(
        jnp.int32, (QB, QB), 1
    )
    one, zero = jnp.ones((), BF16), jnp.zeros((), BF16)
    every = rows(0, CLIP_LEN)
    queries = qkv[every, cols(0)] * jnp.asarray(HEAD_DIM**-0.5, BF16)
    keys = qkv[every, cols(1)]
    values = qkv[every, cols(2)]
    out_grad = grad[every, one_cols]
    shift = lse[every, one_cols]
    row_dot = dots[every, one_cols]
    pick = lambda head, a, b: jnp.where(low, a, b) if head == 0 else jnp.where(low, b, a)
    q_shift = [pick(h, queries, shift) for h in range(2)]
    k_one = [pick(h, keys, one) for h in range(2)]
    v_one = [pick(h, values, one) for h in range(2)]
    g_shift = [pick(h, out_grad, row_dot) for h in range(2)]
    q_zero = [pick(h, queries, zero) for h in range(2)]
    g_zero = [pick(h, out_grad, zero) for h in range(2)]
    keys_t = keys.T
    items = [(block, head) for block in range(CLIP_LEN // QB) for head in range(2)]

    def products(item):
        block, head = item
        n = QB * block
        return (
            dot(k_one[head][n : n + QB], q_shift[head][n:], NT),
            dot(v_one[head][n : n + QB], g_shift[head][n:], NT),
        )

    ahead = 2
    ready = {t: products(items[t]) for t in range(ahead)}
    kept = {}
    for t, (block, head) in enumerate(items):
        n = QB * block
        s, grad_p = ready.pop(t)
        if t + ahead < len(items):
            ready[t + ahead] = products(items[t + ahead])
        probs = jnp.exp(s)
        diagonal = jnp.where(causal, probs[:, :QB], 0.0)
        probs = jnp.concatenate([diagonal, probs[:, QB:]], axis=1) if n + QB < CLIP_LEN else diagonal
        grad_s = (probs * grad_p).astype(BF16)
        kept[head] = (dot(grad_s, q_zero[head][n:]), dot(probs.astype(BF16), g_zero[head][n:]))
        half = slice(64 * head, 64 * head + 64)
        part = dot(keys_t[half, n : n + QB], grad_s)
        if block == 0:
            grad_qt[half, :] = part
        else:
            grad_qt[half, n:] = grad_qt[half, n:] + part
        if head == 1:
            at = rows(n, QB)
            grad_qkv[at, cols(1)] = (kept[0][0] + kept[1][0]).astype(BF16)
            grad_qkv[at, cols(2)] = (kept[0][1] + kept[1][1]).astype(BF16)
    grad_qkv[every, cols(0)] = (grad_qt[...].T * HEAD_DIM**-0.5).astype(BF16)


def block_kernel(dp, fs, tokens_n, linked, names, *refs):
    r = SimpleNamespace(**dict(zip(names, refs)))
    clips = tokens_n // CLIP_LEN
    tiles = tokens_n // TILE
    chunks = FF // CHUNK
    bits = BITS if linked else 0
    lead = (slice(None),) * bits
    base_of, stride_of = {}, {}

    load_x = pltpu.make_async_copy(r.tokens, r.x, r.local.at[0])
    load_cot = pltpu.make_async_copy(r.cotangent, r.dy, r.local.at[1])

    if linked:
        me, partner = place(dp, fs)
        barrier = pltpu.get_barrier_semaphore()
        friends = [mask for hop in (Z, XY, CORE) for mask in masks_of(hop)]
        for mask in friends:
            pl.semaphore_signal(barrier, inc=1, device_id=partner(mask), device_id_type=MESH)
        own = tuple(me)
        loads = {}
        for n, name in enumerate(("vectors", "qkv_weight", "proj_weight", "up_weight", "down_weight")):
            loads[name] = pltpu.make_async_copy(getattr(r, name), getattr(r, "my_" + name), r.local.at[3 + n])
            loads[name].start()
        load_x.start()
        load_cot.start()

        def share(flat, buf, rows, width, place_of):
            for j in range(width):
                part = flat[pl.ds(j, rows, stride=width), :].astype(BF16)
                buf[own + (slice(None), slice(128 * place_of(j), 128 * place_of(j) + 128))] = part

        per = VEC // (dp * fs)
        lane0 = (lax.axis_index("dp") * fs + lax.axis_index("fsdp")) * per % 128
        loads["vectors"].wait()
        part = r.my_vectors[...].astype(BF16).astype(F32)
        lane = lax.broadcasted_iota(jnp.int32, (1, 128), 1)
        first = pltpu.roll(part[:, :128], lane0, 1)
        tail = jnp.concatenate([part[:, 128:], jnp.zeros((1, 256 - per), F32)], axis=1)
        second = pltpu.roll(tail, lane0, 1)
        r.vec_parts[own] = jnp.concatenate(
            [
                jnp.where(lane >= lane0, first, 0.0),
                jnp.where(lane < lane0, first, second),
                jnp.where(lane < lane0, second, 0.0),
                jnp.zeros((5, 128), F32),
            ],
            axis=0,
        )
        loads["qkv_weight"].wait()
        share(r.my_qkv_weight, r.wq, 16, 12, lambda j: (j % PAIRS) * 3 + j // PAIRS)

        jobs = {}
        for n, (name, (hops, left, rows, width, _)) in enumerate(streams_of().items()):
            sems = [lambda k, ref=ref, n=n: ref.at[n, k] for ref in r.sems]
            kind, number = name[0], int(name[1:]) if name[1:].isdigit() else 0
            cols = slice(number * width, number * width + width)
            if name == "vec":
                matrix, stage, cols, base, stride = r.vec_parts, r.gvec_parts, slice(None), 0, 0
            elif kind == "q":
                matrix, stage, base, stride = r.wq, r.sq, 0, 12
            elif kind == "o":
                matrix, stage, base, stride = r.wo, r.wo, 192, 4
            elif kind == "u":
                matrix, stage, base, stride = r.w1, r.w1, 256, 16
            elif name == "dz":
                matrix, stage, cols, base, stride = r.w2, r.down_part, slice(None), 512, 4
            else:
                matrix, stage = r.w2.at[number // 2, number % 2], r.sd.at[number // 2, number % 2]
                cols = slice(None)

            def finish(total, name=name, kind=kind, number=number, rows=rows, width=width):
                if name == "vec":
                    r.total_vec[...] = total
                elif kind == "d" and name != "dz":
                    r.down_part[number // 2, number % 2] = total.astype(BF16)
                else:
                    for j in range(width // 128):
                        col = j * PAIRS + number if kind == "q" else number * (width // 128) + j
                        at = pl.ds(base_of[name] + col, rows, stride=stride_of[name])
                        r.total[at, :] = total[:, 128 * j : 128 * j + 128]

            if name == "vec" or name == "dz" or kind != "d":
                base_of[name], stride_of[name] = base, stride
            jobs["g", name] = Gather(me, partner, hops, left, matrix, cols, *sems[:2])
            sum_left = left if name != "dz" else Z
            jobs["s", name] = Scatter(
                me, partner, hops[::-1], sum_left, stage, cols, r.come[name], *sems[2:], finish
            )
        plan = plan_of()[0]
        pl.semaphore_wait(barrier, len(friends))
    else:
        load_x.start()
        load_cot.start()
        loads = [
            pltpu.make_async_copy(src, dst, r.local.at[3 + n])
            for n, (src, dst) in enumerate(
                [(r.qkv_mat, r.wq), (r.proj_mat, r.wo), (r.up_mat, r.w1), (r.down_mat, r.w2)]
            )
        ]
        for load in loads:
            load.start()
        r.vec[...] = r.vec_in[...]
        for load in loads:
            load.wait()

    def exchange(name, index):
        if not linked:
            return
        for (step, at), taken in plan.items():
            if step != name or not taken:
                continue

            def act(taken=taken):
                for kind, stream, k in taken:
                    jobs[kind, stream].step(k)

            if isinstance(index, int):
                if index == at:
                    act()
            else:
                pl.when(index == at)(act)

    vec, gvec = r.vec, r.gvec
    gvec[...] = jnp.zeros((VROWS, 128), F32)

    def vector(first, count):
        return jnp.concatenate([vec[first + n : first + n + 1, :] for n in range(count)], axis=1)

    def add_vector(first, values):
        for n in range(values.shape[1] // 128):
            gvec[first + n : first + n + 1, :] += values[:, 128 * n : 128 * n + 128]

    def whole(ref, cols):
        got = ref[lead + (slice(None), cols)]
        return got.reshape(-1, got.shape[-1])

    def down_chunk(c):
        if linked:
            return r.w2[c // 2, c % 2].reshape(CHUNK, D)
        return r.w2[pl.ds(pl.multiple_of(c * CHUNK, CHUNK), CHUNK), :]

    rows_of = lambda i, size: pl.ds(pl.multiple_of(i * size, size), size)
    act = lambda rows: r.big.at[rows, pl.ds(0, 512)]
    grad_pre = lambda rows: r.big.at[rows, pl.ds(512, 512)]
    normed_two = lambda rows: r.big.at[rows, pl.ds(1024, 512)]
    everything = pl.ds(0, tokens_n)

    exchange("first", 0)
    if linked:
        for name, buf, rows, width in (
            ("proj_weight", r.wo, 16, 4),
            ("up_weight", r.w1, 16, 16),
            ("down_weight", r.w2, 64, 4),
        ):
            loads[name].wait()
            share(getattr(r, "my_" + name), buf, rows, width, lambda j: j)
    exchange("norm", 0)
    load_x.wait()

    def norm_one(i, carry):
        rows = rows_of(i, 256)
        r.grad_h[rows, :] = norm(r.x[rows, :].astype(F32))[0]
        return carry

    lax.fori_loop(0, tokens_n // 256, norm_one, 0)
    load_cot.wait()

    def mask_one(i, carry):
        rows = rows_of(i, 256)
        per = CLIP_LEN // 256
        place_in = (i % per) * 256 + lax.broadcasted_iota(jnp.int32, (256, 1), 0)
        dy = jnp.where(place_in >= r.cond_frames[i // per] * FRAME_TOK, r.dy[rows, :].astype(F32), 0.0)
        add_vector(B2, column_sum(dy))
        r.dy[rows, :] = dy.astype(BF16)
        return carry

    lax.fori_loop(0, tokens_n // 256, mask_one, 0)
    exchange("affine", 0)
    if linked:
        vec[...] = jnp.zeros((VROWS, 128), F32)
        for n in range(dp * fs):
            row = n * per // 128
            vec[row : row + 3, :] += r.vec_parts[split_bits(n) + (slice(0, 3),)]

    def affine_one(i, carry):
        rows = rows_of(i, 256)
        r.a[rows, :] = (r.grad_h[rows, :] * vector(G1, 4) + vector(S1, 4)).astype(BF16)
        return carry

    lax.fori_loop(0, tokens_n // 256, affine_one, 0)

    def forward(t, carry):
        exchange("fwd", t)
        pair, clip = t // clips, t % clips

        @pl.when(clip == 0)
        def _():
            cols = pl.ds(pl.multiple_of(pair * 384, 128), 384)
            matrix = whole(r.wq, cols)
            bias = jnp.concatenate([vec[pl.ds(BQKV + 4 * n + pair, 1), :] for n in range(3)], axis=1)
            for i in range(tiles):
                rows = slice(i * TILE, i * TILE + TILE)
                r.qkv[rows, cols] = (dot(r.a[rows, :], matrix) + bias).astype(BF16)

        attend_forward(r.qkv, r.mixed, r.lse, clip * CLIP_LEN, pair)
        return carry

    lax.fori_loop(0, PAIRS * clips, forward, 0)

    exchange("mid", 0)

    def middle(i, carry):
        rows = rows_of(i, TILE)
        h = r.x[rows, :].astype(F32) + dot(r.mixed[rows, :], whole(r.wo, slice(None))) + vector(BO, 4)
        hat, scale = norm(h)
        r.hat[rows, :] = hat.astype(BF16)
        r.scale[rows, :] = jnp.broadcast_to(scale, (TILE, 128))
        normed_two(rows)[...] = (hat * vector(G2, 4) + vector(S2, 4)).astype(BF16)
        r.h_low[rows, :] = (h + vector(B2, 4)).astype(BF16)
        r.grad_h[rows, :] = jnp.zeros((TILE, D), F32)
        return carry

    lax.fori_loop(0, tiles, middle, 0)

    def park_of(c):
        cols = pl.ds(pl.multiple_of(c * CHUNK, CHUNK), CHUNK)
        return pltpu.make_async_copy(act(everything), r.parked.at[:, cols], r.local.at[2])

    def feed(c, carry):
        exchange("ffa", c)
        cols = pl.ds(pl.multiple_of(c * CHUNK, CHUNK), CHUNK)
        up, down = whole(r.w1, cols), down_chunk(c)
        bias = jnp.concatenate([vec[pl.ds(B1 + 4 * c + n, 1), :] for n in range(4)], axis=1)
        spans = [slice(i * TILE, i * TILE + TILE) for i in range(tiles)]

        def products(rows):
            return dot(normed_two(rows)[...], up), dot(r.dy[rows, :], down, NT)

        park = park_of(c)

        @pl.when(c > 0)
        def _():
            park.wait()

        ready, late = products(spans[0]), None
        bias_grad = jnp.zeros((1, CHUNK), F32)
        for i, rows in enumerate(spans):
            pre, grad_act = ready
            if i + 1 < tiles:
                ready = products(spans[i + 1])
            value, slope = gelu_both(pre + bias)
            value = value.astype(BF16)
            grad = slope * grad_act
            bias_grad = bias_grad + column_sum(grad)
            grad = grad.astype(BF16)
            act(rows)[...] = value
            grad_pre(rows)[...] = grad
            if late:
                r.grad_h[late[0], :] += dot(late[1], up, NT)
            late = (rows, grad)
        r.grad_h[late[0], :] += dot(late[1], up, NT)
        for n in range(4):
            gvec[pl.ds(B1 + 4 * c + n, 1), :] = bias_grad[:, 128 * n : 128 * n + 128]
        exchange("ffb", c)
        park.start()
        grad_up = dot(normed_two(everything)[...], grad_pre(everything)[...], TN).astype(BF16)
        grad_down = dot(act(everything)[...], r.dy[...], TN).astype(BF16)
        if linked:
            r.w1[lead + (slice(None), cols)] = grad_up.reshape((2,) * bits + (16, CHUNK))
            r.sd[c // 2, c % 2] = grad_down.reshape((2,) * (bits - 2) + (64, D))
        else:
            r.w1[:, cols] = grad_up
            r.sd[rows_of(c, CHUNK), :] = grad_down
        return carry

    lax.fori_loop(0, chunks, feed, 0)
    park_of(0).wait()

    exchange("ln2", 0)
    ri = lax.broadcasted_iota(jnp.int32, (128, 128), 0)
    ci = lax.broadcasted_iota(jnp.int32, (128, 128), 1)
    other_half = jnp.where((ri < 64) != (ci < 64), 1.0, 0.0).astype(BF16)
    other_half = jnp.concatenate([other_half, other_half], axis=0)
    spare = lax.broadcasted_iota(jnp.int32, (TILE, 128), 1) & 63
    proj = whole(r.wo, slice(None))

    def norm_part(rows):
        grad, hat, scale = r.grad_h[rows, :], r.hat[rows, :].astype(F32), r.scale[rows, :1]
        add_vector(G2, column_sum(grad * hat))
        add_vector(S2, column_sum(grad))
        grad = r.dy[rows, :].astype(F32) + norm_back(grad, hat, scale, vector(G2, 4))
        r.grad_h[rows, :] = grad
        low = grad.astype(BF16)
        add_vector(BO, column_sum(low.astype(F32)))
        return low

    def proj_part(rows, low):
        mixed = r.mixed[rows, :]
        part = dot(mixed, low, TN)
        grad_mixed = dot(low, proj, NT).astype(BF16)
        r.dy[rows, :] = grad_mixed
        product = grad_mixed.astype(F32) * mixed.astype(F32)
        high = product.astype(BF16)
        rest = (product - high.astype(F32)).astype(BF16)
        for p in range(PAIRS):
            cols = slice(128 * p, 128 * p + 128)
            row_dot = dot(jnp.concatenate([high[:, cols], rest[:, cols]], axis=1), other_half)
            top = row_dot.astype(BF16).astype(F32)
            r.mixed[rows, cols] = jnp.where(
                spare == 0, -top, jnp.where(spare == 1, top - row_dot, 0.0)
            ).astype(BF16)
        return part

    spans = [slice(i * TILE, i * TILE + TILE) for i in range(tiles)]
    grad_proj = jnp.zeros((D, D), F32)
    low = norm_part(spans[0])
    for i, rows in enumerate(spans):
        after = norm_part(spans[i + 1]) if i + 1 < tiles else None
        grad_proj = grad_proj + proj_part(rows, low)
        low = after
    grad_proj = grad_proj.astype(BF16)
    if linked:
        r.wo[...] = grad_proj.reshape((2,) * bits + (16, D))
    else:
        r.wo[...] = grad_proj

    def backward(t, carry):
        exchange("bwd", t)
        pair, clip = t // clips, t % clips
        attend_backward(r.qkv, r.dy, r.lse, r.mixed, r.big, r.grad_qt, clip * CLIP_LEN, pair)

        @pl.when(clip == clips - 1)
        def _():
            cols = pl.ds(pl.multiple_of(pair * 384, 128), 384)
            grad = r.big[:, cols]
            sums = column_sum(grad.astype(F32))
            for n in range(3):
                gvec[pl.ds(BQKV + 4 * n + pair, 1), :] = sums[:, 128 * n : 128 * n + 128]
            matrix = dot(r.a[...], grad, TN).astype(BF16)
            if linked:
                r.sq[lead + (slice(None), cols)] = matrix.reshape((2,) * bits + (16, 384))
            else:
                r.sq[:, cols] = matrix

        return carry

    lax.fori_loop(0, PAIRS * clips, backward, 0)

    fetches = []
    for c in range(chunks):
        dst = r.qkv.at[:, c * CHUNK : c * CHUNK + CHUNK] if c < 3 else r.dy
        src = r.parked.at[:, c * CHUNK : c * CHUNK + CHUNK]
        fetches.append(pltpu.make_async_copy(src, dst, r.local.at[c]))
        fetches[-1].start()
    matrix = whole(r.wq, slice(None))
    spans = [slice(i * TILE, i * TILE + TILE) for i in range(tiles)]
    for i, rows in enumerate(spans):
        exchange("sums", i)
        grad = dot(r.big[rows, :], matrix, NT)
        hat, scale = norm(r.x[rows, :].astype(F32))
        r.hat[rows, :] = hat.astype(BF16)
        r.scale[rows, :] = jnp.broadcast_to(scale, (TILE, 128))
        add_vector(G1, column_sum(grad * hat))
        add_vector(S1, column_sum(grad))
        r.a[rows, :] = grad.astype(BF16)
    if linked:
        for n in range(dp * fs):
            row = n * per // 128
            r.gvec_parts[split_bits(n)] = jnp.concatenate(
                [gvec[row : row + 3, :], jnp.zeros((5, 128), F32)], axis=0
            )
    stores = []
    for i, rows in enumerate(spans):
        exchange("ln1", i)
        grad = norm_back(r.a[rows, :].astype(F32), r.hat[rows, :].astype(F32), r.scale[rows, :1], vector(G1, 4))
        r.lse[rows, :] = (r.grad_h[rows, :] + grad).astype(BF16)
        stores.append(pltpu.make_async_copy(r.lse.at[rows, :], r.input_grad.at[rows, :], r.local.at[4 + i]))
        stores[-1].start()

    for fetch in fetches:
        fetch.wait()
    down = whole(r.w2, slice(None))
    for i, rows in enumerate(spans):
        exchange("out", i)
        value = jnp.concatenate([r.qkv[rows, :], r.dy[rows, :]], axis=1)
        r.mixed[rows, :] = (r.h_low[rows, :].astype(F32) + dot(value, down)).astype(BF16)
        stores.append(pltpu.make_async_copy(r.mixed.at[rows, :], r.output.at[rows, :], r.local.at[8 + i]))
        stores[-1].start()
    exchange("end", 0)
    if not linked:
        for n, (src, dst) in enumerate(
            [(r.sq, r.qkv_grad), (r.wo, r.proj_grad), (r.w1, r.up_grad), (r.sd, r.down_grad)]
        ):
            stores.append(pltpu.make_async_copy(src, dst, r.local.at[n]))
            stores[-1].start()
        r.total_vec[...] = gvec[...]
    for store in stores:
        store.wait()


def run_block(dp, fs, linked, tokens, cotangent, cond_frames, weights):
    n = tokens.shape[0]
    shape = jax.ShapeDtypeStruct
    vmem, smem, any_ = (
        pl.BlockSpec(memory_space=pltpu.VMEM),
        pl.BlockSpec(memory_space=pltpu.SMEM),
        pl.BlockSpec(memory_space=pl.ANY),
    )
    bits = BITS if linked else 0
    ins = ["tokens", "cotangent", "cond_frames"]
    in_specs = [any_, any_, smem]
    outs = {"output": ((n, D), BF16, any_), "input_grad": ((n, D), BF16, any_)}
    outs["parked"] = ((n, FF), BF16, any_)
    outs["total_vec"] = ((8 if linked else VROWS, 128), F32, vmem)
    if linked:
        ins += ["qkv_weight", "proj_weight", "up_weight", "down_weight", "vectors"]
        in_specs += [any_] * 5
        outs["total"] = ((768, 128), F32, vmem)
        matrix = lambda rows, cols: pltpu.VMEM((2,) * bits + (rows // 2**bits, cols), BF16)
    else:
        ins += ["qkv_mat", "proj_mat", "up_mat", "down_mat", "vec_in"]
        in_specs += [any_] * 4 + [vmem]
        outs["qkv_grad"] = ((D, 3 * D), BF16, any_)
        outs["proj_grad"] = ((D, D), BF16, any_)
        outs["up_grad"] = ((D, FF), BF16, any_)
        outs["down_grad"] = ((FF, D), BF16, any_)
        matrix = lambda rows, cols: pltpu.VMEM((rows, cols), BF16)
    scratch = {
        "x": pltpu.VMEM((n, D), BF16),
        "a": pltpu.VMEM((n, D), BF16),
        "dy": pltpu.VMEM((n, D), BF16),
        "qkv": pltpu.VMEM((n, 3 * D), BF16),
        "mixed": pltpu.VMEM((n, D), BF16),
        "lse": pltpu.VMEM((n, D), BF16),
        "hat": pltpu.VMEM((n, D), BF16),
        "h_low": pltpu.VMEM((n, D), BF16),
        "grad_h": pltpu.VMEM((n, D), F32),
        "scale": pltpu.VMEM((n, 128), F32),
        "big": pltpu.VMEM((n, 3 * D), BF16),
        "grad_qt": pltpu.VMEM((128, CLIP_LEN), F32),
        "wq": matrix(D, 3 * D),
        "sq": matrix(D, 3 * D),
        "wo": matrix(D, D),
        "w1": matrix(D, FF),
        "w2": matrix(FF, D),
        "sd": matrix(FF, D),
        "vec": pltpu.VMEM((VROWS, 128), F32),
        "gvec": pltpu.VMEM((VROWS, 128), F32),
        "local": pltpu.SemaphoreType.DMA((12,)),
    }
    names = ins + list(outs) + list(scratch)
    shapes = list(scratch.values())
    come_names = []
    if linked:
        streams = streams_of()
        for name in ("vec_parts", "gvec_parts"):
            names.append(name)
            shapes.append(pltpu.VMEM((2,) * bits + (8, 128), F32))
        for name, held in zip(ins[3:], weights):
            names.append("my_" + name)
            shapes.append(pltpu.VMEM(held.shape, F32))
        names.append("down_part")
        shapes.append(pltpu.VMEM((2, 2, 64, D), BF16))
        for name in ("gather_send", "gather_recv", "sum_send", "sum_recv"):
            names.append(name)
            shapes.append(pltpu.SemaphoreType.DMA((len(streams), 7)))
        for name, (hops, left, rows, width, size) in streams.items():
            held = len(left) if name != "dz" else 2
            for k, hop in enumerate(hops[::-1]):
                held -= len(hop)
                come_names.append((name, f"{name}_{k}"))
                names.append(f"{name}_{k}")
                kind = BF16 if size == 2 else F32
                shapes.append(pltpu.VMEM((len(masks_of(hop)),) + (2,) * held + (rows, width), kind))

    def body(*refs):
        table = dict(zip(names, refs))
        if linked:
            table["come"] = {}
            for name, key in come_names:
                table["come"].setdefault(name, []).append(table.pop(key))
            keys = ("gather_send", "gather_recv", "sum_send", "sum_recv")
            table["sems"] = [table.pop(key) for key in keys]
        block_kernel(dp, fs, n, linked, list(table), *table.values())

    params = dict(vmem_limit_bytes=64 << 20)
    if linked:
        params.update(collective_id=0, has_side_effects=True)
    return pl.pallas_call(
        body,
        out_shape=[shape(s, t) for s, t, _ in outs.values()],
        in_specs=in_specs,
        out_specs=[spec for *_, spec in outs.values()],
        scratch_shapes=shapes,
        compiler_params=pltpu.CompilerParams(**params),
        name="block",
    )(tokens, cotangent, cond_frames, *weights)


def adamw(weight, grad, first, second, average, rate, decay):
    first_new = BETA_ONE * first + (1.0 - BETA_ONE) * grad
    second_new = BETA_TWO * second + (1.0 - BETA_TWO) * grad * grad
    first_hat = first_new / (1.0 - BETA_ONE**STEP)
    second_hat = second_new / (1.0 - BETA_TWO**STEP)
    weight_new = weight - rate * (first_hat / (jnp.sqrt(second_hat) + ADAM_EPS) + decay * weight)
    average_new = EMA_KEEP * average + (1.0 - EMA_KEEP) * weight_new
    return (first_new, second_new, weight_new, average_new)


def adam_kernel(dp, fs, linked, *refs):
    total, total_vec, output, input_grad = refs[:4]
    ins, outs, (output_new, input_grad_new) = refs[4:24], refs[24:44], refs[44:46]
    held, made = refs[46:66], refs[66:86]
    low_grad, full_grad, out_low, fetched, moved, loaded, stored = refs[86:]
    loads = [pltpu.make_async_copy(a, b, loaded.at[n]) for n, (a, b) in enumerate(zip(ins, held))]
    stores = [pltpu.make_async_copy(a, b, stored.at[n]) for n, (a, b) in enumerate(zip(made, outs))]
    fetches, moves = [], []
    for a, b, c, d in ((input_grad, low_grad, full_grad, input_grad_new), (output, out_low, out_low, output_new)):
        size = a.shape[0] // 4
        for n in range(4):
            rows, at = pl.ds(n * size, size), len(moves)
            fetches.append(pltpu.make_async_copy(a.at[rows, :], b.at[rows, :], fetched.at[at]))
            moves.append(pltpu.make_async_copy(c.at[rows, :], d.at[rows, :], moved.at[at]))
    for load in fetches + loads:
        load.start()
    for n, (fetch, move) in enumerate(zip(fetches, moves)):
        fetch.wait()
        if n < 4:
            rows = slice(n * size, n * size + size)
            full_grad[rows, :] = low_grad[rows, :].astype(F32)
        move.start()

    def update(m, grad, rate, decay):
        for load in loads[4 * m : 4 * m + 4]:
            load.wait()
        weight, first, second, average = (ref[...] for ref in held[4 * m : 4 * m + 4])
        new = adamw(weight, grad, first, second, average, rate, decay)
        for ref, value in zip(made[4 * m : 4 * m + 4], new):
            ref[...] = value
        for store in stores[4 * m : 4 * m + 4]:
            store.start()

    base = 0
    for m in range(4):
        size = held[4 * m].shape[0]
        update(m, total[base : base + size, :], RATE_MATRIX, WEIGHT_DECAY)
        base += size
    per = VEC // (dp * fs)
    start = (lax.axis_index("dp") * fs + lax.axis_index("fsdp")) * per
    lane0 = start % 128
    lane = lax.broadcasted_iota(jnp.int32, (1, 128), 1)
    back = lax.rem(128 - lane0, 128)
    row = 0 if linked else start // 128
    parts = [pltpu.roll(total_vec[pl.ds(row + n, 1), :], back, 1) for n in range(3)]
    keep = 128 - lane0
    grad = jnp.concatenate(
        [jnp.where(lane < keep, parts[0], parts[1]), jnp.where(lane < keep, parts[1], parts[2])], axis=1
    )[:, :per]
    update(4, grad, RATE_VECTOR, 0.0)
    for copy in stores + moves:
        copy.wait()


def run_adam(dp, fs, linked, total, total_vec, output, input_grad, state):
    flat = [a.reshape(-1, 128) for a in state[:16]] + list(state[16:])
    vmem, any_ = pl.BlockSpec(memory_space=pltpu.VMEM), pl.BlockSpec(memory_space=pl.ANY)
    shapes = [jax.ShapeDtypeStruct(a.shape, F32) for a in flat]
    shapes += [jax.ShapeDtypeStruct(output.shape, BF16), jax.ShapeDtypeStruct(output.shape, F32)]
    new = pl.pallas_call(
        functools.partial(adam_kernel, dp, fs, linked),
        out_shape=shapes,
        in_specs=[vmem] * 2 + [any_] * 22,
        out_specs=[any_] * 22,
        scratch_shapes=[pltpu.VMEM(a.shape, F32) for a in flat] * 2
        + [pltpu.VMEM(output.shape, t) for t in (BF16, F32, BF16)]
        + [pltpu.SemaphoreType.DMA((n,)) for n in (8, 8, 20, 20)],
        compiler_params=pltpu.CompilerParams(vmem_limit_bytes=64 << 20),
        name="adam",
    )(total, total_vec, output, input_grad, *flat)
    return list(new[20:]) + [a.reshape(b.shape) for a, b in zip(new, state)]


def local(dp, fs, tokens, cotangent, cond_frames, *state):
    weights, firsts, seconds, averages = (state[5 * n : 5 * n + 5] for n in range(4))
    shards = dp * fs
    linked = shards == 2**BITS and not (dp & (dp - 1))
    if linked:
        shares = [w.reshape(-1, 128) for w in weights[:4]] + [weights[4]]
        output, input_grad, _, total_vec, total = run_block(
            dp, fs, True, tokens, cotangent, cond_frames, shares
        )
    else:
        gathered = [
            lax.all_gather(w.astype(BF16), AXES, axis=0, tiled=True) for w in weights
        ]
        qkv = gathered[0].reshape(D, 3, PAIRS, 128).swapaxes(1, 2).reshape(D, 3 * D)
        vec = jnp.pad(gathered[4].astype(F32).reshape(-1, 128), ((0, VROWS - VEC // 128), (0, 0)))
        mats = [qkv] + [g.reshape(-1, c) for g, c in zip(gathered[1:4], (D, FF, D))] + [vec]
        output, input_grad, _, total_vec, *grads = run_block(
            dp, fs, False, tokens, cotangent, cond_frames, mats
        )
        grads[0] = grads[0].reshape(D, PAIRS, 3, 128).swapaxes(1, 2).reshape(D, 3 * D)
        scatter = lambda g: lax.psum_scatter(
            g.astype(F32).reshape(shards, -1), AXES, scatter_dimension=0, tiled=True
        )
        total = jnp.concatenate([scatter(g).reshape(-1, 128) for g in grads], axis=0)
        total_vec = lax.psum(total_vec, AXES)
    order = [group[m] for m in range(5) for group in (weights, firsts, seconds, averages)]
    return tuple(run_adam(dp, fs, linked, total, total_vec, output, input_grad, order))


def solution(mesh):
    dp, fs = mesh.shape["dp"], mesh.shape["fsdp"]
    split = P(AXES, None)
    return jax.shard_map(
        functools.partial(local, dp, fs),
        mesh=mesh,
        in_specs=(split, split, P(AXES)) + (split,) * 20,
        out_specs=(split,) * 22,
        check_vma=False,
    )
```

```python
import functools
from types import SimpleNamespace

import jax
import jax.numpy as jnp
from jax import lax
from jax.experimental import pallas as pl
from jax.experimental.pallas import tpu as pltpu
from jax.sharding import PartitionSpec as P

D = 512
FF = 2048
HEADS = 8
HEAD_DIM = 64
FRAME_TOK = 64
STEP = 10
CLIP_LEN = 1024
VEC = 9 * D + FF

EPS = 1e-05
BETA_ONE = 0.9
BETA_TWO = 0.95
ADAM_EPS = 1e-08
RATE_MATRIX = 0.02
RATE_VECTOR = 0.2
WEIGHT_DECAY = 0.1
EMA_KEEP = 0.9
NEG = -1e30

AXES = ("dp", "fsdp")
MESH = pl.DeviceIdType.MESH
BF16 = jnp.bfloat16
F32 = jnp.float32
NN = (((1,), (0,)), ((), ()))
NT = (((1,), (1,)), ((), ()))
TN = (((0,), (0,)), ((), ()))
PAIRS = HEADS // 2
QB = 256
TILE = 512
CHUNK = 512
VROWS = 56
G1, S1, BQKV, BO, G2, S2, B1, B2 = 0, 4, 8, 20, 24, 28, 32, 48
GELU_A = 0.7978845608028654
GELU_B = 0.044715


def dot(left, right, dims=NN):
    return lax.dot_general(left, right, dims, preferred_element_type=F32)


BITS = 5
Z, Y, X, XY, CORE = (0, 1), (2,), (3,), (2, 3), (4,)
LINK = {0: "z", 1: "z", 2: "y", 3: "x", 4: "core"}


def masks_of(hop):
    return [(hop[0],)] if len(hop) == 1 else [(hop[1],), (hop[0],), hop]


def place(dp, fs):
    hi, lo = dp.bit_length() - 1, fs.bit_length() - 1
    i, f = lax.axis_index("dp"), lax.axis_index("fsdp")
    me = [(i // 2 ** (hi - 1 - t)) % 2 for t in range(hi)]
    me += [(f // 2 ** (lo - 1 - t)) % 2 for t in range(lo)]

    def partner(mask):
        at_i, at_f = i, f
        for t in mask:
            if t < hi:
                step = 2 ** (hi - 1 - t)
                at_i = at_i + step - 2 * step * me[t]
            else:
                step = 2 ** (hi + lo - 1 - t)
                at_f = at_f + step - 2 * step * me[t]
        return (at_i, at_f)

    return me, partner


def remote(src, dst, send, recv, device):
    return pltpu.make_async_remote_copy(
        src_ref=src, dst_ref=dst, send_sem=send, recv_sem=recv, device_id=device, device_id_type=MESH
    )


def split_bits(n):
    return tuple(n >> (BITS - 1 - t) & 1 for t in range(BITS))


class Transfer:
    def step(self, k):
        if k:
            for copy in self.hops[k - 1]:
                copy.wait_recv()
            self.arrived(k - 1)
        if k < len(self.hops):
            for copy in self.hops[k]:
                copy.start()
        else:
            for hop in self.hops:
                for copy in hop:
                    copy.wait_send()

    def arrived(self, k):
        pass


class Gather(Transfer):
    def __init__(self, me, partner, hops, left, buf, cols, send, recv):
        self.hops = []
        done, n = set(), 0
        for hop in hops:
            at = tuple(slice(None) if t in done else me[t] for t in left)
            ref = buf.at[at + (slice(None), cols)]
            copies = []
            for mask in masks_of(hop):
                copies.append(remote(ref, ref, send(n), recv(n), partner(mask)))
                n += 1
            self.hops.append(copies)
            done.update(hop)


class Scatter(Transfer):
    def __init__(self, me, partner, hops, left, stage, cols, come, send, recv, finish):
        self.hops, self.sums = [], []
        self.finish = finish
        left, n = list(left), 0
        source, source_cols = stage, cols
        for k, hop in enumerate(hops):

            def part(mask):
                at = [(1 - me[t] if t in mask else me[t]) if t in hop else slice(None) for t in left]
                return tuple(at) + (slice(None), source_cols)

            copies = []
            for slot, mask in enumerate(masks_of(hop)):
                copies.append(
                    remote(source.at[part(mask)], come[k].at[slot], send(n), recv(n), partner(mask))
                )
                n += 1
            self.hops.append(copies)
            self.sums.append((source, part(()), come[k], len(copies)))
            left = [t for t in left if t not in hop]
            source, source_cols = come[k].at[0], slice(None)

    def arrived(self, k):
        source, at, come, count = self.sums[k]
        if k + 1 < len(self.hops) and count == 1:
            come[0] = source[at] + come[0]
            return
        total = source[at].astype(F32)
        for slot in range(count):
            total = total + come[slot].astype(F32)
        if k + 1 < len(self.hops):
            come[0] = total.astype(come.dtype)
        else:
            self.finish(total)


def streams_of():
    first, second = (Z, Y, X, CORE), (Z, X, Y, CORE)
    every = (0, 1, 2, 3, 4)
    streams = {"vec": ((Z, XY, CORE), every, 8, 128, 4)}
    for p in range(PAIRS):
        hops = (Z, XY, CORE) if p in (0, 1, PAIRS - 1) else (first, second)[p % 2]
        streams[f"q{p}"] = (hops, every, 16, 384, 2)
    streams["o"] = ((Z, XY, CORE), every, 16, 512, 2)
    streams["u0"] = (second, every, 16, 512, 2)
    streams["dz"] = ((Z,), every, 64, 512, 2)
    streams["d0"] = (first[1:], every[2:], 64, 512, 2)
    for c in range(1, FF // CHUNK):
        streams[f"u{c}"] = ((second, first)[c % 2], every, 16, 512, 2)
        streams[f"d{c}"] = ((first, second)[c % 2][1:], every[2:], 64, 512, 2)
    return streams


def steps_of():
    steps = [("first", 0, 0.6, [], []), ("norm", 0, 1.5, [], []), ("affine", 0, 0.8, ["vec"], [])]
    steps += [("fwd", t, 2.1 + (t % 2 == 0), [f"q{t // 2}"], []) for t in range(2 * PAIRS)]
    steps += [("mid", 0, 3.1, ["o"], [])]
    for c in range(FF // CHUNK):
        steps += [("ffa", c, 4.4, ["dz", f"d{c}", f"u{c}"], []), ("ffb", c, 2.4, [], [f"u{c}", f"d{c}"])]
    steps += [("ln2", 0, 5.5, [], ["o"])]
    steps += [("bwd", t, 3.5 + (t % 2), [], [f"q{t // 2}"] if t % 2 else []) for t in range(2 * PAIRS)]
    steps += [("sums", t, 1.2, [], ["vec"] if t == 3 else []) for t in range(4)]
    steps += [("ln1", t, 0.6, [], []) for t in range(4)]
    steps += [("out", t, 1.1, [], []) for t in range(4)]
    steps += [("end", 0, 0.0, ["all"], [])]
    return steps


def plan_of():
    latency = {"z": 2.5, "y": 2.2, "x": 2.2, "core": 0.8}
    rate = {"z": 45e3, "y": 45e3, "x": 45e3, "core": 250e3}
    free = dict.fromkeys(rate, 0.0)
    streams = streams_of()
    rank = {("g", s): n for n, s in enumerate(streams)}
    rank.update({("s", s): 50 + n for n, s in enumerate(streams)})
    rank["s", f"q{PAIRS - 1}"], rank["s", "vec"] = 1, 0
    arrived = {}
    after = {("g", f"d{c}"): [("g", "dz")] for c in range(4)}
    after["s", "dz"] = [("s", f"d{c}") for c in range(4)]
    early = ("vec", "q0")
    pending = [("g", s, 0, 0.0 if s in early else 0.5) for s in streams if ("g", s) not in after]
    plan, model = {}, []
    now = 0.0

    def cost(kind, name, k):
        hops, bits, rows, cols, size = streams[name]
        hop = (hops if kind == "g" else hops[::-1])[k]
        done = [t for h in (hops[:k] if kind == "g" else hops[: len(hops) - 1 - k]) for t in h]
        held = rows * cols * size * 2 ** len(done)
        if hop == Z:
            return {"z": 4 * held / rate["z"]}
        if hop == XY:
            return {"x": 2 * held / rate["x"], "y": 2 * held / rate["y"]}
        return {LINK[hop[0]]: held / rate[LINK[hop[0]]]}

    def start_of(item):
        kind, name, k, ready = item
        if k == len(streams[name][0]):
            return ready
        return max([ready] + [free[link] for link in cost(kind, name, k)])

    def issue(item, at):
        kind, name, k, ready = item
        pending.remove(item)
        if k == len(streams[name][0]):
            arrived[kind, name] = max(at, ready)
            for other, needs in after.items():
                if (kind, name) in needs and all(n in arrived for n in needs):
                    pending.append((*other, 0, max(at, ready)))
            return
        begin, end = max(at, start_of(item)), 0.0
        for link, time in cost(kind, name, k).items():
            free[link] = begin + time
            end = max(end, begin + time + latency[link])
        pending.append((kind, name, k + 1, end))

    for name, index, time, needs, feeds in steps_of():
        taken = plan.setdefault((name, index), [])

        def missing():
            if "all" in needs:
                return bool(pending)
            return any(("g", n) not in arrived for n in needs)

        begun = now
        while True:
            ready = [
                i
                for i in pending
                if i[3] <= now and start_of(i) <= now + max(1.0, 0.5 * time)
            ]
            if ready:
                item = min(ready, key=lambda i: rank[i[:2]])
            elif missing():
                item = min(pending, key=lambda i: (max(start_of(i), i[3]), rank[i[:2]]))
                now = max(now, item[3], start_of(item))
            else:
                break
            taken.append(item[:3])
            issue(item, now)
        model.append((begun, now, name, index, taken))
        now += time
        for fed in feeds:
            pending.append(("s", fed, 0, now))
    return plan, model


def norm(values):
    mean = jnp.mean(values, axis=-1, keepdims=True)
    centred = values - mean
    scale = lax.rsqrt(jnp.mean(centred * centred, axis=-1, keepdims=True) + EPS)
    return centred * scale, scale


def norm_back(grad, hat, scale, gain):
    inner = grad * gain
    return scale * (
        inner
        - jnp.mean(inner, axis=-1, keepdims=True)
        - hat * jnp.mean(inner * hat, axis=-1, keepdims=True)
    )


def gelu_both(pre):
    square = pre * pre
    half = 0.5 + 0.5 * jnp.tanh(pre * (GELU_A + (GELU_A * GELU_B) * square))
    act = pre * half
    return act, half + (act - act * half) * (2 * GELU_A + (6 * GELU_A * GELU_B) * square)


def column_sum(values):
    return jnp.sum(values, axis=0, keepdims=True)


def attend_forward(qkv, mixed, lse, row0, pair):
    rows = lambda start, size: pl.ds(pl.multiple_of(row0 + start, QB), size)
    cols = lambda part: pl.ds(pl.multiple_of(pair * 384 + part * 128, 128), 128)
    out_cols = pl.ds(pl.multiple_of(pair * 128, 128), 128)
    low_all = lax.broadcasted_iota(jnp.int32, (CLIP_LEN, 128), 1) < 64
    lane = lax.broadcasted_iota(jnp.int32, (QB, 128), 1)
    low = lane < 64
    spare = lane & 63
    causal = lax.broadcasted_iota(jnp.int32, (QB, QB), 1) <= lax.broadcasted_iota(
        jnp.int32, (QB, QB), 0
    )
    one, zero = jnp.ones((), BF16), jnp.zeros((), BF16)
    queries = qkv[rows(0, CLIP_LEN), cols(0)] * jnp.asarray(HEAD_DIM**-0.5, BF16)
    keys = qkv[rows(0, CLIP_LEN), cols(1)]
    values = qkv[rows(0, CLIP_LEN), cols(2)]
    head_q = [jnp.where(low_all, queries, zero), jnp.where(low_all, zero, queries)]
    head_v = [jnp.where(low_all, values, one), jnp.where(low_all, one, values)]

    def scores(item):
        block, head = item
        n = QB * block
        s = dot(head_q[head][n : n + QB], keys[: n + QB], NT)
        diagonal = jnp.where(causal, s[:, n:], NEG)
        return jnp.concatenate([s[:, :n], diagonal], axis=1) if n else diagonal

    items = [(block, head) for block in reversed(range(CLIP_LEN // QB)) for head in range(2)]
    ahead = 3
    ready = {t: scores(items[t]) for t in range(ahead)}
    sums, tops = {}, {}
    for t, (block, head) in enumerate(items):
        s = ready.pop(t)
        top = jnp.max(s, axis=1, keepdims=True)
        if t + ahead < len(items):
            ready[t + ahead] = scores(items[t + ahead])
        weights = jnp.exp(s - top).astype(BF16)
        sums[head] = dot(weights, head_v[head][: QB * (block + 1)])
        tops[head] = top
        if head == 1:
            at = rows(QB * block, QB)
            top_sum = jnp.where(low, sums[0], sums[1])
            total = jnp.where(low, sums[1], sums[0])
            mixed[at, out_cols] = (top_sum / pltpu.roll(total, 64, 1)).astype(BF16)
            log_sum = jnp.where(low, tops[1], tops[0]) + jnp.log(total)
            high = log_sum.astype(BF16).astype(F32)
            lse[at, out_cols] = jnp.where(
                spare == 0, -high, jnp.where(spare == 1, high - log_sum, 0.0)
            ).astype(BF16)


def attend_backward(qkv, grad, lse, dots, grad_qkv, grad_qt, row0, pair):
    rows = lambda start, size: pl.ds(pl.multiple_of(row0 + start, QB), size)
    cols = lambda part: pl.ds(pl.multiple_of(pair * 384 + part * 128, 128), 128)
    one_cols = pl.ds(pl.multiple_of(pair * 128, 128), 128)
    low = lax.broadcasted_iota(jnp.int32, (CLIP_LEN, 128), 1) < 64
    causal = lax.broadcasted_iota(jnp.int32, (QB, QB), 0) <= lax.broadcasted_iota(
        jnp.int32, (QB, QB), 1
    )
    one, zero = jnp.ones((), BF16), jnp.zeros((), BF16)
    every = rows(0, CLIP_LEN)
    queries = qkv[every, cols(0)] * jnp.asarray(HEAD_DIM**-0.5, BF16)
    keys = qkv[every, cols(1)]
    values = qkv[every, cols(2)]
    out_grad = grad[every, one_cols]
    shift = lse[every, one_cols]
    row_dot = dots[every, one_cols]
    pick = lambda head, a, b: jnp.where(low, a, b) if head == 0 else jnp.where(low, b, a)
    q_shift = [pick(h, queries, shift) for h in range(2)]
    k_one = [pick(h, keys, one) for h in range(2)]
    v_one = [pick(h, values, one) for h in range(2)]
    g_shift = [pick(h, out_grad, row_dot) for h in range(2)]
    q_zero = [pick(h, queries, zero) for h in range(2)]
    g_zero = [pick(h, out_grad, zero) for h in range(2)]
    keys_t = keys.T
    items = [(block, head) for block in range(CLIP_LEN // QB) for head in range(2)]

    def products(item):
        block, head = item
        n = QB * block
        return (
            dot(k_one[head][n : n + QB], q_shift[head][n:], NT),
            dot(v_one[head][n : n + QB], g_shift[head][n:], NT),
        )

    ahead = 2
    ready = {t: products(items[t]) for t in range(ahead)}
    kept = {}
    for t, (block, head) in enumerate(items):
        n = QB * block
        s, grad_p = ready.pop(t)
        if t + ahead < len(items):
            ready[t + ahead] = products(items[t + ahead])
        probs = jnp.exp(s)
        diagonal = jnp.where(causal, probs[:, :QB], 0.0)
        probs = jnp.concatenate([diagonal, probs[:, QB:]], axis=1) if n + QB < CLIP_LEN else diagonal
        grad_s = (probs * grad_p).astype(BF16)
        kept[head] = (dot(grad_s, q_zero[head][n:]), dot(probs.astype(BF16), g_zero[head][n:]))
        half = slice(64 * head, 64 * head + 64)
        part = dot(keys_t[half, n : n + QB], grad_s)
        if block == 0:
            grad_qt[half, :] = part
        else:
            grad_qt[half, n:] = grad_qt[half, n:] + part
        if head == 1:
            at = rows(n, QB)
            grad_qkv[at, cols(1)] = (kept[0][0] + kept[1][0]).astype(BF16)
            grad_qkv[at, cols(2)] = (kept[0][1] + kept[1][1]).astype(BF16)
    grad_qkv[every, cols(0)] = (grad_qt[...].T * HEAD_DIM**-0.5).astype(BF16)


def block_kernel(dp, fs, tokens_n, linked, names, *refs):
    r = SimpleNamespace(**dict(zip(names, refs)))
    clips = tokens_n // CLIP_LEN
    tiles = tokens_n // TILE
    chunks = FF // CHUNK
    bits = BITS if linked else 0
    lead = (slice(None),) * bits
    base_of, stride_of = {}, {}

    load_x = pltpu.make_async_copy(r.tokens, r.x, r.local.at[0])
    load_cot = pltpu.make_async_copy(r.cotangent, r.dy, r.local.at[1])

    if linked:
        me, partner = place(dp, fs)
        barrier = pltpu.get_barrier_semaphore()
        friends = [mask for hop in (Z, XY, CORE) for mask in masks_of(hop)]
        for mask in friends:
            pl.semaphore_signal(barrier, inc=1, device_id=partner(mask), device_id_type=MESH)
        own = tuple(me)
        loads = {}
        for n, name in enumerate(("vectors", "qkv_weight", "proj_weight", "up_weight", "down_weight")):
            loads[name] = pltpu.make_async_copy(getattr(r, name), getattr(r, "my_" + name), r.local.at[3 + n])
            loads[name].start()
        load_x.start()
        load_cot.start()

        def share(flat, buf, rows, width, place_of):
            for j in range(width):
                part = flat[pl.ds(j, rows, stride=width), :].astype(BF16)
                buf[own + (slice(None), slice(128 * place_of(j), 128 * place_of(j) + 128))] = part

        per = VEC // (dp * fs)
        lane0 = (lax.axis_index("dp") * fs + lax.axis_index("fsdp")) * per % 128
        loads["vectors"].wait()
        part = r.my_vectors[...].astype(BF16).astype(F32)
        lane = lax.broadcasted_iota(jnp.int32, (1, 128), 1)
        first = pltpu.roll(part[:, :128], lane0, 1)
        tail = jnp.concatenate([part[:, 128:], jnp.zeros((1, 256 - per), F32)], axis=1)
        second = pltpu.roll(tail, lane0, 1)
        r.vec_parts[own] = jnp.concatenate(
            [
                jnp.where(lane >= lane0, first, 0.0),
                jnp.where(lane < lane0, first, second),
                jnp.where(lane < lane0, second, 0.0),
                jnp.zeros((5, 128), F32),
            ],
            axis=0,
        )
        loads["qkv_weight"].wait()
        share(r.my_qkv_weight, r.wq, 16, 12, lambda j: (j % PAIRS) * 3 + j // PAIRS)

        jobs = {}
        for n, (name, (hops, left, rows, width, _)) in enumerate(streams_of().items()):
            sems = [lambda k, ref=ref, n=n: ref.at[n, k] for ref in r.sems]
            kind, number = name[0], int(name[1:]) if name[1:].isdigit() else 0
            cols = slice(number * width, number * width + width)
            if name == "vec":
                matrix, stage, cols, base, stride = r.vec_parts, r.gvec_parts, slice(None), 0, 0
            elif kind == "q":
                matrix, stage, base, stride = r.wq, r.sq, 0, 12
            elif kind == "o":
                matrix, stage, base, stride = r.wo, r.wo, 192, 4
            elif kind == "u":
                matrix, stage, base, stride = r.w1, r.w1, 256, 16
            elif name == "dz":
                matrix, stage, cols, base, stride = r.w2, r.down_part, slice(None), 512, 4
            else:
                matrix, stage = r.w2.at[number // 2, number % 2], r.sd.at[number // 2, number % 2]
                cols = slice(None)

            def finish(total, name=name, kind=kind, number=number, rows=rows, width=width):
                if name == "vec":
                    r.total_vec[...] = total
                elif kind == "d" and name != "dz":
                    r.down_part[number // 2, number % 2] = total.astype(BF16)
                else:
                    for j in range(width // 128):
                        col = j * PAIRS + number if kind == "q" else number * (width // 128) + j
                        at = pl.ds(base_of[name] + col, rows, stride=stride_of[name])
                        r.total[at, :] = total[:, 128 * j : 128 * j + 128]

            if name == "vec" or name == "dz" or kind != "d":
                base_of[name], stride_of[name] = base, stride
            jobs["g", name] = Gather(me, partner, hops, left, matrix, cols, *sems[:2])
            sum_left = left if name != "dz" else Z
            jobs["s", name] = Scatter(
                me, partner, hops[::-1], sum_left, stage, cols, r.come[name], *sems[2:], finish
            )
        plan = plan_of()[0]
        pl.semaphore_wait(barrier, len(friends))
    else:
        load_x.start()
        load_cot.start()
        loads = [
            pltpu.make_async_copy(src, dst, r.local.at[3 + n])
            for n, (src, dst) in enumerate(
                [(r.qkv_mat, r.wq), (r.proj_mat, r.wo), (r.up_mat, r.w1), (r.down_mat, r.w2)]
            )
        ]
        for load in loads:
            load.start()
        r.vec[...] = r.vec_in[...]
        for load in loads:
            load.wait()

    def exchange(name, index):
        if not linked:
            return
        for (step, at), taken in plan.items():
            if step != name or not taken:
                continue

            def act(taken=taken):
                for kind, stream, k in taken:
                    jobs[kind, stream].step(k)

            if isinstance(index, int):
                if index == at:
                    act()
            else:
                pl.when(index == at)(act)

    vec, gvec = r.vec, r.gvec
    gvec[...] = jnp.zeros((VROWS, 128), F32)

    def vector(first, count):
        return jnp.concatenate([vec[first + n : first + n + 1, :] for n in range(count)], axis=1)

    def add_vector(first, values):
        for n in range(values.shape[1] // 128):
            gvec[first + n : first + n + 1, :] += values[:, 128 * n : 128 * n + 128]

    def whole(ref, cols):
        got = ref[lead + (slice(None), cols)]
        return got.reshape(-1, got.shape[-1])

    def down_chunk(c):
        if linked:
            return r.w2[c // 2, c % 2].reshape(CHUNK, D)
        return r.w2[pl.ds(pl.multiple_of(c * CHUNK, CHUNK), CHUNK), :]

    rows_of = lambda i, size: pl.ds(pl.multiple_of(i * size, size), size)
    act = lambda rows: r.big.at[rows, pl.ds(0, 512)]
    grad_pre = lambda rows: r.big.at[rows, pl.ds(512, 512)]
    normed_two = lambda rows: r.big.at[rows, pl.ds(1024, 512)]
    everything = pl.ds(0, tokens_n)

    exchange("first", 0)
    if linked:
        for name, buf, rows, width in (
            ("proj_weight", r.wo, 16, 4),
            ("up_weight", r.w1, 16, 16),
            ("down_weight", r.w2, 64, 4),
        ):
            loads[name].wait()
            share(getattr(r, "my_" + name), buf, rows, width, lambda j: j)
    exchange("norm", 0)
    load_x.wait()

    def norm_one(i, carry):
        rows = rows_of(i, 256)
        r.grad_h[rows, :] = norm(r.x[rows, :].astype(F32))[0]
        return carry

    lax.fori_loop(0, tokens_n // 256, norm_one, 0)
    load_cot.wait()

    def mask_one(i, carry):
        rows = rows_of(i, 256)
        per = CLIP_LEN // 256
        place_in = (i % per) * 256 + lax.broadcasted_iota(jnp.int32, (256, 1), 0)
        dy = jnp.where(place_in >= r.cond_frames[i // per] * FRAME_TOK, r.dy[rows, :].astype(F32), 0.0)
        add_vector(B2, column_sum(dy))
        r.dy[rows, :] = dy.astype(BF16)
        return carry

    lax.fori_loop(0, tokens_n // 256, mask_one, 0)
    exchange("affine", 0)
    if linked:
        vec[...] = jnp.zeros((VROWS, 128), F32)
        for n in range(dp * fs):
            row = n * per // 128
            vec[row : row + 3, :] += r.vec_parts[split_bits(n) + (slice(0, 3),)]

    def affine_one(i, carry):
        rows = rows_of(i, 256)
        r.a[rows, :] = (r.grad_h[rows, :] * vector(G1, 4) + vector(S1, 4)).astype(BF16)
        return carry

    lax.fori_loop(0, tokens_n // 256, affine_one, 0)

    def forward(t, carry):
        exchange("fwd", t)
        pair, clip = t // clips, t % clips

        @pl.when(clip == 0)
        def _():
            cols = pl.ds(pl.multiple_of(pair * 384, 128), 384)
            matrix = whole(r.wq, cols)
            bias = jnp.concatenate([vec[pl.ds(BQKV + 4 * n + pair, 1), :] for n in range(3)], axis=1)
            for i in range(tiles):
                rows = slice(i * TILE, i * TILE + TILE)
                r.qkv[rows, cols] = (dot(r.a[rows, :], matrix) + bias).astype(BF16)

        attend_forward(r.qkv, r.mixed, r.lse, clip * CLIP_LEN, pair)
        return carry

    lax.fori_loop(0, PAIRS * clips, forward, 0)

    exchange("mid", 0)

    def middle(i, carry):
        rows = rows_of(i, TILE)
        h = r.x[rows, :].astype(F32) + dot(r.mixed[rows, :], whole(r.wo, slice(None))) + vector(BO, 4)
        hat, scale = norm(h)
        r.hat[rows, :] = hat.astype(BF16)
        r.scale[rows, :] = jnp.broadcast_to(scale, (TILE, 128))
        normed_two(rows)[...] = (hat * vector(G2, 4) + vector(S2, 4)).astype(BF16)
        r.h_low[rows, :] = (h + vector(B2, 4)).astype(BF16)
        r.grad_h[rows, :] = jnp.zeros((TILE, D), F32)
        return carry

    lax.fori_loop(0, tiles, middle, 0)

    def park_of(c):
        cols = pl.ds(pl.multiple_of(c * CHUNK, CHUNK), CHUNK)
        return pltpu.make_async_copy(act(everything), r.parked.at[:, cols], r.local.at[2])

    def feed(c, carry):
        exchange("ffa", c)
        cols = pl.ds(pl.multiple_of(c * CHUNK, CHUNK), CHUNK)
        up, down = whole(r.w1, cols), down_chunk(c)
        bias = jnp.concatenate([vec[pl.ds(B1 + 4 * c + n, 1), :] for n in range(4)], axis=1)
        spans = [slice(i * TILE, i * TILE + TILE) for i in range(tiles)]

        def products(rows):
            return dot(normed_two(rows)[...], up), dot(r.dy[rows, :], down, NT)

        park = park_of(c)

        @pl.when(c > 0)
        def _():
            park.wait()

        ready, late = products(spans[0]), None
        bias_grad = jnp.zeros((1, CHUNK), F32)
        for i, rows in enumerate(spans):
            pre, grad_act = ready
            if i + 1 < tiles:
                ready = products(spans[i + 1])
            value, slope = gelu_both(pre + bias)
            value = value.astype(BF16)
            grad = slope * grad_act
            bias_grad = bias_grad + column_sum(grad)
            grad = grad.astype(BF16)
            act(rows)[...] = value
            grad_pre(rows)[...] = grad
            if late:
                r.grad_h[late[0], :] += dot(late[1], up, NT)
            late = (rows, grad)
        r.grad_h[late[0], :] += dot(late[1], up, NT)
        for n in range(4):
            gvec[pl.ds(B1 + 4 * c + n, 1), :] = bias_grad[:, 128 * n : 128 * n + 128]
        exchange("ffb", c)
        park.start()
        grad_up = dot(normed_two(everything)[...], grad_pre(everything)[...], TN).astype(BF16)
        grad_down = dot(act(everything)[...], r.dy[...], TN).astype(BF16)
        if linked:
            r.w1[lead + (slice(None), cols)] = grad_up.reshape((2,) * bits + (16, CHUNK))
            r.sd[c // 2, c % 2] = grad_down.reshape((2,) * (bits - 2) + (64, D))
        else:
            r.w1[:, cols] = grad_up
            r.sd[rows_of(c, CHUNK), :] = grad_down
        return carry

    lax.fori_loop(0, chunks, feed, 0)
    park_of(0).wait()

    exchange("ln2", 0)
    ri = lax.broadcasted_iota(jnp.int32, (128, 128), 0)
    ci = lax.broadcasted_iota(jnp.int32, (128, 128), 1)
    other_half = jnp.where((ri < 64) != (ci < 64), 1.0, 0.0).astype(BF16)
    other_half = jnp.concatenate([other_half, other_half], axis=0)
    spare = lax.broadcasted_iota(jnp.int32, (TILE, 128), 1) & 63
    proj = whole(r.wo, slice(None))

    def norm_part(rows):
        grad, hat, scale = r.grad_h[rows, :], r.hat[rows, :].astype(F32), r.scale[rows, :1]
        add_vector(G2, column_sum(grad * hat))
        add_vector(S2, column_sum(grad))
        grad = r.dy[rows, :].astype(F32) + norm_back(grad, hat, scale, vector(G2, 4))
        r.grad_h[rows, :] = grad
        low = grad.astype(BF16)
        add_vector(BO, column_sum(low.astype(F32)))
        return low

    def proj_part(rows, low):
        mixed = r.mixed[rows, :]
        part = dot(mixed, low, TN)
        grad_mixed = dot(low, proj, NT).astype(BF16)
        r.dy[rows, :] = grad_mixed
        product = grad_mixed.astype(F32) * mixed.astype(F32)
        high = product.astype(BF16)
        rest = (product - high.astype(F32)).astype(BF16)
        for p in range(PAIRS):
            cols = slice(128 * p, 128 * p + 128)
            row_dot = dot(jnp.concatenate([high[:, cols], rest[:, cols]], axis=1), other_half)
            top = row_dot.astype(BF16).astype(F32)
            r.mixed[rows, cols] = jnp.where(
                spare == 0, -top, jnp.where(spare == 1, top - row_dot, 0.0)
            ).astype(BF16)
        return part

    spans = [slice(i * TILE, i * TILE + TILE) for i in range(tiles)]
    grad_proj = jnp.zeros((D, D), F32)
    low = norm_part(spans[0])
    for i, rows in enumerate(spans):
        after = norm_part(spans[i + 1]) if i + 1 < tiles else None
        grad_proj = grad_proj + proj_part(rows, low)
        low = after
    grad_proj = grad_proj.astype(BF16)
    if linked:
        r.wo[...] = grad_proj.reshape((2,) * bits + (16, D))
    else:
        r.wo[...] = grad_proj

    def backward(t, carry):
        exchange("bwd", t)
        pair, clip = t // clips, t % clips
        attend_backward(r.qkv, r.dy, r.lse, r.mixed, r.big, r.grad_qt, clip * CLIP_LEN, pair)

        @pl.when(clip == clips - 1)
        def _():
            cols = pl.ds(pl.multiple_of(pair * 384, 128), 384)
            grad = r.big[:, cols]
            sums = column_sum(grad.astype(F32))
            for n in range(3):
                gvec[pl.ds(BQKV + 4 * n + pair, 1), :] = sums[:, 128 * n : 128 * n + 128]
            matrix = dot(r.a[...], grad, TN).astype(BF16)
            if linked:
                r.sq[lead + (slice(None), cols)] = matrix.reshape((2,) * bits + (16, 384))
            else:
                r.sq[:, cols] = matrix

        return carry

    lax.fori_loop(0, PAIRS * clips, backward, 0)

    fetches = []
    for c in range(chunks):
        dst = r.qkv.at[:, c * CHUNK : c * CHUNK + CHUNK] if c < 3 else r.dy
        src = r.parked.at[:, c * CHUNK : c * CHUNK + CHUNK]
        fetches.append(pltpu.make_async_copy(src, dst, r.local.at[c]))
        fetches[-1].start()
    matrix = whole(r.wq, slice(None))
    spans = [slice(i * TILE, i * TILE + TILE) for i in range(tiles)]
    for i, rows in enumerate(spans):
        exchange("sums", i)
        grad = dot(r.big[rows, :], matrix, NT)
        hat, scale = norm(r.x[rows, :].astype(F32))
        r.hat[rows, :] = hat.astype(BF16)
        r.scale[rows, :] = jnp.broadcast_to(scale, (TILE, 128))
        add_vector(G1, column_sum(grad * hat))
        add_vector(S1, column_sum(grad))
        r.a[rows, :] = grad.astype(BF16)
    if linked:
        for n in range(dp * fs):
            row = n * per // 128
            r.gvec_parts[split_bits(n)] = jnp.concatenate(
                [gvec[row : row + 3, :], jnp.zeros((5, 128), F32)], axis=0
            )
    stores = []
    for i, rows in enumerate(spans):
        exchange("ln1", i)
        grad = norm_back(r.a[rows, :].astype(F32), r.hat[rows, :].astype(F32), r.scale[rows, :1], vector(G1, 4))
        r.lse[rows, :] = (r.grad_h[rows, :] + grad).astype(BF16)
        stores.append(pltpu.make_async_copy(r.lse.at[rows, :], r.input_grad.at[rows, :], r.local.at[4 + i]))
        stores[-1].start()

    for fetch in fetches:
        fetch.wait()
    down = whole(r.w2, slice(None))
    for i, rows in enumerate(spans):
        exchange("out", i)
        value = jnp.concatenate([r.qkv[rows, :], r.dy[rows, :]], axis=1)
        r.mixed[rows, :] = (r.h_low[rows, :].astype(F32) + dot(value, down)).astype(BF16)
        stores.append(pltpu.make_async_copy(r.mixed.at[rows, :], r.output.at[rows, :], r.local.at[8 + i]))
        stores[-1].start()
    exchange("end", 0)
    if not linked:
        for n, (src, dst) in enumerate(
            [(r.sq, r.qkv_grad), (r.wo, r.proj_grad), (r.w1, r.up_grad), (r.sd, r.down_grad)]
        ):
            stores.append(pltpu.make_async_copy(src, dst, r.local.at[n]))
            stores[-1].start()
        r.total_vec[...] = gvec[...]
    for store in stores:
        store.wait()


def run_block(dp, fs, linked, tokens, cotangent, cond_frames, weights):
    n = tokens.shape[0]
    shape = jax.ShapeDtypeStruct
    vmem, smem, any_ = (
        pl.BlockSpec(memory_space=pltpu.VMEM),
        pl.BlockSpec(memory_space=pltpu.SMEM),
        pl.BlockSpec(memory_space=pl.ANY),
    )
    bits = BITS if linked else 0
    ins = ["tokens", "cotangent", "cond_frames"]
    in_specs = [any_, any_, smem]
    outs = {"output": ((n, D), BF16, any_), "input_grad": ((n, D), BF16, any_)}
    outs["parked"] = ((n, FF), BF16, any_)
    outs["total_vec"] = ((8 if linked else VROWS, 128), F32, vmem)
    if linked:
        ins += ["qkv_weight", "proj_weight", "up_weight", "down_weight", "vectors"]
        in_specs += [any_] * 5
        outs["total"] = ((768, 128), F32, vmem)
        matrix = lambda rows, cols: pltpu.VMEM((2,) * bits + (rows // 2**bits, cols), BF16)
    else:
        ins += ["qkv_mat", "proj_mat", "up_mat", "down_mat", "vec_in"]
        in_specs += [any_] * 4 + [vmem]
        outs["qkv_grad"] = ((D, 3 * D), BF16, any_)
        outs["proj_grad"] = ((D, D), BF16, any_)
        outs["up_grad"] = ((D, FF), BF16, any_)
        outs["down_grad"] = ((FF, D), BF16, any_)
        matrix = lambda rows, cols: pltpu.VMEM((rows, cols), BF16)
    scratch = {
        "x": pltpu.VMEM((n, D), BF16),
        "a": pltpu.VMEM((n, D), BF16),
        "dy": pltpu.VMEM((n, D), BF16),
        "qkv": pltpu.VMEM((n, 3 * D), BF16),
        "mixed": pltpu.VMEM((n, D), BF16),
        "lse": pltpu.VMEM((n, D), BF16),
        "hat": pltpu.VMEM((n, D), BF16),
        "h_low": pltpu.VMEM((n, D), BF16),
        "grad_h": pltpu.VMEM((n, D), F32),
        "scale": pltpu.VMEM((n, 128), F32),
        "big": pltpu.VMEM((n, 3 * D), BF16),
        "grad_qt": pltpu.VMEM((128, CLIP_LEN), F32),
        "wq": matrix(D, 3 * D),
        "sq": matrix(D, 3 * D),
        "wo": matrix(D, D),
        "w1": matrix(D, FF),
        "w2": matrix(FF, D),
        "sd": matrix(FF, D),
        "vec": pltpu.VMEM((VROWS, 128), F32),
        "gvec": pltpu.VMEM((VROWS, 128), F32),
        "local": pltpu.SemaphoreType.DMA((12,)),
    }
    names = ins + list(outs) + list(scratch)
    shapes = list(scratch.values())
    come_names = []
    if linked:
        streams = streams_of()
        for name in ("vec_parts", "gvec_parts"):
            names.append(name)
            shapes.append(pltpu.VMEM((2,) * bits + (8, 128), F32))
        for name, held in zip(ins[3:], weights):
            names.append("my_" + name)
            shapes.append(pltpu.VMEM(held.shape, F32))
        names.append("down_part")
        shapes.append(pltpu.VMEM((2, 2, 64, D), BF16))
        for name in ("gather_send", "gather_recv", "sum_send", "sum_recv"):
            names.append(name)
            shapes.append(pltpu.SemaphoreType.DMA((len(streams), 7)))
        for name, (hops, left, rows, width, size) in streams.items():
            held = len(left) if name != "dz" else 2
            for k, hop in enumerate(hops[::-1]):
                held -= len(hop)
                come_names.append((name, f"{name}_{k}"))
                names.append(f"{name}_{k}")
                kind = BF16 if size == 2 else F32
                shapes.append(pltpu.VMEM((len(masks_of(hop)),) + (2,) * held + (rows, width), kind))

    def body(*refs):
        table = dict(zip(names, refs))
        if linked:
            table["come"] = {}
            for name, key in come_names:
                table["come"].setdefault(name, []).append(table.pop(key))
            keys = ("gather_send", "gather_recv", "sum_send", "sum_recv")
            table["sems"] = [table.pop(key) for key in keys]
        block_kernel(dp, fs, n, linked, list(table), *table.values())

    params = dict(vmem_limit_bytes=64 << 20)
    if linked:
        params.update(collective_id=0, has_side_effects=True)
    return pl.pallas_call(
        body,
        out_shape=[shape(s, t) for s, t, _ in outs.values()],
        in_specs=in_specs,
        out_specs=[spec for *_, spec in outs.values()],
        scratch_shapes=shapes,
        compiler_params=pltpu.CompilerParams(**params),
        name="block",
    )(tokens, cotangent, cond_frames, *weights)


def adamw(weight, grad, first, second, average, rate, decay):
    first_new = BETA_ONE * first + (1.0 - BETA_ONE) * grad
    second_new = BETA_TWO * second + (1.0 - BETA_TWO) * grad * grad
    first_hat = first_new / (1.0 - BETA_ONE**STEP)
    second_hat = second_new / (1.0 - BETA_TWO**STEP)
    weight_new = weight - rate * (first_hat / (jnp.sqrt(second_hat) + ADAM_EPS) + decay * weight)
    average_new = EMA_KEEP * average + (1.0 - EMA_KEEP) * weight_new
    return (first_new, second_new, weight_new, average_new)


def adam_kernel(dp, fs, linked, *refs):
    total, total_vec, output, input_grad = refs[:4]
    ins, outs, (output_new, input_grad_new) = refs[4:24], refs[24:44], refs[44:46]
    held, made = refs[46:66], refs[66:86]
    low_grad, full_grad, out_low, fetched, moved, loaded, stored = refs[86:]
    loads = [pltpu.make_async_copy(a, b, loaded.at[n]) for n, (a, b) in enumerate(zip(ins, held))]
    stores = [pltpu.make_async_copy(a, b, stored.at[n]) for n, (a, b) in enumerate(zip(made, outs))]
    fetches, moves = [], []
    for a, b, c, d in ((input_grad, low_grad, full_grad, input_grad_new), (output, out_low, out_low, output_new)):
        size = a.shape[0] // 4
        for n in range(4):
            rows, at = pl.ds(n * size, size), len(moves)
            fetches.append(pltpu.make_async_copy(a.at[rows, :], b.at[rows, :], fetched.at[at]))
            moves.append(pltpu.make_async_copy(c.at[rows, :], d.at[rows, :], moved.at[at]))
    for load in fetches + loads:
        load.start()
    for n, (fetch, move) in enumerate(zip(fetches, moves)):
        fetch.wait()
        if n < 4:
            rows = slice(n * size, n * size + size)
            full_grad[rows, :] = low_grad[rows, :].astype(F32)
        move.start()

    def update(m, grad, rate, decay):
        for load in loads[4 * m : 4 * m + 4]:
            load.wait()
        weight, first, second, average = (ref[...] for ref in held[4 * m : 4 * m + 4])
        new = adamw(weight, grad, first, second, average, rate, decay)
        for ref, value in zip(made[4 * m : 4 * m + 4], new):
            ref[...] = value
        for store in stores[4 * m : 4 * m + 4]:
            store.start()

    base = 0
    for m in range(4):
        size = held[4 * m].shape[0]
        update(m, total[base : base + size, :], RATE_MATRIX, WEIGHT_DECAY)
        base += size
    per = VEC // (dp * fs)
    start = (lax.axis_index("dp") * fs + lax.axis_index("fsdp")) * per
    lane0 = start % 128
    lane = lax.broadcasted_iota(jnp.int32, (1, 128), 1)
    back = lax.rem(128 - lane0, 128)
    row = 0 if linked else start // 128
    parts = [pltpu.roll(total_vec[pl.ds(row + n, 1), :], back, 1) for n in range(3)]
    keep = 128 - lane0
    grad = jnp.concatenate(
        [jnp.where(lane < keep, parts[0], parts[1]), jnp.where(lane < keep, parts[1], parts[2])], axis=1
    )[:, :per]
    update(4, grad, RATE_VECTOR, 0.0)
    for copy in stores + moves:
        copy.wait()


def run_adam(dp, fs, linked, total, total_vec, output, input_grad, state):
    flat = [a.reshape(-1, 128) for a in state[:16]] + list(state[16:])
    vmem, any_ = pl.BlockSpec(memory_space=pltpu.VMEM), pl.BlockSpec(memory_space=pl.ANY)
    shapes = [jax.ShapeDtypeStruct(a.shape, F32) for a in flat]
    shapes += [jax.ShapeDtypeStruct(output.shape, BF16), jax.ShapeDtypeStruct(output.shape, F32)]
    new = pl.pallas_call(
        functools.partial(adam_kernel, dp, fs, linked),
        out_shape=shapes,
        in_specs=[vmem] * 2 + [any_] * 22,
        out_specs=[any_] * 22,
        scratch_shapes=[pltpu.VMEM(a.shape, F32) for a in flat] * 2
        + [pltpu.VMEM(output.shape, t) for t in (BF16, F32, BF16)]
        + [pltpu.SemaphoreType.DMA((n,)) for n in (8, 8, 20, 20)],
        compiler_params=pltpu.CompilerParams(vmem_limit_bytes=64 << 20),
        name="adam",
    )(total, total_vec, output, input_grad, *flat)
    return list(new[20:]) + [a.reshape(b.shape) for a, b in zip(new, state)]


def local(dp, fs, tokens, cotangent, cond_frames, *state):
    weights, firsts, seconds, averages = (state[5 * n : 5 * n + 5] for n in range(4))
    shards = dp * fs
    linked = shards == 2**BITS and not (dp & (dp - 1))
    if linked:
        shares = [w.reshape(-1, 128) for w in weights[:4]] + [weights[4]]
        output, input_grad, _, total_vec, total = run_block(
            dp, fs, True, tokens, cotangent, cond_frames, shares
        )
    else:
        gathered = [
            lax.all_gather(w.astype(BF16), AXES, axis=0, tiled=True) for w in weights
        ]
        qkv = gathered[0].reshape(D, 3, PAIRS, 128).swapaxes(1, 2).reshape(D, 3 * D)
        vec = jnp.pad(gathered[4].astype(F32).reshape(-1, 128), ((0, VROWS - VEC // 128), (0, 0)))
        mats = [qkv] + [g.reshape(-1, c) for g, c in zip(gathered[1:4], (D, FF, D))] + [vec]
        output, input_grad, _, total_vec, *grads = run_block(
            dp, fs, False, tokens, cotangent, cond_frames, mats
        )
        grads[0] = grads[0].reshape(D, PAIRS, 3, 128).swapaxes(1, 2).reshape(D, 3 * D)
        scatter = lambda g: lax.psum_scatter(
            g.astype(F32).reshape(shards, -1), AXES, scatter_dimension=0, tiled=True
        )
        total = jnp.concatenate([scatter(g).reshape(-1, 128) for g in grads], axis=0)
        total_vec = lax.psum(total_vec, AXES)
    order = [group[m] for m in range(5) for group in (weights, firsts, seconds, averages)]
    return tuple(run_adam(dp, fs, linked, total, total_vec, output, input_grad, order))


def solution(mesh):
    dp, fs = mesh.shape["dp"], mesh.shape["fsdp"]
    split = P(AXES, None)
    return jax.shard_map(
        functools.partial(local, dp, fs),
        mesh=mesh,
        in_specs=(split, split, P(AXES)) + (split,) * 20,
        out_specs=(split,) * 22,
        check_vma=False,
    )
```
